512 devices in a mesh: dom: 64 (over y, z), gz: 8 (over x, core).
Axes of the slice: x: 4, y: 8, z: 8, core: 2. Of those that a mesh axis runs over, the one named last changes fastest.
Arguments:
- features: float32 [65536, 128], P(('dom', 'gz')), may hold values from -6 to 6
- positions: float32 [3, 65536], P(None, ('dom', 'gz')), may hold values from 0 to 1
- send_ids: int32 [512, 608], P(('dom', 'gz')), may hold values from 0 to 127
- ghost_prefix: int32 [512, 27], P(('dom', 'gz')), may hold values from 0 to 608, as said below
- edge_fill: int32 [512], P(('dom', 'gz')), may hold values from 128 to 512, as said below
- edge_src: int32 [512, 512], P(('dom', 'gz')), may hold values from 0 to 127
- edge_dst: int32 [512, 512], P(('dom', 'gz')), may hold values from 0 to 735, as said below
- weight_src: bfloat16 [128, 128], replicated, may hold values from -0.5 to 0.5
- weight_dst: bfloat16 [128, 128], replicated, may hold values from -0.5 to 0.5
- weight_radial: bfloat16 [8, 128], replicated, may hold values from -2 to 2
- weight_env: bfloat16 [128, 128], replicated, may hold values from -0.5 to 0.5
- weight_latent: bfloat16 [512, 128], replicated, may hold values from -0.25 to 0.25
- weight_hidden: bfloat16 [128, 128], replicated, may hold values from -0.5 to 0.5
- weight_readout: float32 [128], replicated, may hold values from -0.5 to 0.5
Outputs:
- forces: float32 [3, 65536], P(None, ('dom', 'gz'))
- feat_grad: float32 [65536, 128], P(('dom', 'gz'))
The draws below stay inside these ranges and needn't reach their ends.
Inputs may be any that keep to these rules, and one draw needn't show every extreme that they name: `ghost_prefix`: each row starts at 0 and rises; the count of direction n lies between cap_n - cap_n // 2 and cap_n, and on one domain every count equals its capacity. `edge_fill`: A multiple of 128, at least 128 * max(512 // 512, 1); one domain uses all 512 slots. `edge_dst`: never equal to edge_src.
All inputs are finite; a program needn't handle non-finite values.
Results may differ from the reference program's by a relative error of at most 0.015.
Values sent between devices are 32-bit elements; how exact they have to be, the bound alone decides.
A program may use at most 64 MiB of HBM per device.

```python
import math
import jax
import jax.numpy as jnp
import numpy as np
from jax import lax

CHANNELS = 128
BASIS = 8
NEIGHBOURS = 4
ATOMS = 128
CAP_FACE = 64
CAP_EDGE = 16
CAP_CORNER = 4
GHOSTS = 608
EDGES = 512
DOMS = 512
DOM_Y = 8
DOM_X = 8
ZDOM = 8
ATOMS_ALL = 65536


def capacity_vector():
    capacity = []
    for first in (-1, 0, 1):
        for second in (-1, 0, 1):
            for third in (-1, 0, 1):
                nonzero = abs(first) + abs(second) + abs(third)
                if nonzero > 0:
                    capacity.append((0, CAP_FACE, CAP_EDGE, CAP_CORNER)[nonzero])
    return jnp.array(capacity, jnp.int32)


def edge_pairs(key):
    key_source, key_local, key_stride, key_ghost = jax.random.split(key, 4)
    layout = (DOMS, EDGES)
    source = jax.random.randint(key_source, layout, 0, ATOMS)
    choose_local = jax.random.randint(key_local, layout, 0, 2)
    stride = jax.random.randint(key_stride, layout, 1, ATOMS)
    ghost_slot = jax.random.randint(key_ghost, layout, 0, GHOSTS)
    target = jnp.where(choose_local == 1, (source + stride) % ATOMS, ATOMS + ghost_slot)
    return (source.astype(jnp.int32), target.astype(jnp.int32))


def draw_edge_src(key, part):
    return edge_pairs(key)[0]


def draw_edge_dst(key, part):
    return edge_pairs(key)[1]


def draw_ghost_prefix(key, part):
    key = jax.random.fold_in(key, 11)
    key_count, key_full = jax.random.split(key, 2)
    capacity = capacity_vector()
    spread = jax.random.randint(key_count, (DOMS, 26), 0, 1 << 20) % (capacity // 2 + 1)[None, :]
    counts = capacity[None, :] - capacity[None, :] // 2 + spread
    full_device = jax.random.randint(key_full, (), 0, DOMS)
    counts = jnp.where(jnp.arange(DOMS)[:, None] == full_device, capacity[None, :], counts)
    prefix = jnp.concatenate([jnp.zeros((DOMS, 1), jnp.int32), jnp.cumsum(counts, axis=1).astype(jnp.int32)], axis=1)
    return prefix.astype(jnp.int32)


def draw_edge_fill(key, part):
    key = jax.random.fold_in(key, 12)
    key_first, key_second, key_full = jax.random.split(key, 3)
    blocks = EDGES // 128
    lowest = max(blocks // 4, 1)
    first_draw = jax.random.randint(key_first, (DOMS,), lowest, blocks + 1)
    second_draw = jax.random.randint(key_second, (DOMS,), lowest, blocks + 1)
    used = jnp.minimum(first_draw, second_draw)
    full_device = jax.random.randint(key_full, (), 0, DOMS)
    used = jnp.where(jnp.arange(DOMS) == full_device, blocks, used)
    return (128 * used).astype(jnp.int32)


def plant(values, own_key, least, top_value):
    shape = values.shape
    spot = [jax.random.randint(jax.random.fold_in(own_key, axis), (), 0, shape[axis]) for axis in range(len(shape))]
    values = values.at[tuple(spot)].set(least)
    longest = shape.index(max(shape))
    spot[longest] = (spot[longest] + 1) % shape[longest]
    return values.at[tuple(spot)].set(top_value)


def steps_of(stream_key, dims, shards, least, high):
    gain = 1.0
    for position, shards_of in shards:
        steps = jax.random.uniform(jax.random.fold_in(jax.random.fold_in(stream_key, 6), position), (shards_of,), jnp.float32, least / len(shards), high / len(shards))
        gain = gain * jnp.repeat(jnp.exp(steps), dims[position] // shards_of).reshape((-1,) + (1,) * (len(dims) - 1 - position))
    return gain


def centred(stream_key, dims, scale, reach, shards=(), dtype=jnp.bfloat16):
    entries = jax.random.normal(stream_key, dims, jnp.float32) * scale
    if len(shards) > 0:
        entries = steps_of(stream_key, dims, shards, -0.22, 0.18) * entries
    return jnp.clip(entries, min=-reach, max=reach).astype(dtype)


def setup_inputs(seed: int = 0) -> dict:
    streams_of = jax.random.split(jax.random.key(seed), 15)
    features = centred(streams_of[0], (ATOMS_ALL, CHANNELS), 1.0, 6.0, ((0, 512),), jnp.float32)
    positions = jnp.clip(1.0 * jax.random.uniform(streams_of[1], (3, ATOMS_ALL), jnp.float32) ** steps_of(streams_of[1], (3, ATOMS_ALL), ((1, 512),), -0.2, 0.2), 0.0, 1.0)
    send_ids = plant(jax.random.randint(streams_of[2], (DOMS, GHOSTS), 0, ATOMS), jax.random.fold_in(streams_of[2], 1), 0, ATOMS - 1).astype(jnp.int32)
    ghost_prefix = draw_ghost_prefix(jax.random.fold_in(streams_of[14], 71), 0)
    edge_fill = draw_edge_fill(jax.random.fold_in(streams_of[14], 71), 0)
    edge_src = draw_edge_src(jax.random.fold_in(streams_of[14], 71), 0)
    edge_dst = draw_edge_dst(jax.random.fold_in(streams_of[14], 71), 0)
    weight_src = centred(streams_of[7], (CHANNELS, CHANNELS), CHANNELS ** -0.5, 0.5)
    weight_dst = centred(streams_of[8], (CHANNELS, CHANNELS), CHANNELS ** -0.5, 0.5)
    weight_radial = centred(streams_of[9], (BASIS, CHANNELS), BASIS ** -0.5, 2.0)
    weight_env = centred(streams_of[10], (CHANNELS, CHANNELS), CHANNELS ** -0.5, 0.5)
    weight_latent = centred(streams_of[11], (4 * CHANNELS, CHANNELS), (4 * CHANNELS) ** -0.5, 0.25)
    weight_hidden = centred(streams_of[12], (CHANNELS, CHANNELS), CHANNELS ** -0.5, 0.5)
    weight_readout = centred(streams_of[13], (CHANNELS,), CHANNELS ** -0.5, 0.5, (), jnp.float32)
    return dict(features=features, positions=positions, send_ids=send_ids, ghost_prefix=ghost_prefix, edge_fill=edge_fill, edge_src=edge_src, edge_dst=edge_dst, weight_src=weight_src, weight_dst=weight_dst, weight_radial=weight_radial, weight_env=weight_env, weight_latent=weight_latent, weight_hidden=weight_hidden, weight_readout=weight_readout)


CUTOFF = 1.0
SHARPNESS = 8.0

def direction_table(face_cap, edge_cap, corner_cap):
    vectors = []
    capacity = []
    for first in (-1, 0, 1):
        for second in (-1, 0, 1):
            for third in (-1, 0, 1):
                nonzero = abs(first) + abs(second) + abs(third)
                if nonzero > 0:
                    vectors.append((first, second, third))
                    capacity.append((0, face_cap, edge_cap, corner_cap)[nonzero])
    offsets = np.concatenate([[0], np.cumsum(capacity)]).astype(np.int64)
    slot_dir = np.repeat(np.arange(26), capacity)
    slot_index = np.concatenate([np.arange(width) for width in capacity])
    return (np.array(vectors), capacity, offsets, slot_dir, slot_index)

def harmonics(scaled):
    x_part, y_part, z_part = (scaled[0], scaled[1], scaled[2])
    root_three = math.sqrt(3.0)
    root_fifteen = math.sqrt(15.0)
    root_five = math.sqrt(5.0)
    return jnp.stack([jnp.ones_like(x_part), root_three * x_part, root_three * y_part, root_three * z_part, root_fifteen * x_part * y_part, root_fifteen * y_part * z_part, root_fifteen * z_part * x_part, 0.5 * root_fifteen * (x_part * x_part - y_part * y_part), 0.5 * root_five * (2.0 * z_part * z_part - x_part * x_part - y_part * y_part)])

def local_energy(node_pos, node_feat, node_live, edge_source, edge_target, fill, own_count, norm, weight_src, weight_dst, weight_radial, weight_env, weight_latent, weight_hidden, weight_readout):
    half_feat = node_feat.astype(jnp.bfloat16)
    proj_source = jnp.dot(half_feat[:own_count], weight_src, preferred_element_type=jnp.float32)
    proj_target = jnp.dot(half_feat, weight_dst, preferred_element_type=jnp.float32)
    relative = jnp.take(node_pos, edge_target, axis=1) - jnp.take(node_pos, edge_source, axis=1)
    scaled = relative / CUTOFF
    radius_sq = lax.optimization_barrier(jnp.sum(scaled * scaled, axis=0))
    edge_total = edge_source.shape[0]
    in_use = (jnp.arange(edge_total) < fill).astype(jnp.float32) * node_live[edge_target]
    inside = radius_sq < 1.0
    envelope = jnp.where(inside, jnp.square(1.0 - jnp.minimum(radius_sq, 1.0)), 0.0) * in_use
    basis_count = weight_radial.shape[0]
    centers = jnp.arange(basis_count).astype(jnp.float32) / (basis_count - 1)
    radial_basis = jnp.exp(-SHARPNESS * jnp.square(radius_sq[None, :] - centers[:, None])).astype(jnp.bfloat16)
    radial = lax.dot_general(radial_basis, weight_radial, (((0,), (0,)), ((), ())), preferred_element_type=jnp.float32)
    pre_act = proj_source[edge_source] + proj_target[edge_target] + radial
    latent = (jax.nn.silu(pre_act) * envelope[:, None]).astype(jnp.bfloat16)
    env_weight = jnp.dot(latent, weight_env, preferred_element_type=jnp.float32)
    channels = env_weight.shape[1]
    harmonic = harmonics(scaled)
    harmonic_rows = jnp.transpose(harmonic)
    weighted = (harmonic_rows[:, :, None] * env_weight[:, None, :]).reshape(edge_total, 9 * channels)
    environment = jax.ops.segment_sum(weighted, edge_source, num_segments=own_count) / norm
    gathered = environment[edge_source].reshape(edge_total, 9, channels)
    scalar_parts = []
    for lower, upper in ((0, 1), (1, 4), (4, 9)):
        scalar_parts.append(lax.optimization_barrier(jnp.sum(harmonic_rows[:, lower:upper, None] * gathered[:, lower:upper, :], axis=1)))
    scalars = jnp.concatenate(scalar_parts, axis=1).astype(jnp.bfloat16)
    joined = jnp.concatenate([latent, scalars], axis=1)
    update = jnp.dot(joined, weight_latent, preferred_element_type=jnp.float32)
    updated = (latent.astype(jnp.float32) + jax.nn.silu(update)).astype(jnp.bfloat16)
    hidden = jax.nn.silu(jnp.dot(updated, weight_hidden, preferred_element_type=jnp.float32))
    edge_energy = jnp.dot(hidden, weight_readout, precision=lax.Precision.HIGHEST) * envelope
    return jnp.sum(edge_energy)

def reference(features, positions, send_ids, ghost_prefix, edge_fill, edge_src, edge_dst, weight_src, weight_dst, weight_radial, weight_env, weight_latent, weight_hidden, weight_readout):
    vectors, capacity, offsets, slot_dir, slot_index = direction_table(CAP_FACE, CAP_EDGE, CAP_CORNER)
    slot_step_x = jnp.array(vectors[slot_dir, 0]).astype(jnp.int32)
    slot_step_y = jnp.array(vectors[slot_dir, 1]).astype(jnp.int32)
    slot_step_z = jnp.array(vectors[slot_dir, 2]).astype(jnp.int32)
    slot_dir_arr = jnp.array(slot_dir).astype(jnp.int32)
    slot_index_arr = jnp.array(slot_index).astype(jnp.int32)
    slot_vec = jnp.array(vectors[slot_dir].T).astype(jnp.float32)
    counts = ghost_prefix[:, 1:] - ghost_prefix[:, :-1]
    norm = float(NEIGHBOURS)

    def one_device(device):
        coord_x = device // (DOM_Y * ZDOM)
        coord_y = device // ZDOM % DOM_Y
        coord_z = device % ZDOM
        source_x = (coord_x - slot_step_x) % DOM_X
        source_y = (coord_y - slot_step_y) % DOM_Y
        source_z = (coord_z - slot_step_z) % ZDOM
        source = ((source_x * DOM_Y + source_y) * ZDOM + source_z).astype(jnp.int32)
        live_slot = (slot_index_arr < counts[source, slot_dir_arr]).astype(jnp.float32)
        list_start = (ghost_prefix[source, slot_dir_arr] + slot_index_arr).astype(jnp.int32)
        global_row = (source * ATOMS + send_ids[source, list_start]).astype(jnp.int32)
        ghost_feat = features[global_row] * live_slot[:, None]
        ghost_pos = positions[:, global_row] * live_slot[None, :] - slot_vec
        own_feat = lax.dynamic_slice_in_dim(features, (device * ATOMS).astype(jnp.int32), ATOMS, 0)
        own_pos = lax.dynamic_slice_in_dim(positions, (device * ATOMS).astype(jnp.int32), ATOMS, 1)
        node_pos = jnp.concatenate([own_pos, ghost_pos], axis=1)
        node_feat = jnp.concatenate([own_feat, ghost_feat], axis=0)
        node_live = jnp.concatenate([jnp.ones((ATOMS,), jnp.float32), live_slot])

        def energy_of(pos_in, feat_in):
            return local_energy(pos_in, feat_in, node_live, edge_src[device], edge_dst[device], edge_fill[device], ATOMS, norm, weight_src, weight_dst, weight_radial, weight_env, weight_latent, weight_hidden, weight_readout)
        energy, pullback = jax.vjp(energy_of, node_pos, node_feat)
        grad_pos, grad_feat = pullback(jnp.ones_like(energy))
        return (grad_pos, grad_feat, global_row, live_slot)
    grad_pos, grad_feat, rows, live_all = lax.map(one_device, jnp.arange(DOMS).astype(jnp.int32))
    own_pos_grad = jnp.transpose(grad_pos[:, :, :ATOMS], (1, 0, 2)).reshape(3, ATOMS_ALL)
    ghost_pos_grad = jnp.transpose(grad_pos[:, :, ATOMS:] * live_all[:, None, :], (0, 2, 1)).reshape(-1, 3)
    flat_rows = rows.reshape(-1)
    returned_pos = jax.ops.segment_sum(ghost_pos_grad, flat_rows, num_segments=ATOMS_ALL)
    forces = -(own_pos_grad + returned_pos.T)
    own_feat_grad = grad_feat[:, :ATOMS].reshape(ATOMS_ALL, CHANNELS)
    ghost_feat_grad = (grad_feat[:, ATOMS:] * live_all[:, :, None]).reshape(-1, CHANNELS)
    feat_grad = own_feat_grad + jax.ops.segment_sum(ghost_feat_grad, flat_rows, num_segments=ATOMS_ALL)
    return (forces, feat_grad)
```

```python
import math

import jax
import jax.numpy as jnp
import numpy as np
from jax import lax
from jax.experimental import pallas as pl
from jax.experimental.pallas import tpu as pltpu
from jax.sharding import PartitionSpec as P

NEIGHBOURS = 4
CAPS = (0, 64, 16, 4)
ROW_Y = 8

ATOMS = 128
EDGES = 512
CH = 128
SLOTS = 640
SHARPNESS = 8.0
VMEM = 56 * 1024 * 1024

BF16 = jnp.bfloat16
F32 = jnp.float32
MESH = pl.DeviceIdType.MESH


def directions():
    table = []
    offset = 0
    number = 0
    for a in (-1, 0, 1):
        for b in (-1, 0, 1):
            for c in (-1, 0, 1):
                kind = abs(a) + abs(b) + abs(c)
                if kind == 0:
                    continue
                cap = CAPS[kind]
                table.append(dict(vec=(a, b, c), kind=kind, cap=cap, number=number, offset=offset))
                offset += cap
                number += 1
    table.sort(key=lambda d: (d["kind"], d["number"]))
    row = 0
    slot = 0
    for d in table:
        d["rows"] = {1: 64, 2: 16, 3: 8}[d["kind"]]
        d["slot"] = slot
        d["at"] = row
        d["size"] = {1: 72, 2: 24, 3: 8}[d["kind"]]
        d["tile"] = row + {1: 64, 2: 16, 3: 0}[d["kind"]]
        slot += d["rows"]
        row += d["size"]
    assert slot == SLOTS
    return table, row


TABLE, PACK = directions()


def mm(a, b):
    return lax.dot_general(a, b, (((1,), (0,)), ((), ())), preferred_element_type=F32)


def nt(a, b):
    return lax.dot_general(a, b, (((1,), (1,)), ((), ())), preferred_element_type=F32)


def tn(a, b):
    return lax.dot_general(a, b, (((0,), (0,)), ((), ())), preferred_element_type=F32)


def iota(shape, dim):
    return lax.broadcasted_iota(jnp.int32, shape, dim)


def onehot(cond):
    return jnp.where(cond, 1.0, 0.0).astype(BF16)


def split(x, pieces):
    out = []
    for step in range(pieces):
        part = x.astype(BF16)
        out.append(part)
        if step + 1 < pieces:
            x = x - part.astype(F32)
    return out


def split_rows(x, pieces):
    parts = []
    for step in range(pieces):
        part = x.astype(BF16).astype(F32)
        parts.append(part)
        x = x - part
    if pieces % 2:
        parts.append(jnp.zeros_like(x))
    return jnp.concatenate(parts, axis=0).astype(BF16)


def sum_pieces(x, pieces):
    total = x[0:8]
    for step in range(1, pieces):
        total = total + x[8 * step : 8 * step + 8]
    return total


def sigmoid(v):
    return 0.5 * jnp.tanh(0.5 * v) + 0.5


def silu_pair(v):
    sig = sigmoid(v)
    value = v * sig
    return value, sig + value * (1.0 - sig)


def rows_to_eight(rows, first):
    place = iota((8, rows[0].shape[1]), 0)
    out = jnp.zeros((8, rows[0].shape[1]), F32)
    for step, row in enumerate(rows):
        out = jnp.where(place == first + step, row, out)
    return out


def slot_ids(dst_row):
    blocks = []
    for d in TABLE:
        if d["kind"] <= 2:
            place = iota((d["rows"], EDGES), 0) + (ATOMS + d["offset"])
            blocks.append(onehot(place == dst_row))
    corners = [d for d in TABLE if d["kind"] == 3]
    place = iota((8 * len(corners), EDGES), 0)
    inner = place % 8
    base = jnp.zeros_like(place)
    for step, d in enumerate(corners):
        base = jnp.where(place // 8 == step, ATOMS + d["offset"], base)
    blocks.append(onehot((inner < 4) & (base + inner == dst_row)))
    return jnp.concatenate(blocks, axis=0)


def edge_pass(pre_nodes, pos_i, pos_j, in_fill, same, w):
    diff = pos_j - pos_i
    qx, qy, qz = diff[4:5], diff[5:6], diff[6:7]
    live = pos_j[7:8]
    rsq = qx * qx + qy * qy + qz * qz
    in_use = in_fill * live
    inside = jnp.where(rsq < 1.0, 1.0 - rsq, 0.0)
    env = inside * inside * in_use
    centers = iota((8, EDGES), 0).astype(F32) / 7.0
    offset = rsq - centers
    radial = jnp.exp(-SHARPNESS * offset * offset)

    r3, r15, r5 = math.sqrt(3.0), math.sqrt(15.0), math.sqrt(5.0)
    y1 = rows_to_eight([r3 * qx, r3 * qy, r3 * qz], 0)
    y2 = rows_to_eight(
        [
            r15 * qx * qy,
            r15 * qy * qz,
            r15 * qz * qx,
            0.5 * r15 * (qx * qx - qy * qy),
            0.5 * r5 * (2.0 * qz * qz - qx * qx - qy * qy),
        ],
        0,
    )
    h1, l1 = (part.astype(F32) for part in split(y1, 2))
    h2, l2 = (part.astype(F32) for part in split(y2, 2))
    zero8 = jnp.zeros((8, EDGES), F32)
    left1 = jnp.concatenate([h1, h1, l1, zero8], axis=0).astype(BF16)
    right1 = jnp.concatenate([h1, l1, h1, zero8], axis=0).astype(BF16)
    left2 = jnp.concatenate([h2, h2, l2, zero8], axis=0).astype(BF16)
    right2 = jnp.concatenate([h2, l2, h2, zero8], axis=0).astype(BF16)
    k0 = same
    k1 = tn(left1, right1).astype(BF16) * same
    k2 = tn(left2, right2).astype(BF16) * same

    pre = pre_nodes + mm(w["rad_t"], radial.astype(BF16))
    act, dact = silu_pair(pre)
    latent = (act * env).astype(BF16)
    envw = mm(w["env_t"], latent).astype(BF16)
    scal0 = mm(envw, k0).astype(BF16)
    scal1 = mm(envw, k1).astype(BF16)
    scal2 = mm(envw, k2).astype(BF16)
    joined = jnp.concatenate([latent, scal0, scal1, scal2], axis=0)
    upd = mm(w["lat_t"], joined)
    upd_act, upd_d = silu_pair(upd)
    updated = (latent.astype(F32) + upd_act).astype(BF16)
    hid = mm(w["hid_t"], updated)
    hid_act, hid_d = silu_pair(hid)
    ro = w["ro"]
    denv = jnp.sum(hid_act * ro, axis=0, keepdims=True)
    dhid = (hid_d * ro * env).astype(BF16)
    dupdated = mm(w["hid"], dhid).astype(BF16).astype(F32)
    dupd = (dupdated * upd_d).astype(BF16)
    djoined = mm(w["lat"], dupd).astype(BF16)
    ds0 = djoined[CH : 2 * CH]
    ds1 = djoined[2 * CH : 3 * CH]
    ds2 = djoined[3 * CH :]
    denvw = (mm(ds0, k0) + mm(ds1, k1) + mm(ds2, k2)).astype(BF16)
    dlatent = dupdated + djoined[:CH].astype(F32) + mm(w["env"], denvw)
    dpre = (dlatent * env * dact).astype(BF16)
    denv = denv + jnp.sum(dlatent * act, axis=0, keepdims=True)

    envw_t = envw.T
    t1 = mm(jnp.concatenate([ds1.T, envw_t], axis=1), jnp.concatenate([envw, ds1], axis=0)).astype(BF16) * same
    t2 = mm(jnp.concatenate([ds2.T, envw_t], axis=1), jnp.concatenate([envw, ds2], axis=0)).astype(BF16) * same
    dy1 = mm(left1, t1)
    dy1 = dy1[0:8] + dy1[16:24]
    dy2 = mm(left2, t2)
    dy2 = dy2[0:8] + dy2[16:24]

    drad = mm(w["rad"], dpre)
    drsq = jnp.sum(drad * radial * offset, axis=0, keepdims=True) * (-2.0 * SHARPNESS)
    drsq = drsq - 2.0 * denv * in_use * inside
    a0, a1, a2, a3, a4 = (dy2[step : step + 1] for step in range(5))
    two = 2.0 * drsq
    gx = two * qx + r3 * dy1[0:1] + r15 * (a0 * qy + a2 * qz + a3 * qx) - r5 * a4 * qx
    gy = two * qy + r3 * dy1[1:2] + r15 * (a0 * qx + a1 * qz - a3 * qy) - r5 * a4 * qy
    gz = two * qz + r3 * dy1[2:3] + r15 * (a1 * qy + a2 * qx) + 2.0 * r5 * a4 * qz
    return dpre, rows_to_eight([gx, gy, gz], 4)


def kernel(
    prefix_hbm,
    fill_hbm,
    feat_hbm,
    pos_hbm,
    send_hbm,
    src_hbm,
    dst_hbm,
    wsrc_hbm,
    wdst_hbm,
    wrad_hbm,
    wenv_hbm,
    wlat_hbm,
    whid_hbm,
    wro_hbm,
    force_ref,
    grad_ref,
    prefix,
    fill,
    feat_v,
    pos_v,
    send_v,
    src_v,
    dst_v,
    wsrc_v,
    wdst_v,
    wrad_v,
    wenv_v,
    wlat_v,
    whid_v,
    wro_v,
    list_v,
    pick_v,
    out1,
    in1,
    out2,
    in2,
    in_sem,
    s1,
    r1,
    s2,
    r2,
):
    planes = lax.axis_size("dom") // ROW_Y
    depth = lax.axis_size("gz")
    dom = lax.axis_index("dom")
    cz = lax.axis_index("gz")
    cx, cy = dom // ROW_Y, dom % ROW_Y

    def place(vec, sign):
        x = (cx + sign * vec[0] + planes) % planes
        y = (cy + sign * vec[1] + ROW_Y) % ROW_Y
        z = (cz + sign * vec[2] + depth) % depth
        return (x * ROW_Y + y, z)

    loads = []
    for step, (source, target) in enumerate(
        [
            (send_hbm, send_v),
            (prefix_hbm, prefix),
            (feat_hbm, feat_v),
            (pos_hbm, pos_v),
            (src_hbm, src_v),
            (dst_hbm, dst_v),
            (wsrc_hbm, wsrc_v),
            (wdst_hbm, wdst_v),
            (wrad_hbm, wrad_v),
            (wenv_hbm, wenv_v),
            (wlat_hbm, wlat_v),
            (whid_hbm, whid_v),
            (wro_hbm, wro_v),
            (fill_hbm, fill),
        ]
    ):
        copy = pltpu.make_async_copy(source, target, in_sem.at[step])
        copy.start()
        loads.append(copy)

    barrier = pltpu.get_barrier_semaphore()
    for d in TABLE:
        pl.semaphore_signal(barrier, inc=1, device_id=place(d["vec"], 1), device_id_type=MESH)

    loads[0].wait()
    listed = jnp.where(iota((ATOMS, 608), 0) == send_v[...], 1.0, 0.0)
    list_v[0:608, :] = listed.T
    list_v[608:640, :] = jnp.zeros((32, ATOMS), F32)
    loads[1].wait()
    loads[2].wait()
    loads[3].wait()
    feat16 = feat_v[...].astype(BF16)
    pos = pos_v[...]
    own8 = rows_to_eight([pos[0:1], pos[1:2], pos[2:3], jnp.ones((1, ATOMS), F32)], 4)
    own_pieces = split_rows(own8, 3)
    lane = iota((8, 128), 1)
    line = iota((8, 128), 0)

    def store(ref, table, lines, slots, shifted):
        base = table[0]["slot"]
        for d in table:
            first = d["slot"] - base
            tile, low = first // 128 * 128, d["slot"] % 128
            inside = (lane >= low) & (lane < low + d["rows"]) & (line >= 4)
            coords = slots[:, tile : tile + 128]
            if shifted:
                shift = jnp.zeros((8, 128), F32)
                for step in range(3):
                    if d["vec"][step]:
                        shift = jnp.where(line == 4 + step, float(d["vec"][step]), shift)
                coords = coords - shift
            coords = jnp.where(inside, coords, 0.0)
            part = lines[first : first + d["rows"]]
            if d["kind"] == 3:
                ref[d["at"] : d["at"] + 8, :] = jnp.where(line < 4, part, coords)
            else:
                ref[d["at"] : d["at"] + d["rows"], :] = part
                ref[d["tile"] : d["tile"] + 8, :] = coords

    def send(table, source, target, send_sem, recv_sem, sign):
        for d in table:
            rows = pl.ds(d["at"], d["size"])
            pltpu.make_async_remote_copy(
                src_ref=source.at[rows],
                dst_ref=target.at[rows],
                send_sem=send_sem,
                recv_sem=recv_sem,
                device_id=place(d["vec"], sign),
                device_id_type=MESH,
            ).start()

    groups = [[d for d in TABLE if d["kind"] == 1], [d for d in TABLE if d["kind"] > 1]]
    picks = []
    for step, table in enumerate(groups):
        for d in table:
            n, rows = d["number"], d["rows"]
            count = prefix[0, n + 1] - prefix[0, n]
            lines = list_v[pl.ds(prefix[0, n], rows), :]
            pick_v[d["slot"] : d["slot"] + rows, :] = jnp.where(iota((rows, ATOMS), 0) < count, lines, 0.0)
        first, last = table[0]["slot"], table[-1]["slot"] + table[-1]["rows"]
        pick = pick_v[first:last, :].astype(BF16)
        picks.append(pick)
        store(out1, table, mm(pick, feat16), sum_pieces(nt(own_pieces, pick), 3), True)
        if step == 0:
            pl.semaphore_wait(barrier, len(TABLE))
        send(table, out1, in1, s1, r1, 1)
    pick = jnp.concatenate(picks, axis=0)

    for copy in loads[4:]:
        copy.wait()
    src_row, dst_row = src_v[...], dst_v[...]
    centre = onehot(iota((ATOMS, EDGES), 0) == src_row)
    near = onehot(iota((ATOMS, EDGES), 0) == dst_row)
    ghost = slot_ids(dst_row)
    same = (tn(centre, centre) * (1.0 / NEIGHBOURS)).astype(BF16)
    in_fill = jnp.where(iota((1, EDGES), 1) < fill[0], 1.0, 0.0)
    eye = iota((CH, CH), 0) == iota((CH, CH), 1)
    w = dict(
        dst_t=wdst_v[...].T,
        rad_t=wrad_v[...].T,
        env_t=wenv_v[...].T,
        lat_t=wlat_v[...].T,
        hid_t=whid_v[...].T,
        rad=wrad_v[...],
        env=wenv_v[...],
        lat=wlat_v[...],
        hid=whid_v[...],
        ro=jnp.sum(jnp.where(eye, wro_v[...], 0.0), axis=1, keepdims=True),
    )
    feat_t = feat16.T
    own_lhs = jnp.concatenate([feat_t, own_pieces], axis=0)
    at_i = mm(own_lhs, centre)
    at_j = mm(own_lhs, near)
    pre_own = mm(wsrc_v[...].T, at_i[:CH].astype(BF16)) + mm(w["dst_t"], at_j[:CH].astype(BF16))
    pos_i = sum_pieces(at_i[CH:], 3)
    pos_j_own = sum_pieces(at_j[CH:], 3)
    pick_t = pick.T

    def all_of(source, target, send_sem, recv_sem):
        return pltpu.make_async_remote_copy(
            src_ref=source,
            dst_ref=target,
            send_sem=send_sem,
            recv_sem=recv_sem,
            device_id=place(TABLE[0]["vec"], 1),
            device_id_type=MESH,
        )

    def unpack(ref):
        lines = jnp.concatenate([ref[d["at"] : d["at"] + d["rows"], :] for d in TABLE], axis=0)
        tiles = [None] * 5
        for d in TABLE:
            tile = d["slot"] // 128
            piece = ref[d["tile"] : d["tile"] + 8, :]
            tiles[tile] = piece if tiles[tile] is None else tiles[tile] + piece
        coords = jnp.concatenate(tiles, axis=1)
        coords = jnp.where(iota(coords.shape, 0) >= 4, coords, 0.0)
        return lines.astype(BF16), coords

    all_of(out1, in1, s1, r1).wait_recv()
    ghost_feat, ghost8 = unpack(in1)
    far = nt(w["dst_t"], ghost_feat).astype(BF16)
    arrived = mm(jnp.concatenate([far, split_rows(ghost8, 3)], axis=0), ghost)
    pos_j = pos_j_own + sum_pieces(arrived[CH:], 3)
    dpre, dq = edge_pass(pre_own + arrived[:CH], pos_i, pos_j, in_fill, same, w)

    dq_pieces = split_rows(dq, 2)
    for table in groups:
        first, last = table[0]["slot"], table[-1]["slot"] + table[-1]["rows"]
        hot = ghost[first:last]
        store(out2, table, nt(hot, dpre), sum_pieces(nt(dq_pieces, hot), 2), False)
        send(table, out2, in2, s2, r2, -1)

    own = nt(jnp.concatenate([centre, near], axis=0), dpre)
    own_src = nt(own[:ATOMS].astype(BF16), wsrc_v[...])
    own_dst = own[ATOMS:]
    own8 = sum_pieces(nt(dq_pieces, near - centre), 2)

    all_of(out2, in2, s2, r2).wait_recv()
    back_feat, back_pos = unpack(in2)
    sum_dst = own_dst + mm(pick_t, back_feat)
    grad_ref[...] = own_src + nt(sum_dst.astype(BF16), wdst_v[...])
    total8 = own8 + sum_pieces(mm(split_rows(back_pos, 2), pick), 2)
    force_ref[...] = -total8[4:7]
    all_of(out1, in1, s1, r1).wait_send()
    all_of(out2, in2, s2, r2).wait_send()


def pass_on(force_in, grad_in, force_out, grad_out, sems):
    copies = [
        pltpu.make_async_copy(force_in, force_out, sems.at[0]),
        pltpu.make_async_copy(grad_in, grad_out, sems.at[1]),
    ]
    for copy in copies:
        copy.start()
    for copy in copies:
        copy.wait()


def body(
    features,
    positions,
    send_ids,
    ghost_prefix,
    edge_fill,
    edge_src,
    edge_dst,
    weight_src,
    weight_dst,
    weight_radial,
    weight_env,
    weight_latent,
    weight_hidden,
    weight_readout,
):
    arrays = [
        features,
        positions,
        send_ids,
        edge_src,
        edge_dst,
        weight_src,
        weight_dst,
        weight_radial,
        weight_env,
        weight_latent,
        weight_hidden,
        weight_readout.reshape(1, CH),
    ]
    hbm = pl.BlockSpec(memory_space=pltpu.HBM)
    vmem = pl.BlockSpec(memory_space=pltpu.VMEM)
    results = (
        jax.ShapeDtypeStruct((3, ATOMS), F32),
        jax.ShapeDtypeStruct((ATOMS, CH), F32),
    )
    forces, feat_grad = pl.pallas_call(
        kernel,
        out_shape=results,
        in_specs=[hbm] * (2 + len(arrays)),
        out_specs=(vmem, vmem),
        scratch_shapes=[pltpu.SMEM(ghost_prefix.shape, jnp.int32), pltpu.SMEM(edge_fill.shape, jnp.int32)]
        + [pltpu.VMEM(a.shape, a.dtype) for a in arrays]
        + [
            pltpu.VMEM((SLOTS, ATOMS), F32),
            pltpu.VMEM((SLOTS, ATOMS), F32),
            pltpu.VMEM((PACK, CH), F32),
            pltpu.VMEM((PACK, CH), F32),
            pltpu.VMEM((PACK, CH), F32),
            pltpu.VMEM((PACK, CH), F32),
            pltpu.SemaphoreType.DMA((2 + len(arrays),)),
            pltpu.SemaphoreType.DMA,
            pltpu.SemaphoreType.DMA,
            pltpu.SemaphoreType.DMA,
            pltpu.SemaphoreType.DMA,
        ],
        compiler_params=pltpu.CompilerParams(
            collective_id=0, has_side_effects=True, vmem_limit_bytes=VMEM
        ),
        name="allegro",
    )(ghost_prefix, edge_fill, *arrays)
    return pl.pallas_call(
        pass_on,
        out_shape=results,
        in_specs=[hbm, hbm],
        out_specs=(hbm, hbm),
        scratch_shapes=[pltpu.SemaphoreType.DMA((2,))],
        compiler_params=pltpu.CompilerParams(vmem_limit_bytes=VMEM),
        name="pass_on",
    )(forces, feat_grad)


def solution(mesh):
    return jax.shard_map(
        body,
        mesh=mesh,
        in_specs=(
            P(("dom", "gz"), None),
            P(None, ("dom", "gz")),
            P(("dom", "gz"), None),
            P(("dom", "gz"), None),
            P(("dom", "gz")),
            P(("dom", "gz"), None),
            P(("dom", "gz"), None),
            P(),
            P(),
            P(),
            P(),
            P(),
            P(),
            P(),
        ),
        out_specs=(P(None, ("dom", "gz")), P(("dom", "gz"), None)),
        check_vma=False,
    )
```

```python
import math

import jax
import jax.numpy as jnp
import numpy as np
from jax import lax
from jax.experimental import pallas as pl
from jax.experimental.pallas import tpu as pltpu
from jax.sharding import PartitionSpec as P

NEIGHBOURS = 4
CAPS = (0, 64, 16, 4)
ROW_Y = 8

ATOMS = 128
EDGES = 512
CH = 128
SLOTS = 640
SHARPNESS = 8.0
VMEM = 56 * 1024 * 1024

BF16 = jnp.bfloat16
F32 = jnp.float32
MESH = pl.DeviceIdType.MESH


def directions():
    table = []
    offset = 0
    number = 0
    for a in (-1, 0, 1):
        for b in (-1, 0, 1):
            for c in (-1, 0, 1):
                kind = abs(a) + abs(b) + abs(c)
                if kind == 0:
                    continue
                cap = CAPS[kind]
                table.append(dict(vec=(a, b, c), kind=kind, cap=cap, number=number, offset=offset))
                offset += cap
                number += 1
    table.sort(key=lambda d: (d["kind"], d["number"]))
    row = 0
    slot = 0
    for d in table:
        d["rows"] = {1: 64, 2: 16, 3: 8}[d["kind"]]
        d["slot"] = slot
        d["at"] = row
        d["size"] = {1: 72, 2: 24, 3: 8}[d["kind"]]
        d["tile"] = row + {1: 64, 2: 16, 3: 0}[d["kind"]]
        slot += d["rows"]
        row += d["size"]
    assert slot == SLOTS
    return table, row


TABLE, PACK = directions()


def mm(a, b):
    return lax.dot_general(a, b, (((1,), (0,)), ((), ())), preferred_element_type=F32)


def nt(a, b):
    return lax.dot_general(a, b, (((1,), (1,)), ((), ())), preferred_element_type=F32)


def tn(a, b):
    return lax.dot_general(a, b, (((0,), (0,)), ((), ())), preferred_element_type=F32)


def iota(shape, dim):
    return lax.broadcasted_iota(jnp.int32, shape, dim)


def onehot(cond):
    return jnp.where(cond, 1.0, 0.0).astype(BF16)


def split(x, pieces):
    out = []
    for step in range(pieces):
        part = x.astype(BF16)
        out.append(part)
        if step + 1 < pieces:
            x = x - part.astype(F32)
    return out


def split_rows(x, pieces):
    parts = []
    for step in range(pieces):
        part = x.astype(BF16).astype(F32)
        parts.append(part)
        x = x - part
    if pieces % 2:
        parts.append(jnp.zeros_like(x))
    return jnp.concatenate(parts, axis=0).astype(BF16)


def sum_pieces(x, pieces):
    total = x[0:8]
    for step in range(1, pieces):
        total = total + x[8 * step : 8 * step + 8]
    return total


def sigmoid(v):
    return 0.5 * jnp.tanh(0.5 * v) + 0.5


def silu_pair(v):
    sig = sigmoid(v)
    value = v * sig
    return value, sig + value * (1.0 - sig)


def rows_to_eight(rows, first):
    place = iota((8, rows[0].shape[1]), 0)
    out = jnp.zeros((8, rows[0].shape[1]), F32)
    for step, row in enumerate(rows):
        out = jnp.where(place == first + step, row, out)
    return out


def slot_ids(dst_row):
    blocks = []
    for d in TABLE:
        if d["kind"] <= 2:
            place = iota((d["rows"], EDGES), 0) + (ATOMS + d["offset"])
            blocks.append(onehot(place == dst_row))
    corners = [d for d in TABLE if d["kind"] == 3]
    place = iota((8 * len(corners), EDGES), 0)
    inner = place % 8
    base = jnp.zeros_like(place)
    for step, d in enumerate(corners):
        base = jnp.where(place // 8 == step, ATOMS + d["offset"], base)
    blocks.append(onehot((inner < 4) & (base + inner == dst_row)))
    return jnp.concatenate(blocks, axis=0)


def edge_pass(pre_nodes, pos_i, pos_j, in_fill, same, w):
    diff = pos_j - pos_i
    qx, qy, qz = diff[4:5], diff[5:6], diff[6:7]
    live = pos_j[7:8]
    rsq = qx * qx + qy * qy + qz * qz
    in_use = in_fill * live
    inside = jnp.where(rsq < 1.0, 1.0 - rsq, 0.0)
    env = inside * inside * in_use
    centers = iota((8, EDGES), 0).astype(F32) / 7.0
    offset = rsq - centers
    radial = jnp.exp(-SHARPNESS * offset * offset)

    r3, r15, r5 = math.sqrt(3.0), math.sqrt(15.0), math.sqrt(5.0)
    y1 = rows_to_eight([r3 * qx, r3 * qy, r3 * qz], 0)
    y2 = rows_to_eight(
        [
            r15 * qx * qy,
            r15 * qy * qz,
            r15 * qz * qx,
            0.5 * r15 * (qx * qx - qy * qy),
            0.5 * r5 * (2.0 * qz * qz - qx * qx - qy * qy),
        ],
        0,
    )
    h1, l1 = (part.astype(F32) for part in split(y1, 2))
    h2, l2 = (part.astype(F32) for part in split(y2, 2))
    zero8 = jnp.zeros((8, EDGES), F32)
    left1 = jnp.concatenate([h1, h1, l1, zero8], axis=0).astype(BF16)
    right1 = jnp.concatenate([h1, l1, h1, zero8], axis=0).astype(BF16)
    left2 = jnp.concatenate([h2, h2, l2, zero8], axis=0).astype(BF16)
    right2 = jnp.concatenate([h2, l2, h2, zero8], axis=0).astype(BF16)
    k0 = same
    k1 = tn(left1, right1).astype(BF16) * same
    k2 = tn(left2, right2).astype(BF16) * same

    pre = pre_nodes + mm(w["rad_t"], radial.astype(BF16))
    act, dact = silu_pair(pre)
    latent = (act * env).astype(BF16)
    envw = mm(w["env_t"], latent).astype(BF16)
    scal0 = mm(envw, k0).astype(BF16)
    scal1 = mm(envw, k1).astype(BF16)
    scal2 = mm(envw, k2).astype(BF16)
    joined = jnp.concatenate([latent, scal0, scal1, scal2], axis=0)
    upd = mm(w["lat_t"], joined)
    upd_act, upd_d = silu_pair(upd)
    updated = (latent.astype(F32) + upd_act).astype(BF16)
    hid = mm(w["hid_t"], updated)
    hid_act, hid_d = silu_pair(hid)
    ro = w["ro"]
    denv = jnp.sum(hid_act * ro, axis=0, keepdims=True)
    dhid = (hid_d * ro * env).astype(BF16)
    dupdated = mm(w["hid"], dhid).astype(BF16).astype(F32)
    dupd = (dupdated * upd_d).astype(BF16)
    djoined = mm(w["lat"], dupd).astype(BF16)
    ds0 = djoined[CH : 2 * CH]
    ds1 = djoined[2 * CH : 3 * CH]
    ds2 = djoined[3 * CH :]
    denvw = (mm(ds0, k0) + mm(ds1, k1) + mm(ds2, k2)).astype(BF16)
    dlatent = dupdated + djoined[:CH].astype(F32) + mm(w["env"], denvw)
    dpre = (dlatent * env * dact).astype(BF16)
    denv = denv + jnp.sum(dlatent * act, axis=0, keepdims=True)

    envw_t = envw.T
    t1 = mm(jnp.concatenate([ds1.T, envw_t], axis=1), jnp.concatenate([envw, ds1], axis=0)).astype(BF16) * same
    t2 = mm(jnp.concatenate([ds2.T, envw_t], axis=1), jnp.concatenate([envw, ds2], axis=0)).astype(BF16) * same
    dy1 = mm(left1, t1)
    dy1 = dy1[0:8] + dy1[16:24]
    dy2 = mm(left2, t2)
    dy2 = dy2[0:8] + dy2[16:24]

    drad = mm(w["rad"], dpre)
    drsq = jnp.sum(drad * radial * offset, axis=0, keepdims=True) * (-2.0 * SHARPNESS)
    drsq = drsq - 2.0 * denv * in_use * inside
    a0, a1, a2, a3, a4 = (dy2[step : step + 1] for step in range(5))
    two = 2.0 * drsq
    gx = two * qx + r3 * dy1[0:1] + r15 * (a0 * qy + a2 * qz + a3 * qx) - r5 * a4 * qx
    gy = two * qy + r3 * dy1[1:2] + r15 * (a0 * qx + a1 * qz - a3 * qy) - r5 * a4 * qy
    gz = two * qz + r3 * dy1[2:3] + r15 * (a1 * qy + a2 * qx) + 2.0 * r5 * a4 * qz
    return dpre, rows_to_eight([gx, gy, gz], 4)


def unpack(ref):
    lines = jnp.concatenate([ref[d["at"] : d["at"] + d["rows"], :] for d in TABLE], axis=0)
    tiles = [None] * 5
    for d in TABLE:
        tile = d["slot"] // 128
        piece = ref[d["tile"] : d["tile"] + 8, :]
        tiles[tile] = piece if tiles[tile] is None else tiles[tile] + piece
    coords = jnp.concatenate(tiles, axis=1)
    coords = jnp.where(iota(coords.shape, 0) >= 4, coords, 0.0)
    return lines.astype(BF16), coords


def kernel(
    prefix_hbm,
    fill_hbm,
    feat_hbm,
    pos_hbm,
    send_hbm,
    src_hbm,
    dst_hbm,
    wsrc_hbm,
    wdst_hbm,
    wrad_hbm,
    wenv_hbm,
    wlat_hbm,
    whid_hbm,
    wro_hbm,
    in2,
    own_hbm,
    pick_hbm,
    prefix,
    fill,
    feat_v,
    pos_v,
    send_v,
    src_v,
    dst_v,
    wsrc_v,
    wdst_v,
    wrad_v,
    wenv_v,
    wlat_v,
    whid_v,
    wro_v,
    list_v,
    pick_v,
    out1,
    in1,
    out2,
    own_v,
    pick_t_v,
    in_sem,
    s1,
    r1,
    s2,
    r2,
    out_sem,
):
    planes = lax.axis_size("dom") // ROW_Y
    depth = lax.axis_size("gz")
    dom = lax.axis_index("dom")
    cz = lax.axis_index("gz")
    cx, cy = dom // ROW_Y, dom % ROW_Y

    def place(vec, sign):
        x = (cx + sign * vec[0] + planes) % planes
        y = (cy + sign * vec[1] + ROW_Y) % ROW_Y
        z = (cz + sign * vec[2] + depth) % depth
        return (x * ROW_Y + y, z)

    loads = []
    for step, (source, target) in enumerate(
        [
            (send_hbm, send_v),
            (prefix_hbm, prefix),
            (feat_hbm, feat_v),
            (pos_hbm, pos_v),
            (src_hbm, src_v),
            (dst_hbm, dst_v),
            (wsrc_hbm, wsrc_v),
            (wdst_hbm, wdst_v),
            (wrad_hbm, wrad_v),
            (wenv_hbm, wenv_v),
            (wlat_hbm, wlat_v),
            (whid_hbm, whid_v),
            (wro_hbm, wro_v),
            (fill_hbm, fill),
        ]
    ):
        copy = pltpu.make_async_copy(source, target, in_sem.at[step])
        copy.start()
        loads.append(copy)

    barrier = pltpu.get_barrier_semaphore()
    for d in TABLE:
        pl.semaphore_signal(barrier, inc=1, device_id=place(d["vec"], 1), device_id_type=MESH)

    loads[0].wait()
    listed = jnp.where(iota((ATOMS, 608), 0) == send_v[...], 1.0, 0.0)
    list_v[0:608, :] = listed.T
    list_v[608:640, :] = jnp.zeros((32, ATOMS), F32)
    loads[1].wait()
    loads[2].wait()
    loads[3].wait()
    feat16 = feat_v[...].astype(BF16)
    pos = pos_v[...]
    own8 = rows_to_eight([pos[0:1], pos[1:2], pos[2:3], jnp.ones((1, ATOMS), F32)], 4)
    own_pieces = split_rows(own8, 3)
    lane = iota((8, 128), 1)
    line = iota((8, 128), 0)

    def store(ref, table, lines, slots, shifted):
        base = table[0]["slot"]
        for d in table:
            first = d["slot"] - base
            tile, low = first // 128 * 128, d["slot"] % 128
            inside = (lane >= low) & (lane < low + d["rows"]) & (line >= 4)
            coords = slots[:, tile : tile + 128]
            if shifted:
                shift = jnp.zeros((8, 128), F32)
                for step in range(3):
                    if d["vec"][step]:
                        shift = jnp.where(line == 4 + step, float(d["vec"][step]), shift)
                coords = coords - shift
            coords = jnp.where(inside, coords, 0.0)
            part = lines[first : first + d["rows"]]
            if d["kind"] == 3:
                ref[d["at"] : d["at"] + 8, :] = jnp.where(line < 4, part, coords)
            else:
                ref[d["at"] : d["at"] + d["rows"], :] = part
                ref[d["tile"] : d["tile"] + 8, :] = coords

    def send(table, source, target, send_sem, recv_sem, sign):
        for d in table:
            rows = pl.ds(d["at"], d["size"])
            pltpu.make_async_remote_copy(
                src_ref=source.at[rows],
                dst_ref=target.at[rows],
                send_sem=send_sem,
                recv_sem=recv_sem,
                device_id=place(d["vec"], sign),
                device_id_type=MESH,
            ).start()

    groups = [[d for d in TABLE if d["kind"] == 1], [d for d in TABLE if d["kind"] > 1]]
    picks = []
    for step, table in enumerate(groups):
        for d in table:
            n, rows = d["number"], d["rows"]
            count = prefix[0, n + 1] - prefix[0, n]
            lines = list_v[pl.ds(prefix[0, n], rows), :]
            pick_v[d["slot"] : d["slot"] + rows, :] = jnp.where(iota((rows, ATOMS), 0) < count, lines, 0.0)
        first, last = table[0]["slot"], table[-1]["slot"] + table[-1]["rows"]
        pick = pick_v[first:last, :].astype(BF16)
        picks.append(pick)
        store(out1, table, mm(pick, feat16), sum_pieces(nt(own_pieces, pick), 3), True)
        if step == 0:
            pl.semaphore_wait(barrier, len(TABLE))
        send(table, out1, in1, s1, r1, 1)
    pick = jnp.concatenate(picks, axis=0)

    for copy in loads[4:]:
        copy.wait()
    src_row, dst_row = src_v[...], dst_v[...]
    centre = onehot(iota((ATOMS, EDGES), 0) == src_row)
    near = onehot(iota((ATOMS, EDGES), 0) == dst_row)
    ghost = slot_ids(dst_row)
    same = (tn(centre, centre) * (1.0 / NEIGHBOURS)).astype(BF16)
    in_fill = jnp.where(iota((1, EDGES), 1) < fill[...], 1.0, 0.0)
    eye = iota((CH, CH), 0) == iota((CH, CH), 1)
    w = dict(
        dst_t=wdst_v[...].T,
        rad_t=wrad_v[...].T,
        env_t=wenv_v[...].T,
        lat_t=wlat_v[...].T,
        hid_t=whid_v[...].T,
        rad=wrad_v[...],
        env=wenv_v[...],
        lat=wlat_v[...],
        hid=whid_v[...],
        ro=jnp.sum(jnp.where(eye, wro_v[...], 0.0), axis=1, keepdims=True),
    )
    feat_t = feat16.T
    own_lhs = jnp.concatenate([feat_t, own_pieces], axis=0)
    at_i = mm(own_lhs, centre)
    at_j = mm(own_lhs, near)
    pre_own = mm(wsrc_v[...].T, at_i[:CH].astype(BF16)) + mm(w["dst_t"], at_j[:CH].astype(BF16))
    pos_i = sum_pieces(at_i[CH:], 3)
    pos_j_own = sum_pieces(at_j[CH:], 3)
    pick_t_v[...] = pick.T
    pick_out = pltpu.make_async_copy(pick_t_v, pick_hbm, out_sem.at[0])
    pick_out.start()

    def all_of(source, target, send_sem, recv_sem):
        return pltpu.make_async_remote_copy(
            src_ref=source,
            dst_ref=target,
            send_sem=send_sem,
            recv_sem=recv_sem,
            device_id=place(TABLE[0]["vec"], 1),
            device_id_type=MESH,
        )

    all_of(out1, in1, s1, r1).wait_recv()
    ghost_feat, ghost8 = unpack(in1)
    far = nt(w["dst_t"], ghost_feat).astype(BF16)
    arrived = mm(jnp.concatenate([far, split_rows(ghost8, 3)], axis=0), ghost)
    pos_j = pos_j_own + sum_pieces(arrived[CH:], 3)
    dpre, dq = edge_pass(pre_own + arrived[:CH], pos_i, pos_j, in_fill, same, w)

    dq_pieces = split_rows(dq, 2)
    for table in groups:
        first, last = table[0]["slot"], table[-1]["slot"] + table[-1]["rows"]
        hot = ghost[first:last]
        store(out2, table, nt(hot, dpre), sum_pieces(nt(dq_pieces, hot), 2), False)
        send(table, out2, in2, s2, r2, -1)

    own = nt(jnp.concatenate([centre, near], axis=0), dpre).astype(BF16)
    own_v[0:ATOMS, :] = nt(own[:ATOMS], wsrc_v[...]) + nt(own[ATOMS:], wdst_v[...])
    own_v[ATOMS:, :] = sum_pieces(nt(dq_pieces, near - centre), 2)
    own_out = pltpu.make_async_copy(own_v, own_hbm, out_sem.at[1])
    own_out.start()

    pick_out.wait()
    own_out.wait()
    all_of(out1, in1, s1, r1).wait_send()
    all_of(out2, in2, s2, r2).wait()


def finish(back_ref, own_ref, pick_ref, wdst_ref, force_ref, grad_ref):
    back_feat, back_pos = unpack(back_ref)
    pick_t = pick_ref[...]
    returned = mm(pick_t, back_feat).astype(BF16)
    grad_ref[...] = own_ref[0:ATOMS, :] + nt(returned, wdst_ref[...])
    total8 = own_ref[ATOMS:, :] + sum_pieces(nt(split_rows(back_pos, 2), pick_t), 2)
    force_ref[...] = -total8[4:7]


def body(
    features,
    positions,
    send_ids,
    ghost_prefix,
    edge_fill,
    edge_src,
    edge_dst,
    weight_src,
    weight_dst,
    weight_radial,
    weight_env,
    weight_latent,
    weight_hidden,
    weight_readout,
):
    arrays = [
        features,
        positions,
        send_ids,
        edge_src,
        edge_dst,
        weight_src,
        weight_dst,
        weight_radial,
        weight_env,
        weight_latent,
        weight_hidden,
        weight_readout.reshape(1, CH),
    ]
    hbm = pl.BlockSpec(memory_space=pltpu.HBM)
    vmem = pl.BlockSpec(memory_space=pltpu.VMEM)
    back, own, pick_t = pl.pallas_call(
        kernel,
        out_shape=(
            jax.ShapeDtypeStruct((PACK, CH), F32),
            jax.ShapeDtypeStruct((ATOMS + 8, CH), F32),
            jax.ShapeDtypeStruct((ATOMS, SLOTS), BF16),
        ),
        in_specs=[hbm] * (2 + len(arrays)),
        out_specs=(hbm, hbm, hbm),
        scratch_shapes=[pltpu.SMEM(ghost_prefix.shape, jnp.int32), pltpu.VMEM((1, 1), jnp.int32)]
        + [pltpu.VMEM(a.shape, a.dtype) for a in arrays]
        + [
            pltpu.VMEM((SLOTS, ATOMS), F32),
            pltpu.VMEM((SLOTS, ATOMS), F32),
            pltpu.VMEM((PACK, CH), F32),
            pltpu.VMEM((PACK, CH), F32),
            pltpu.VMEM((PACK, CH), F32),
            pltpu.VMEM((ATOMS + 8, CH), F32),
            pltpu.VMEM((ATOMS, SLOTS), BF16),
            pltpu.SemaphoreType.DMA((2 + len(arrays),)),
            pltpu.SemaphoreType.DMA,
            pltpu.SemaphoreType.DMA,
            pltpu.SemaphoreType.DMA,
            pltpu.SemaphoreType.DMA,
            pltpu.SemaphoreType.DMA((2,)),
        ],
        compiler_params=pltpu.CompilerParams(collective_id=0, has_side_effects=True, vmem_limit_bytes=VMEM),
        name="allegro",
    )(ghost_prefix, edge_fill.reshape(1, 1), *arrays)
    return pl.pallas_call(
        finish,
        out_shape=(
            jax.ShapeDtypeStruct((3, ATOMS), F32),
            jax.ShapeDtypeStruct((ATOMS, CH), F32),
        ),
        in_specs=[vmem] * 4,
        out_specs=(vmem, vmem),
        compiler_params=pltpu.CompilerParams(vmem_limit_bytes=VMEM),
        name="finish",
    )(back, own, pick_t, weight_dst)


def solution(mesh):
    return jax.shard_map(
        body,
        mesh=mesh,
        in_specs=(
            P(("dom", "gz"), None),
            P(None, ("dom", "gz")),
            P(("dom", "gz"), None),
            P(("dom", "gz"), None),
            P(("dom", "gz")),
            P(("dom", "gz"), None),
            P(("dom", "gz"), None),
            P(),
            P(),
            P(),
            P(),
            P(),
            P(),
            P(),
        ),
        out_specs=(P(None, ("dom", "gz")), P(("dom", "gz"), None)),
        check_vma=False,
    )
```

```python
import math

import jax
import jax.numpy as jnp
import numpy as np
from jax import lax
from jax.experimental import pallas as pl
from jax.experimental.pallas import tpu as pltpu
from jax.sharding import PartitionSpec as P

NEIGHBOURS = 4
CAPS = (0, 64, 16, 4)
ROW_Y = 8

ATOMS = 128
EDGES = 512
CH = 128
SLOTS = 640
SHARPNESS = 8.0
VMEM = 56 * 1024 * 1024

BF16 = jnp.bfloat16
F32 = jnp.float32
MESH = pl.DeviceIdType.MESH


def directions():
    table = []
    offset = 0
    number = 0
    for a in (-1, 0, 1):
        for b in (-1, 0, 1):
            for c in (-1, 0, 1):
                kind = abs(a) + abs(b) + abs(c)
                if kind == 0:
                    continue
                cap = CAPS[kind]
                table.append(dict(vec=(a, b, c), kind=kind, cap=cap, number=number, offset=offset))
                offset += cap
                number += 1
    table.sort(key=lambda d: (d["kind"], d["number"]))
    slot = 0
    for step, d in enumerate(table):
        d["rows"] = {1: 64, 2: 16, 3: 8}[d["kind"]]
        d["slot"] = slot
        d["tile"] = 8 * step
        slot += d["rows"]
    assert slot == SLOTS
    return table


TABLE = directions()
FEAT_SENT = sum(d["cap"] for d in TABLE)
COORDS = 8 * len(TABLE)
COORDS_SENT = 4 * len(TABLE)


def mm(a, b):
    return lax.dot_general(a, b, (((1,), (0,)), ((), ())), preferred_element_type=F32)


def nt(a, b):
    return lax.dot_general(a, b, (((1,), (1,)), ((), ())), preferred_element_type=F32)


def tn(a, b):
    return lax.dot_general(a, b, (((0,), (0,)), ((), ())), preferred_element_type=F32)


def iota(shape, dim):
    return lax.broadcasted_iota(jnp.int32, shape, dim)


def onehot(cond):
    return jnp.where(cond, 1.0, 0.0).astype(BF16)


def split(x, pieces):
    out = []
    for step in range(pieces):
        part = x.astype(BF16)
        out.append(part)
        if step + 1 < pieces:
            x = x - part.astype(F32)
    return out


def split_rows(x, pieces):
    parts = []
    for step in range(pieces):
        part = x.astype(BF16).astype(F32)
        parts.append(part)
        x = x - part
    if pieces % 2:
        parts.append(jnp.zeros_like(x))
    return jnp.concatenate(parts, axis=0).astype(BF16)


def sum_pieces(x, pieces):
    total = x[0:8]
    for step in range(1, pieces):
        total = total + x[8 * step : 8 * step + 8]
    return total


def sigmoid(v):
    return 0.5 * jnp.tanh(0.5 * v) + 0.5


def silu_pair(v):
    sig = sigmoid(v)
    value = v * sig
    return value, sig + value * (1.0 - sig)


def rows_to_eight(rows, first):
    place = iota((8, rows[0].shape[1]), 0)
    out = jnp.zeros((8, rows[0].shape[1]), F32)
    for step, row in enumerate(rows):
        out = jnp.where(place == first + step, row, out)
    return out


def slot_ids(dst_row):
    blocks = []
    for d in TABLE:
        if d["kind"] <= 2:
            place = iota((d["rows"], EDGES), 0) + (ATOMS + d["offset"])
            blocks.append(onehot(place == dst_row))
    corners = [d for d in TABLE if d["kind"] == 3]
    place = iota((8 * len(corners), EDGES), 0)
    inner = place % 8
    base = jnp.zeros_like(place)
    for step, d in enumerate(corners):
        base = jnp.where(place // 8 == step, ATOMS + d["offset"], base)
    blocks.append(onehot((inner < 4) & (base + inner == dst_row)))
    return jnp.concatenate(blocks, axis=0)


def geometry(pos_i, pos_j, in_fill, same):
    diff = pos_j - pos_i
    qx, qy, qz = diff[4:5], diff[5:6], diff[6:7]
    live = pos_j[7:8]
    rsq = qx * qx + qy * qy + qz * qz
    in_use = in_fill * live
    inside = jnp.where(rsq < 1.0, 1.0 - rsq, 0.0)
    env = inside * inside * in_use
    centers = iota((8, EDGES), 0).astype(F32) / 7.0
    offset = rsq - centers
    radial = jnp.exp(-SHARPNESS * offset * offset)

    r3, r15, r5 = math.sqrt(3.0), math.sqrt(15.0), math.sqrt(5.0)
    y1 = rows_to_eight([r3 * qx, r3 * qy, r3 * qz], 0)
    y2 = rows_to_eight(
        [
            r15 * qx * qy,
            r15 * qy * qz,
            r15 * qz * qx,
            0.5 * r15 * (qx * qx - qy * qy),
            0.5 * r5 * (2.0 * qz * qz - qx * qx - qy * qy),
        ],
        0,
    )
    h1, l1 = (part.astype(F32) for part in split(y1, 2))
    h2, l2 = (part.astype(F32) for part in split(y2, 2))
    zero8 = jnp.zeros((8, EDGES), F32)
    left1 = jnp.concatenate([h1, h1, l1, zero8], axis=0).astype(BF16)
    right1 = jnp.concatenate([h1, l1, h1, zero8], axis=0).astype(BF16)
    left2 = jnp.concatenate([h2, h2, l2, zero8], axis=0).astype(BF16)
    right2 = jnp.concatenate([h2, l2, h2, zero8], axis=0).astype(BF16)
    k1 = tn(left1, right1).astype(BF16) * same
    k2 = tn(left2, right2).astype(BF16) * same

    return dict(
        q=(qx, qy, qz),
        in_use=in_use,
        inside=inside,
        env=env,
        offset=offset,
        radial=radial,
        left1=left1,
        left2=left2,
        kernels=(same, k1, k2),
    )


def edge_pass(pre_nodes, geo, same, w):
    env = geo["env"]
    k0, k1, k2 = geo["kernels"]
    pre = pre_nodes + mm(w["rad_t"], geo["radial"].astype(BF16))
    act, dact = silu_pair(pre)
    latent = (act * env).astype(BF16)
    envw = mm(w["env_t"], latent).astype(BF16)
    scal0 = mm(envw, k0).astype(BF16)
    scal1 = mm(envw, k1).astype(BF16)
    scal2 = mm(envw, k2).astype(BF16)
    joined = jnp.concatenate([latent, scal0, scal1, scal2], axis=0)
    upd = mm(w["lat_t"], joined)
    upd_act, upd_d = silu_pair(upd)
    updated = (latent.astype(F32) + upd_act).astype(BF16)
    hid = mm(w["hid_t"], updated)
    hid_act, hid_d = silu_pair(hid)
    ro = w["ro"]
    denv = jnp.sum(hid_act * ro, axis=0, keepdims=True)
    dhid = (hid_d * ro * env).astype(BF16)
    dupdated = mm(w["hid"], dhid).astype(BF16).astype(F32)
    dupd = (dupdated * upd_d).astype(BF16)
    djoined = mm(w["lat"], dupd).astype(BF16)
    ds0 = djoined[CH : 2 * CH]
    ds1 = djoined[2 * CH : 3 * CH]
    ds2 = djoined[3 * CH :]
    denvw = (mm(ds0, k0) + mm(ds1, k1) + mm(ds2, k2)).astype(BF16)
    dlatent = dupdated + djoined[:CH].astype(F32) + mm(w["env"], denvw)
    dpre = (dlatent * env * dact).astype(BF16)
    return dpre, (dlatent, act, denv, envw, ds1, ds2)


def edge_coords(dpre, kept, geo, same, w):
    dlatent, act, denv, envw, ds1, ds2 = kept
    r3, r15, r5 = math.sqrt(3.0), math.sqrt(15.0), math.sqrt(5.0)
    qx, qy, qz = geo["q"]
    denv = denv + jnp.sum(dlatent * act, axis=0, keepdims=True)
    envw_t = envw.T
    t1 = mm(jnp.concatenate([ds1.T, envw_t], axis=1), jnp.concatenate([envw, ds1], axis=0)).astype(BF16) * same
    t2 = mm(jnp.concatenate([ds2.T, envw_t], axis=1), jnp.concatenate([envw, ds2], axis=0)).astype(BF16) * same
    dy1 = mm(geo["left1"], t1)
    dy1 = dy1[0:8] + dy1[16:24]
    dy2 = mm(geo["left2"], t2)
    dy2 = dy2[0:8] + dy2[16:24]

    drad = mm(w["rad"], dpre)
    drsq = jnp.sum(drad * geo["radial"] * geo["offset"], axis=0, keepdims=True) * (-2.0 * SHARPNESS)
    drsq = drsq - 2.0 * denv * geo["in_use"] * geo["inside"]
    a0, a1, a2, a3, a4 = (dy2[step : step + 1] for step in range(5))
    two = 2.0 * drsq
    gx = two * qx + r3 * dy1[0:1] + r15 * (a0 * qy + a2 * qz + a3 * qx) - r5 * a4 * qx
    gy = two * qy + r3 * dy1[1:2] + r15 * (a0 * qx + a1 * qz - a3 * qy) - r5 * a4 * qy
    gz = two * qz + r3 * dy1[2:3] + r15 * (a1 * qy + a2 * qx) + 2.0 * r5 * a4 * qz
    return rows_to_eight([gx, gy, gz], 4)


def unpack_lines(ref):
    first = [d for d in TABLE if d["kind"] == 3][0]["slot"]
    corners = ref[first:, :]
    corners = jnp.where(iota(corners.shape, 0) % 8 < 4, corners, 0.0)
    return jnp.concatenate([ref[0:first, :], corners], axis=0).astype(BF16)


def unpack_coords(ref):
    tiles = [None] * (SLOTS // 128)
    for d in TABLE:
        tile = d["slot"] // 128
        piece = ref[d["tile"] : d["tile"] + 4, :]
        tiles[tile] = piece if tiles[tile] is None else tiles[tile] + piece
    coords = jnp.concatenate(tiles, axis=1)
    return jnp.concatenate([jnp.zeros_like(coords), coords], axis=0)


def kernel(
    prefix_hbm,
    fill_hbm,
    feat_hbm,
    pos_hbm,
    send_hbm,
    src_hbm,
    dst_hbm,
    wsrc_hbm,
    wdst_hbm,
    wrad_hbm,
    wenv_hbm,
    wlat_hbm,
    whid_hbm,
    wro_hbm,
    in2,
    coords_in2,
    own_hbm,
    pick_hbm,
    prefix,
    fill,
    feat_v,
    pos_v,
    send_v,
    src_v,
    dst_v,
    wsrc_v,
    wdst_v,
    wrad_v,
    wenv_v,
    wlat_v,
    whid_v,
    wro_v,
    list_v,
    pick_v,
    out1,
    in1,
    coords_out1,
    coords_in1,
    out2,
    coords_out2,
    own_v,
    pick_t_v,
    in_sem,
    sems,
    out_sem,
):
    planes = lax.axis_size("dom") // ROW_Y
    depth = lax.axis_size("gz")
    dom = lax.axis_index("dom")
    cz = lax.axis_index("gz")
    cx, cy = dom // ROW_Y, dom % ROW_Y

    def place(vec, sign):
        x = (cx + sign * vec[0] + planes) % planes
        y = (cy + sign * vec[1] + ROW_Y) % ROW_Y
        z = (cz + sign * vec[2] + depth) % depth
        return (x * ROW_Y + y, z)

    loads = []
    for step, (source, target) in enumerate(
        [
            (send_hbm, send_v),
            (prefix_hbm, prefix),
            (feat_hbm, feat_v),
            (pos_hbm, pos_v),
            (src_hbm, src_v),
            (dst_hbm, dst_v),
            (wsrc_hbm, wsrc_v),
            (wdst_hbm, wdst_v),
            (wrad_hbm, wrad_v),
            (wenv_hbm, wenv_v),
            (wlat_hbm, wlat_v),
            (whid_hbm, whid_v),
            (wro_hbm, wro_v),
            (fill_hbm, fill),
        ]
    ):
        copy = pltpu.make_async_copy(source, target, in_sem.at[step])
        copy.start()
        loads.append(copy)

    barrier = pltpu.get_barrier_semaphore()
    for d in TABLE:
        pl.semaphore_signal(barrier, inc=1, device_id=place(d["vec"], 1), device_id_type=MESH)

    loads[0].wait()
    listed = jnp.where(iota((ATOMS, 608), 0) == send_v[...], 1.0, 0.0)
    list_v[0:608, :] = listed.T
    list_v[608:640, :] = jnp.zeros((32, ATOMS), F32)
    loads[1].wait()
    loads[2].wait()
    loads[3].wait()
    feat16 = feat_v[...].astype(BF16)
    pos = pos_v[...]
    own8 = rows_to_eight([pos[0:1], pos[1:2], pos[2:3], jnp.ones((1, ATOMS), F32)], 4)
    own_pieces = split_rows(own8, 3)
    lane = iota((8, 128), 1)
    line = iota((8, 128), 0)

    def store_coords(ref, slots, shifted):
        for d in TABLE:
            tile, low = d["slot"] // 128 * 128, d["slot"] % 128
            inside = (lane >= low) & (lane < low + d["rows"])
            coords = slots[:, tile : tile + 128]
            if shifted:
                shift = jnp.zeros((8, 128), F32)
                for step in range(3):
                    if d["vec"][step]:
                        shift = jnp.where(line == 4 + step, float(d["vec"][step]), shift)
                coords = coords - shift
            ref[d["tile"] : d["tile"] + 4, :] = jnp.where(inside, coords, 0.0)[4:8]

    def remote(source, target, start, size, pair, vec, sign):
        rows = pl.ds(start, size)
        return pltpu.make_async_remote_copy(
            src_ref=source.at[rows],
            dst_ref=target.at[rows],
            send_sem=sems.at[pair],
            recv_sem=sems.at[pair + 1],
            device_id=place(vec, sign),
            device_id_type=MESH,
        )

    def send_lines(table, source, target, pair, sign):
        for d in table:
            remote(source, target, d["slot"], d["cap"], pair, d["vec"], sign).start()

    def send_coords(source, target, pair, sign):
        for d in TABLE:
            remote(source, target, d["tile"], 4, pair, d["vec"], sign).start()

    def lines_of(source, target, pair):
        return remote(source, target, 0, FEAT_SENT, pair, TABLE[0]["vec"], 1)

    def coords_of(source, target, pair):
        return remote(source, target, 0, COORDS_SENT, pair, TABLE[0]["vec"], 1)

    for d in TABLE:
        n, rows = d["number"], d["rows"]
        count = prefix[0, n + 1] - prefix[0, n]
        lines = list_v[pl.ds(prefix[0, n], rows), :]
        pick_v[d["slot"] : d["slot"] + rows, :] = jnp.where(iota((rows, ATOMS), 0) < count, lines, 0.0)
    pick = pick_v[...].astype(BF16)
    store_coords(coords_out1, sum_pieces(nt(own_pieces, pick), 3), True)
    pl.semaphore_wait(barrier, len(TABLE))
    send_coords(coords_out1, coords_in1, 0, 1)
    groups = [[d for d in TABLE if d["kind"] == 1], [d for d in TABLE if d["kind"] > 1]]
    spans = [(table[0]["slot"], table[-1]["slot"] + table[-1]["rows"]) for table in groups]
    for table, (first, last) in zip(groups, spans):
        out1[first:last, :] = mm(pick[first:last], feat16)
        send_lines(table, out1, in1, 2, 1)

    for copy in loads[4:]:
        copy.wait()
    src_row, dst_row = src_v[...], dst_v[...]
    centre = onehot(iota((ATOMS, EDGES), 0) == src_row)
    near = onehot(iota((ATOMS, EDGES), 0) == dst_row)
    ghost = slot_ids(dst_row)
    same = (tn(centre, centre) * (1.0 / NEIGHBOURS)).astype(BF16)
    in_fill = jnp.where(iota((1, EDGES), 1) < fill[...], 1.0, 0.0)
    eye = iota((CH, CH), 0) == iota((CH, CH), 1)
    w = dict(
        dst_t=wdst_v[...].T,
        rad_t=wrad_v[...].T,
        env_t=wenv_v[...].T,
        lat_t=wlat_v[...].T,
        hid_t=whid_v[...].T,
        rad=wrad_v[...],
        env=wenv_v[...],
        lat=wlat_v[...],
        hid=whid_v[...],
        ro=jnp.sum(jnp.where(eye, wro_v[...], 0.0), axis=1, keepdims=True),
    )
    feat_t = feat16.T
    own_lhs = jnp.concatenate([feat_t, own_pieces], axis=0)
    at_i = mm(own_lhs, centre)
    at_j = mm(own_lhs, near)
    pre_own = mm(wsrc_v[...].T, at_i[:CH].astype(BF16)) + mm(w["dst_t"], at_j[:CH].astype(BF16))
    pos_i = sum_pieces(at_i[CH:], 3)
    pos_j_own = sum_pieces(at_j[CH:], 3)
    pick_t_v[...] = pick.T
    pick_out = pltpu.make_async_copy(pick_t_v, pick_hbm, out_sem.at[0])
    pick_out.start()

    coords_of(coords_out1, coords_in1, 0).wait_recv()
    pos_g = mm(split_rows(unpack_coords(coords_in1), 3), ghost)
    geo = geometry(pos_i, pos_j_own + sum_pieces(pos_g, 3), in_fill, same)

    lines_of(out1, in1, 2).wait_recv()
    far = nt(w["dst_t"], unpack_lines(in1)).astype(BF16)
    dpre, kept = edge_pass(pre_own + mm(far, ghost), geo, same, w)

    for table, (first, last) in zip(groups, spans):
        out2[first:last, :] = nt(ghost[first:last], dpre)
        send_lines(table, out2, in2, 4, -1)
    dq_pieces = split_rows(edge_coords(dpre, kept, geo, same, w), 2)
    store_coords(coords_out2, sum_pieces(nt(dq_pieces, ghost), 2), False)
    send_coords(coords_out2, coords_in2, 6, -1)

    own = nt(jnp.concatenate([centre, near], axis=0), dpre).astype(BF16)
    own_v[0:ATOMS, :] = nt(own[:ATOMS], wsrc_v[...]) + nt(own[ATOMS:], wdst_v[...])
    own_v[ATOMS:, :] = sum_pieces(nt(dq_pieces, near - centre), 2)
    own_out = pltpu.make_async_copy(own_v, own_hbm, out_sem.at[1])
    own_out.start()

    pick_out.wait()
    own_out.wait()
    coords_of(coords_out1, coords_in1, 0).wait_send()
    lines_of(out1, in1, 2).wait_send()
    lines_of(out2, in2, 4).wait()
    coords_of(coords_out2, coords_in2, 6).wait()


def finish(back_ref, coords_ref, own_ref, pick_ref, wdst_ref, force_ref, grad_ref):
    pick_t = pick_ref[...]
    returned = mm(pick_t, unpack_lines(back_ref)).astype(BF16)
    grad_ref[...] = own_ref[0:ATOMS, :] + nt(returned, wdst_ref[...])
    total8 = own_ref[ATOMS:, :] + sum_pieces(nt(split_rows(unpack_coords(coords_ref), 2), pick_t), 2)
    force_ref[...] = -total8[4:7]


def body(
    features,
    positions,
    send_ids,
    ghost_prefix,
    edge_fill,
    edge_src,
    edge_dst,
    weight_src,
    weight_dst,
    weight_radial,
    weight_env,
    weight_latent,
    weight_hidden,
    weight_readout,
):
    arrays = [
        features,
        positions,
        send_ids,
        edge_src,
        edge_dst,
        weight_src,
        weight_dst,
        weight_radial,
        weight_env,
        weight_latent,
        weight_hidden,
        weight_readout.reshape(1, CH),
    ]
    hbm = pl.BlockSpec(memory_space=pltpu.HBM)
    vmem = pl.BlockSpec(memory_space=pltpu.VMEM)
    back, coords, own, pick_t = pl.pallas_call(
        kernel,
        out_shape=(
            jax.ShapeDtypeStruct((SLOTS, CH), F32),
            jax.ShapeDtypeStruct((COORDS, CH), F32),
            jax.ShapeDtypeStruct((ATOMS + 8, CH), F32),
            jax.ShapeDtypeStruct((ATOMS, SLOTS), BF16),
        ),
        in_specs=[hbm] * (2 + len(arrays)),
        out_specs=(hbm, hbm, hbm, hbm),
        scratch_shapes=[pltpu.SMEM(ghost_prefix.shape, jnp.int32), pltpu.VMEM((1, 1), jnp.int32)]
        + [pltpu.VMEM(a.shape, a.dtype) for a in arrays]
        + [
            pltpu.VMEM((SLOTS, ATOMS), F32),
            pltpu.VMEM((SLOTS, ATOMS), F32),
            pltpu.VMEM((SLOTS, CH), F32),
            pltpu.VMEM((SLOTS, CH), F32),
            pltpu.VMEM((COORDS, CH), F32),
            pltpu.VMEM((COORDS, CH), F32),
            pltpu.VMEM((SLOTS, CH), F32),
            pltpu.VMEM((COORDS, CH), F32),
            pltpu.VMEM((ATOMS + 8, CH), F32),
            pltpu.VMEM((ATOMS, SLOTS), BF16),
            pltpu.SemaphoreType.DMA((2 + len(arrays),)),
            pltpu.SemaphoreType.DMA((8,)),
            pltpu.SemaphoreType.DMA((2,)),
        ],
        compiler_params=pltpu.CompilerParams(collective_id=0, has_side_effects=True, vmem_limit_bytes=VMEM),
        name="allegro",
    )(ghost_prefix, edge_fill.reshape(1, 1), *arrays)
    return pl.pallas_call(
        finish,
        out_shape=(
            jax.ShapeDtypeStruct((3, ATOMS), F32),
            jax.ShapeDtypeStruct((ATOMS, CH), F32),
        ),
        in_specs=[vmem] * 5,
        out_specs=(vmem, vmem),
        compiler_params=pltpu.CompilerParams(vmem_limit_bytes=VMEM),
        name="finish",
    )(back, coords, own, pick_t, weight_dst)


def solution(mesh):
    return jax.shard_map(
        body,
        mesh=mesh,
        in_specs=(
            P(("dom", "gz"), None),
            P(None, ("dom", "gz")),
            P(("dom", "gz"), None),
            P(("dom", "gz"), None),
            P(("dom", "gz")),
            P(("dom", "gz"), None),
            P(("dom", "gz"), None),
            P(),
            P(),
            P(),
            P(),
            P(),
            P(),
            P(),
        ),
        out_specs=(P(None, ("dom", "gz")), P(("dom", "gz"), None)),
        check_vma=False,
    )
```

```python
import math

import jax
import jax.numpy as jnp
import numpy as np
from jax import lax
from jax.experimental import pallas as pl
from jax.experimental.pallas import tpu as pltpu
from jax.sharding import PartitionSpec as P

NEIGHBOURS = 4
CAPS = (0, 64, 16, 4)
ROW_Y = 8

ATOMS = 128
EDGES = 512
CH = 128
SLOTS = 640
SHARPNESS = 8.0
VMEM = 56 * 1024 * 1024

BF16 = jnp.bfloat16
F32 = jnp.float32
MESH = pl.DeviceIdType.MESH


def directions():
    table = []
    offset = 0
    number = 0
    for a in (-1, 0, 1):
        for b in (-1, 0, 1):
            for c in (-1, 0, 1):
                kind = abs(a) + abs(b) + abs(c)
                if kind == 0:
                    continue
                cap = CAPS[kind]
                table.append(dict(vec=(a, b, c), kind=kind, cap=cap, number=number, offset=offset))
                offset += cap
                number += 1
    table.sort(key=lambda d: (d["kind"], d["number"]))
    slot = 0
    for step, d in enumerate(table):
        d["rows"] = {1: 64, 2: 16, 3: 8}[d["kind"]]
        d["slot"] = slot
        d["tile"] = 8 * step
        slot += d["rows"]
    assert slot == SLOTS
    return table


TABLE = directions()
FEAT_SENT = sum(d["cap"] for d in TABLE)
COORDS = 8 * len(TABLE)
COORDS_SENT = 4 * len(TABLE)


def mm(a, b):
    return lax.dot_general(a, b, (((1,), (0,)), ((), ())), preferred_element_type=F32)


def nt(a, b):
    return lax.dot_general(a, b, (((1,), (1,)), ((), ())), preferred_element_type=F32)


def tn(a, b):
    return lax.dot_general(a, b, (((0,), (0,)), ((), ())), preferred_element_type=F32)


def iota(shape, dim):
    return lax.broadcasted_iota(jnp.int32, shape, dim)


def onehot(cond):
    return jnp.where(cond, 1.0, 0.0).astype(BF16)


def split(x, pieces):
    out = []
    for step in range(pieces):
        part = x.astype(BF16)
        out.append(part)
        if step + 1 < pieces:
            x = x - part.astype(F32)
    return out


def split_rows(x, pieces):
    parts = []
    for step in range(pieces):
        part = x.astype(BF16).astype(F32)
        parts.append(part)
        x = x - part
    if pieces % 2:
        parts.append(jnp.zeros_like(x))
    return jnp.concatenate(parts, axis=0).astype(BF16)


def sum_pieces(x, pieces):
    total = x[0:8]
    for step in range(1, pieces):
        total = total + x[8 * step : 8 * step + 8]
    return total


def sigmoid(v):
    return 0.5 * jnp.tanh(0.5 * v) + 0.5


def silu_pair(v):
    sig = sigmoid(v)
    value = v * sig
    return value, sig + value * (1.0 - sig)


def rows_to_eight(rows, first):
    place = iota((8, rows[0].shape[1]), 0)
    out = jnp.zeros((8, rows[0].shape[1]), F32)
    for step, row in enumerate(rows):
        out = jnp.where(place == first + step, row, out)
    return out


def slot_ids(dst_row):
    blocks = []
    for d in TABLE:
        if d["kind"] <= 2:
            place = iota((d["rows"], EDGES), 0) + (ATOMS + d["offset"])
            blocks.append(onehot(place == dst_row))
    corners = [d for d in TABLE if d["kind"] == 3]
    place = iota((8 * len(corners), EDGES), 0)
    inner = place % 8
    base = jnp.zeros_like(place)
    for step, d in enumerate(corners):
        base = jnp.where(place // 8 == step, ATOMS + d["offset"], base)
    blocks.append(onehot((inner < 4) & (base + inner == dst_row)))
    return jnp.concatenate(blocks, axis=0)


def geometry(pos_i, pos_j, in_fill, same):
    diff = pos_j - pos_i
    qx, qy, qz = diff[4:5], diff[5:6], diff[6:7]
    live = pos_j[7:8]
    rsq = qx * qx + qy * qy + qz * qz
    in_use = in_fill * live
    inside = jnp.where(rsq < 1.0, 1.0 - rsq, 0.0)
    env = inside * inside * in_use
    centers = iota((8, EDGES), 0).astype(F32) / 7.0
    offset = rsq - centers
    radial = jnp.exp(-SHARPNESS * offset * offset)

    r3, r15, r5 = math.sqrt(3.0), math.sqrt(15.0), math.sqrt(5.0)
    y1 = rows_to_eight([r3 * qx, r3 * qy, r3 * qz], 0)
    y2 = rows_to_eight(
        [
            r15 * qx * qy,
            r15 * qy * qz,
            r15 * qz * qx,
            0.5 * r15 * (qx * qx - qy * qy),
            0.5 * r5 * (2.0 * qz * qz - qx * qx - qy * qy),
        ],
        0,
    )
    h1, l1 = (part.astype(F32) for part in split(y1, 2))
    h2, l2 = (part.astype(F32) for part in split(y2, 2))
    zero8 = jnp.zeros((8, EDGES), F32)
    left1 = jnp.concatenate([h1, h1, l1, zero8], axis=0).astype(BF16)
    right1 = jnp.concatenate([h1, l1, h1, zero8], axis=0).astype(BF16)
    left2 = jnp.concatenate([h2, h2, l2, zero8], axis=0).astype(BF16)
    right2 = jnp.concatenate([h2, l2, h2, zero8], axis=0).astype(BF16)
    k1 = tn(left1, right1).astype(BF16) * same
    k2 = tn(left2, right2).astype(BF16) * same

    return dict(
        q=(qx, qy, qz),
        in_use=in_use,
        inside=inside,
        env=env,
        offset=offset,
        radial=radial,
        left1=left1,
        left2=left2,
        kernels=(same, k1, k2),
    )


def edge_pass(pre_nodes, geo, same, w):
    env = geo["env"]
    k0, k1, k2 = geo["kernels"]
    pre = pre_nodes + mm(w["rad_t"], geo["radial"].astype(BF16))
    act, dact = silu_pair(pre)
    latent = (act * env).astype(BF16)
    envw = mm(w["env_t"], latent).astype(BF16)
    scal0 = mm(envw, k0).astype(BF16)
    scal1 = mm(envw, k1).astype(BF16)
    scal2 = mm(envw, k2).astype(BF16)
    joined = jnp.concatenate([latent, scal0, scal1, scal2], axis=0)
    upd = mm(w["lat_t"], joined)
    upd_act, upd_d = silu_pair(upd)
    updated = (latent.astype(F32) + upd_act).astype(BF16)
    hid = mm(w["hid_t"], updated)
    hid_act, hid_d = silu_pair(hid)
    ro = w["ro"]
    denv = jnp.sum(hid_act * ro, axis=0, keepdims=True)
    dhid = (hid_d * ro * env).astype(BF16)
    dupdated = mm(w["hid"], dhid).astype(BF16).astype(F32)
    dupd = (dupdated * upd_d).astype(BF16)
    djoined = mm(w["lat"], dupd).astype(BF16)
    ds0 = djoined[CH : 2 * CH]
    ds1 = djoined[2 * CH : 3 * CH]
    ds2 = djoined[3 * CH :]
    denvw = (mm(ds0, k0) + mm(ds1, k1) + mm(ds2, k2)).astype(BF16)
    dlatent = dupdated + djoined[:CH].astype(F32) + mm(w["env"], denvw)
    dpre = (dlatent * env * dact).astype(BF16)
    return dpre, (dlatent, act, denv, envw, ds1, ds2)


def edge_coords(dpre, kept, geo, same, w):
    dlatent, act, denv, envw, ds1, ds2 = kept
    r3, r15, r5 = math.sqrt(3.0), math.sqrt(15.0), math.sqrt(5.0)
    qx, qy, qz = geo["q"]
    denv = denv + jnp.sum(dlatent * act, axis=0, keepdims=True)
    envw_t = envw.T
    t1 = mm(jnp.concatenate([ds1.T, envw_t], axis=1), jnp.concatenate([envw, ds1], axis=0)).astype(BF16) * same
    t2 = mm(jnp.concatenate([ds2.T, envw_t], axis=1), jnp.concatenate([envw, ds2], axis=0)).astype(BF16) * same
    dy1 = mm(geo["left1"], t1)
    dy1 = dy1[0:8] + dy1[16:24]
    dy2 = mm(geo["left2"], t2)
    dy2 = dy2[0:8] + dy2[16:24]

    drad = mm(w["rad"], dpre)
    drsq = jnp.sum(drad * geo["radial"] * geo["offset"], axis=0, keepdims=True) * (-2.0 * SHARPNESS)
    drsq = drsq - 2.0 * denv * geo["in_use"] * geo["inside"]
    a0, a1, a2, a3, a4 = (dy2[step : step + 1] for step in range(5))
    two = 2.0 * drsq
    gx = two * qx + r3 * dy1[0:1] + r15 * (a0 * qy + a2 * qz + a3 * qx) - r5 * a4 * qx
    gy = two * qy + r3 * dy1[1:2] + r15 * (a0 * qx + a1 * qz - a3 * qy) - r5 * a4 * qy
    gz = two * qz + r3 * dy1[2:3] + r15 * (a1 * qy + a2 * qx) + 2.0 * r5 * a4 * qz
    return rows_to_eight([gx, gy, gz], 4)


def unpack_lines(ref):
    first = [d for d in TABLE if d["kind"] == 3][0]["slot"]
    corners = ref[first:, :]
    corners = jnp.where(iota(corners.shape, 0) % 8 < 4, corners, 0.0)
    return jnp.concatenate([ref[0:first, :], corners], axis=0).astype(BF16)


def unpack_coords(ref):
    tiles = [None] * (SLOTS // 128)
    for d in TABLE:
        tile = d["slot"] // 128
        piece = ref[d["tile"] : d["tile"] + 4, :]
        tiles[tile] = piece if tiles[tile] is None else tiles[tile] + piece
    coords = jnp.concatenate(tiles, axis=1)
    return jnp.concatenate([jnp.zeros_like(coords), coords], axis=0)


def kernel(
    prefix_hbm,
    fill_hbm,
    feat_hbm,
    pos_hbm,
    send_hbm,
    src_hbm,
    dst_hbm,
    wsrc_hbm,
    wdst_hbm,
    wrad_hbm,
    wenv_hbm,
    wlat_hbm,
    whid_hbm,
    wro_hbm,
    in2,
    coords_in2,
    own_hbm,
    pick_hbm,
    prefix,
    fill,
    feat_v,
    pos_v,
    send_v,
    src_v,
    dst_v,
    wsrc_v,
    wdst_v,
    wrad_v,
    wenv_v,
    wlat_v,
    whid_v,
    wro_v,
    list_v,
    pick_v,
    out1,
    in1,
    coords_out1,
    coords_in1,
    out2,
    coords_out2,
    own_v,
    pick_t_v,
    in_sem,
    sems,
    out_sem,
):
    planes = lax.axis_size("dom") // ROW_Y
    depth = lax.axis_size("gz")
    dom = lax.axis_index("dom")
    cz = lax.axis_index("gz")
    cx, cy = lax.div(dom, ROW_Y), lax.rem(dom, ROW_Y)
    along_x = {step: lax.rem(cx + (step + planes), planes) * ROW_Y for step in (-1, 0, 1)}
    along_y = {step: lax.rem(cy + (step + ROW_Y), ROW_Y) for step in (-1, 0, 1)}
    along_z = {step: lax.rem(cz + (step + depth), depth) for step in (-1, 0, 1)}

    def place(vec, sign):
        return (along_x[sign * vec[0]] + along_y[sign * vec[1]], along_z[sign * vec[2]])

    loads = []
    for step, (source, target) in enumerate(
        [
            (send_hbm, send_v),
            (prefix_hbm, prefix),
            (feat_hbm, feat_v),
            (pos_hbm, pos_v),
            (src_hbm, src_v),
            (dst_hbm, dst_v),
            (wsrc_hbm, wsrc_v),
            (wdst_hbm, wdst_v),
            (wrad_hbm, wrad_v),
            (wenv_hbm, wenv_v),
            (wlat_hbm, wlat_v),
            (whid_hbm, whid_v),
            (wro_hbm, wro_v),
            (fill_hbm, fill),
        ]
    ):
        copy = pltpu.make_async_copy(source, target, in_sem.at[step])
        copy.start()
        loads.append(copy)

    barrier = pltpu.get_barrier_semaphore()
    for d in TABLE:
        pl.semaphore_signal(barrier, inc=1, device_id=place(d["vec"], 1), device_id_type=MESH)

    loads[0].wait()
    listed = jnp.where(iota((ATOMS, 608), 0) == send_v[...], 1.0, 0.0)
    list_v[0:608, :] = listed.T
    list_v[608:640, :] = jnp.zeros((32, ATOMS), F32)
    loads[1].wait()
    loads[2].wait()
    loads[3].wait()
    feat16 = feat_v[...].astype(BF16)
    pos = pos_v[...]
    own8 = rows_to_eight([pos[0:1], pos[1:2], pos[2:3], jnp.ones((1, ATOMS), F32)], 4)
    own_pieces = split_rows(own8, 3)
    lane = iota((8, 128), 1)
    line = iota((8, 128), 0)

    def store_coords(ref, slots, shifted):
        for d in TABLE:
            tile, low = d["slot"] // 128 * 128, d["slot"] % 128
            inside = (lane >= low) & (lane < low + d["rows"])
            coords = slots[:, tile : tile + 128]
            if shifted:
                shift = jnp.zeros((8, 128), F32)
                for step in range(3):
                    if d["vec"][step]:
                        shift = jnp.where(line == 4 + step, float(d["vec"][step]), shift)
                coords = coords - shift
            ref[d["tile"] : d["tile"] + 4, :] = jnp.where(inside, coords, 0.0)[4:8]

    def remote(source, target, start, size, pair, vec, sign):
        rows = pl.ds(start, size)
        return pltpu.make_async_remote_copy(
            src_ref=source.at[rows],
            dst_ref=target.at[rows],
            send_sem=sems.at[pair],
            recv_sem=sems.at[pair + 1],
            device_id=place(vec, sign),
            device_id_type=MESH,
        )

    def send_lines(table, source, target, pair, sign):
        for d in table:
            remote(source, target, d["slot"], d["cap"], pair, d["vec"], sign).start()

    def send_coords(source, target, pair, sign):
        for d in TABLE[::-1]:
            remote(source, target, d["tile"], 4, pair, d["vec"], sign).start()

    def lines_of(source, target, pair):
        return remote(source, target, 0, FEAT_SENT, pair, TABLE[0]["vec"], 1)

    def coords_of(source, target, pair):
        return remote(source, target, 0, COORDS_SENT, pair, TABLE[0]["vec"], 1)

    for d in TABLE:
        n, rows = d["number"], d["rows"]
        count = prefix[0, n + 1] - prefix[0, n]
        lines = list_v[pl.ds(prefix[0, n], rows), :]
        pick_v[d["slot"] : d["slot"] + rows, :] = jnp.where(iota((rows, ATOMS), 0) < count, lines, 0.0)
    pick = pick_v[...].astype(BF16)
    store_coords(coords_out1, sum_pieces(nt(own_pieces, pick), 3), True)
    out1[...] = mm(pick, feat16)
    groups = [[d for d in TABLE[::-1] if d["kind"] > 1], [d for d in TABLE if d["kind"] == 1]]
    split_at = groups[1][-1]["slot"] + groups[1][-1]["rows"]
    spans = [(split_at, SLOTS), (0, split_at)]
    pl.semaphore_wait(barrier, len(TABLE))
    send_coords(coords_out1, coords_in1, 0, 1)
    for table in groups:
        send_lines(table, out1, in1, 2, 1)

    for copy in loads[4:]:
        copy.wait()
    src_row, dst_row = src_v[...], dst_v[...]
    centre = onehot(iota((ATOMS, EDGES), 0) == src_row)
    near = onehot(iota((ATOMS, EDGES), 0) == dst_row)
    ghost = slot_ids(dst_row)
    same = (tn(centre, centre) * (1.0 / NEIGHBOURS)).astype(BF16)
    in_fill = jnp.where(iota((1, EDGES), 1) < fill[...], 1.0, 0.0)
    eye = iota((CH, CH), 0) == iota((CH, CH), 1)
    w = dict(
        dst_t=wdst_v[...].T,
        rad_t=wrad_v[...].T,
        env_t=wenv_v[...].T,
        lat_t=wlat_v[...].T,
        hid_t=whid_v[...].T,
        rad=wrad_v[...],
        env=wenv_v[...],
        lat=wlat_v[...],
        hid=whid_v[...],
        ro=jnp.sum(jnp.where(eye, wro_v[...], 0.0), axis=1, keepdims=True),
    )
    feat_t = feat16.T
    own_lhs = jnp.concatenate([feat_t, own_pieces], axis=0)
    at_i = mm(own_lhs, centre)
    at_j = mm(own_lhs, near)
    pre_own = mm(wsrc_v[...].T, at_i[:CH].astype(BF16)) + mm(w["dst_t"], at_j[:CH].astype(BF16))
    pos_i = sum_pieces(at_i[CH:], 3)
    pos_j_own = sum_pieces(at_j[CH:], 3)
    pick_t_v[...] = pick.T
    pick_out = pltpu.make_async_copy(pick_t_v, pick_hbm, out_sem.at[0])
    pick_out.start()

    coords_of(coords_out1, coords_in1, 0).wait_recv()
    pos_g = mm(split_rows(unpack_coords(coords_in1), 3), ghost)
    geo = geometry(pos_i, pos_j_own + sum_pieces(pos_g, 3), in_fill, same)

    lines_of(out1, in1, 2).wait_recv()
    far = nt(w["dst_t"], unpack_lines(in1)).astype(BF16)
    dpre, kept = edge_pass(pre_own + mm(far, ghost), geo, same, w)

    for table, (first, last) in zip(groups, spans):
        out2[first:last, :] = nt(ghost[first:last], dpre)
        send_lines(table, out2, in2, 4, -1)
    dq_pieces = split_rows(edge_coords(dpre, kept, geo, same, w), 2)
    store_coords(coords_out2, sum_pieces(nt(dq_pieces, ghost), 2), False)
    send_coords(coords_out2, coords_in2, 6, -1)

    own = nt(jnp.concatenate([centre, near], axis=0), dpre).astype(BF16)
    own_v[0:ATOMS, :] = nt(own[:ATOMS], wsrc_v[...]) + nt(own[ATOMS:], wdst_v[...])
    own_v[ATOMS:, :] = sum_pieces(nt(dq_pieces, near - centre), 2)
    own_out = pltpu.make_async_copy(own_v, own_hbm, out_sem.at[1])
    own_out.start()

    pick_out.wait()
    own_out.wait()
    coords_of(coords_out1, coords_in1, 0).wait_send()
    lines_of(out1, in1, 2).wait_send()
    lines_of(out2, in2, 4).wait()
    coords_of(coords_out2, coords_in2, 6).wait()


def finish(back_ref, coords_ref, own_ref, pick_ref, wdst_ref, force_ref, grad_ref):
    pick_t = pick_ref[...]
    returned = mm(pick_t, unpack_lines(back_ref)).astype(BF16)
    grad_ref[...] = own_ref[0:ATOMS, :] + nt(returned, wdst_ref[...])
    total8 = own_ref[ATOMS:, :] + sum_pieces(nt(split_rows(unpack_coords(coords_ref), 2), pick_t), 2)
    force_ref[...] = -total8[4:7]


def body(
    features,
    positions,
    send_ids,
    ghost_prefix,
    edge_fill,
    edge_src,
    edge_dst,
    weight_src,
    weight_dst,
    weight_radial,
    weight_env,
    weight_latent,
    weight_hidden,
    weight_readout,
):
    arrays = [
        features,
        positions,
        send_ids,
        edge_src,
        edge_dst,
        weight_src,
        weight_dst,
        weight_radial,
        weight_env,
        weight_latent,
        weight_hidden,
        weight_readout.reshape(1, CH),
    ]
    hbm = pl.BlockSpec(memory_space=pltpu.HBM)
    vmem = pl.BlockSpec(memory_space=pltpu.VMEM)
    back, coords, own, pick_t = pl.pallas_call(
        kernel,
        out_shape=(
            jax.ShapeDtypeStruct((SLOTS, CH), F32),
            jax.ShapeDtypeStruct((COORDS, CH), F32),
            jax.ShapeDtypeStruct((ATOMS + 8, CH), F32),
            jax.ShapeDtypeStruct((ATOMS, SLOTS), BF16),
        ),
        in_specs=[hbm] * (2 + len(arrays)),
        out_specs=(hbm, hbm, hbm, hbm),
        scratch_shapes=[pltpu.SMEM(ghost_prefix.shape, jnp.int32), pltpu.VMEM((1, 1), jnp.int32)]
        + [pltpu.VMEM(a.shape, a.dtype) for a in arrays]
        + [
            pltpu.VMEM((SLOTS, ATOMS), F32),
            pltpu.VMEM((SLOTS, ATOMS), F32),
            pltpu.VMEM((SLOTS, CH), F32),
            pltpu.VMEM((SLOTS, CH), F32),
            pltpu.VMEM((COORDS, CH), F32),
            pltpu.VMEM((COORDS, CH), F32),
            pltpu.VMEM((SLOTS, CH), F32),
            pltpu.VMEM((COORDS, CH), F32),
            pltpu.VMEM((ATOMS + 8, CH), F32),
            pltpu.VMEM((ATOMS, SLOTS), BF16),
            pltpu.SemaphoreType.DMA((2 + len(arrays),)),
            pltpu.SemaphoreType.DMA((8,)),
            pltpu.SemaphoreType.DMA((2,)),
        ],
        compiler_params=pltpu.CompilerParams(collective_id=0, has_side_effects=True, vmem_limit_bytes=VMEM),
        name="allegro",
    )(ghost_prefix, edge_fill.reshape(1, 1), *arrays)
    return pl.pallas_call(
        finish,
        out_shape=(
            jax.ShapeDtypeStruct((3, ATOMS), F32),
            jax.ShapeDtypeStruct((ATOMS, CH), F32),
        ),
        in_specs=[vmem] * 5,
        out_specs=(vmem, vmem),
        compiler_params=pltpu.CompilerParams(vmem_limit_bytes=VMEM),
        name="finish",
    )(back, coords, own, pick_t, weight_dst)


def solution(mesh):
    return jax.shard_map(
        body,
        mesh=mesh,
        in_specs=(
            P(("dom", "gz"), None),
            P(None, ("dom", "gz")),
            P(("dom", "gz"), None),
            P(("dom", "gz"), None),
            P(("dom", "gz")),
            P(("dom", "gz"), None),
            P(("dom", "gz"), None),
            P(),
            P(),
            P(),
            P(),
            P(),
            P(),
            P(),
        ),
        out_specs=(P(None, ("dom", "gz")), P(("dom", "gz"), None)),
        check_vma=False,
    )
```

```python
import math

import jax
import jax.numpy as jnp
import numpy as np
from jax import lax
from jax.experimental import pallas as pl
from jax.experimental.pallas import tpu as pltpu
from jax.sharding import PartitionSpec as P

NEIGHBOURS = 4
CAPS = (0, 64, 16, 4)
ROW_Y = 8

ATOMS = 128
EDGES = 512
CH = 128
SLOTS = 640
SHARPNESS = 8.0
VMEM = 56 * 1024 * 1024

BF16 = jnp.bfloat16
F32 = jnp.float32
MESH = pl.DeviceIdType.MESH


def directions():
    table = []
    offset = 0
    number = 0
    for a in (-1, 0, 1):
        for b in (-1, 0, 1):
            for c in (-1, 0, 1):
                kind = abs(a) + abs(b) + abs(c)
                if kind == 0:
                    continue
                cap = CAPS[kind]
                table.append(dict(vec=(a, b, c), kind=kind, cap=cap, number=number, offset=offset))
                offset += cap
                number += 1
    table.sort(key=lambda d: (d["kind"], d["number"]))
    slot = 0
    for step, d in enumerate(table):
        d["rows"] = {1: 64, 2: 16, 3: 8}[d["kind"]]
        d["slot"] = slot
        d["tile"] = 8 * step
        slot += d["rows"]
    assert slot == SLOTS
    return table


TABLE = directions()
FEAT_SENT = sum(d["cap"] for d in TABLE)
COORDS = 8 * len(TABLE)
COORDS_SENT = 4 * len(TABLE)


def mm(a, b):
    return lax.dot_general(a, b, (((1,), (0,)), ((), ())), preferred_element_type=F32)


def nt(a, b):
    return lax.dot_general(a, b, (((1,), (1,)), ((), ())), preferred_element_type=F32)


def tn(a, b):
    return lax.dot_general(a, b, (((0,), (0,)), ((), ())), preferred_element_type=F32)


def iota(shape, dim):
    return lax.broadcasted_iota(jnp.int32, shape, dim)


def onehot(cond):
    return jnp.where(cond, 1.0, 0.0).astype(BF16)


def split(x, pieces):
    out = []
    for step in range(pieces):
        part = x.astype(BF16)
        out.append(part)
        if step + 1 < pieces:
            x = x - part.astype(F32)
    return out


def split_rows(x, pieces):
    parts = []
    for step in range(pieces):
        part = x.astype(BF16).astype(F32)
        parts.append(part)
        x = x - part
    if pieces % 2:
        parts.append(jnp.zeros_like(x))
    return jnp.concatenate(parts, axis=0).astype(BF16)


def sum_pieces(x, pieces):
    total = x[0:8]
    for step in range(1, pieces):
        total = total + x[8 * step : 8 * step + 8]
    return total


def sigmoid(v):
    return 0.5 * jnp.tanh(0.5 * v) + 0.5


def silu_pair(v):
    sig = sigmoid(v)
    value = v * sig
    return value, sig + value * (1.0 - sig)


def rows_to_eight(rows, first):
    place = iota((8, rows[0].shape[1]), 0)
    out = jnp.zeros((8, rows[0].shape[1]), F32)
    for step, row in enumerate(rows):
        out = jnp.where(place == first + step, row, out)
    return out


def slot_ids(dst_row):
    blocks = []
    for d in TABLE:
        if d["kind"] <= 2:
            place = iota((d["rows"], EDGES), 0) + (ATOMS + d["offset"])
            blocks.append(onehot(place == dst_row))
    corners = [d for d in TABLE if d["kind"] == 3]
    place = iota((8 * len(corners), EDGES), 0)
    inner = place % 8
    base = jnp.zeros_like(place)
    for step, d in enumerate(corners):
        base = jnp.where(place // 8 == step, ATOMS + d["offset"], base)
    blocks.append(onehot((inner < 4) & (base + inner == dst_row)))
    return jnp.concatenate(blocks, axis=0)


def side_by_side(x):
    rows = x.shape[0] // 3
    return jnp.concatenate([x[rows * step : rows * (step + 1)] for step in range(3)], axis=1)


def mixing(wenv, wlat):
    parts = [wlat[:CH]]
    for step in range(1, 4):
        parts.append(mm(wenv, wlat[CH * step : CH * (step + 1)]).astype(BF16))
    return parts


def geometry(pos_i, pos_j, in_fill, same):
    diff = pos_j - pos_i
    qx, qy, qz = diff[4:5], diff[5:6], diff[6:7]
    live = pos_j[7:8]
    rsq = qx * qx + qy * qy + qz * qz
    in_use = in_fill * live
    inside = jnp.where(rsq < 1.0, 1.0 - rsq, 0.0)
    env = inside * inside * in_use
    centers = iota((8, EDGES), 0).astype(F32) / 7.0
    offset = rsq - centers
    radial = jnp.exp(-SHARPNESS * offset * offset)

    r3, r15, r5 = math.sqrt(3.0), math.sqrt(15.0), math.sqrt(5.0)
    y1 = rows_to_eight([r3 * qx, r3 * qy, r3 * qz], 0)
    y2 = rows_to_eight(
        [
            r15 * qx * qy,
            r15 * qy * qz,
            r15 * qz * qx,
            0.5 * r15 * (qx * qx - qy * qy),
            0.5 * r5 * (2.0 * qz * qz - qx * qx - qy * qy),
        ],
        0,
    )
    h1, l1 = (part.astype(F32) for part in split(y1, 2))
    h2, l2 = (part.astype(F32) for part in split(y2, 2))
    zero8 = jnp.zeros((8, EDGES), F32)
    left1 = jnp.concatenate([h1, h1, l1, zero8], axis=0).astype(BF16)
    right1 = jnp.concatenate([h1, l1, h1, zero8], axis=0).astype(BF16)
    left2 = jnp.concatenate([h2, h2, l2, zero8], axis=0).astype(BF16)
    right2 = jnp.concatenate([h2, l2, h2, zero8], axis=0).astype(BF16)
    k1 = tn(left1, right1).astype(BF16) * same
    k2 = tn(left2, right2).astype(BF16) * same

    return dict(
        q=(qx, qy, qz),
        in_use=in_use,
        inside=inside,
        env=env,
        offset=offset,
        radial=radial,
        left1=left1,
        left2=left2,
        kernels=jnp.concatenate([same, k1, k2], axis=0),
    )


def edge_pass(pre, geo, w):
    env, kernels = geo["env"], geo["kernels"]
    act, dact = silu_pair(pre)
    latent = (act * env).astype(BF16)
    mixed = mm(w["mix_t"], latent)
    near_far = mixed[CH:].astype(BF16)
    upd = mixed[:CH] + mm(side_by_side(near_far), kernels)
    upd_act, upd_d = silu_pair(upd)
    updated = (latent.astype(F32) + upd_act).astype(BF16)
    hid = mm(w["hid_t"], updated)
    hid_act, hid_d = silu_pair(hid)
    ro = w["ro"]
    dhid = (hid_d * ro * env).astype(BF16)
    dupdated = mm(w["hid"], dhid).astype(BF16).astype(F32)
    dupd = (dupdated * upd_d).astype(BF16)
    dmixed = mm(w["mix"], dupd)
    dlatent = dupdated + dmixed[:CH] + mm(side_by_side(dmixed[CH:].astype(BF16)), kernels)
    dpre = (dlatent * env * dact).astype(BF16)
    return dpre, (dlatent, act, hid_act, near_far[CH : 2 * CH], near_far[2 * CH :], dupd)


def edge_coords(dpre, kept, geo, same, w):
    dlatent, act, hid_act, b1, b2, dupd = kept
    r3, r15, r5 = math.sqrt(3.0), math.sqrt(15.0), math.sqrt(5.0)
    qx, qy, qz = geo["q"]
    denv = jnp.sum(hid_act * w["ro"] + dlatent * act, axis=0, keepdims=True)
    dupd_t = dupd.T
    t1 = mm(jnp.concatenate([dupd_t, b1.T], axis=1), jnp.concatenate([b1, dupd], axis=0)).astype(BF16) * same
    t2 = mm(jnp.concatenate([dupd_t, b2.T], axis=1), jnp.concatenate([b2, dupd], axis=0)).astype(BF16) * same
    dy1 = mm(geo["left1"], t1)
    dy1 = dy1[0:8] + dy1[16:24]
    dy2 = mm(geo["left2"], t2)
    dy2 = dy2[0:8] + dy2[16:24]

    drad = mm(w["rad"], dpre)
    drsq = jnp.sum(drad * geo["radial"] * geo["offset"], axis=0, keepdims=True) * (-2.0 * SHARPNESS)
    drsq = drsq - 2.0 * denv * geo["in_use"] * geo["inside"]
    a0, a1, a2, a3, a4 = (dy2[step : step + 1] for step in range(5))
    two = 2.0 * drsq
    gx = two * qx + r3 * dy1[0:1] + r15 * (a0 * qy + a2 * qz + a3 * qx) - r5 * a4 * qx
    gy = two * qy + r3 * dy1[1:2] + r15 * (a0 * qx + a1 * qz - a3 * qy) - r5 * a4 * qy
    gz = two * qz + r3 * dy1[2:3] + r15 * (a1 * qy + a2 * qx) + 2.0 * r5 * a4 * qz
    return rows_to_eight([gx, gy, gz], 4)


def unpack_lines(ref):
    first = [d for d in TABLE if d["kind"] == 3][0]["slot"]
    corners = ref[first:, :]
    corners = jnp.where(iota(corners.shape, 0) % 8 < 4, corners, 0.0)
    return jnp.concatenate([ref[0:first, :], corners], axis=0).astype(BF16)


def unpack_coords(ref):
    tiles = [None] * (SLOTS // 128)
    for d in TABLE:
        tile = d["slot"] // 128
        piece = ref[d["tile"] : d["tile"] + 4, :]
        tiles[tile] = piece if tiles[tile] is None else tiles[tile] + piece
    coords = jnp.concatenate(tiles, axis=1)
    return jnp.concatenate([jnp.zeros_like(coords), coords], axis=0)


def kernel(
    prefix_hbm,
    fill_hbm,
    feat_hbm,
    pos_hbm,
    send_hbm,
    src_hbm,
    dst_hbm,
    wsrc_hbm,
    wdst_hbm,
    wrad_hbm,
    wenv_hbm,
    wlat_hbm,
    whid_hbm,
    wro_hbm,
    in2,
    coords_in2,
    own_hbm,
    pick_hbm,
    prefix,
    fill,
    feat_v,
    pos_v,
    send_v,
    src_v,
    dst_v,
    wsrc_v,
    wdst_v,
    wrad_v,
    wenv_v,
    wlat_v,
    whid_v,
    wro_v,
    list_v,
    pick_v,
    out1,
    in1,
    coords_out1,
    coords_in1,
    out2,
    coords_out2,
    own_v,
    pick_t_v,
    in_sem,
    sems,
    out_sem,
):
    planes = lax.axis_size("dom") // ROW_Y
    depth = lax.axis_size("gz")
    dom = lax.axis_index("dom")
    cz = lax.axis_index("gz")
    cx, cy = lax.div(dom, ROW_Y), lax.rem(dom, ROW_Y)
    along_x = {step: lax.rem(cx + (step + planes), planes) * ROW_Y for step in (-1, 0, 1)}
    along_y = {step: lax.rem(cy + (step + ROW_Y), ROW_Y) for step in (-1, 0, 1)}
    along_z = {step: lax.rem(cz + (step + depth), depth) for step in (-1, 0, 1)}

    def place(vec, sign):
        return (along_x[sign * vec[0]] + along_y[sign * vec[1]], along_z[sign * vec[2]])

    loads = []
    for step, (source, target) in enumerate(
        [
            (send_hbm, send_v),
            (prefix_hbm, prefix),
            (feat_hbm, feat_v),
            (pos_hbm, pos_v),
            (src_hbm, src_v),
            (dst_hbm, dst_v),
            (wsrc_hbm, wsrc_v),
            (wdst_hbm, wdst_v),
            (wrad_hbm, wrad_v),
            (wenv_hbm, wenv_v),
            (wlat_hbm, wlat_v),
            (whid_hbm, whid_v),
            (wro_hbm, wro_v),
            (fill_hbm, fill),
        ]
    ):
        copy = pltpu.make_async_copy(source, target, in_sem.at[step])
        copy.start()
        loads.append(copy)

    barrier = pltpu.get_barrier_semaphore()
    for d in TABLE:
        pl.semaphore_signal(barrier, inc=1, device_id=place(d["vec"], 1), device_id_type=MESH)

    loads[0].wait()
    listed = jnp.where(iota((ATOMS, 608), 0) == send_v[...], 1.0, 0.0)
    list_v[0:608, :] = listed.T
    list_v[608:640, :] = jnp.zeros((32, ATOMS), F32)
    loads[1].wait()
    loads[2].wait()
    loads[3].wait()
    feat16 = feat_v[...].astype(BF16)
    pos = pos_v[...]
    own8 = rows_to_eight([pos[0:1], pos[1:2], pos[2:3], jnp.ones((1, ATOMS), F32)], 4)
    own_pieces = split_rows(own8, 3)
    lane = iota((8, 128), 1)
    line = iota((8, 128), 0)

    def store_coords(ref, slots, shifted):
        for d in TABLE:
            tile, low = d["slot"] // 128 * 128, d["slot"] % 128
            inside = (lane >= low) & (lane < low + d["rows"])
            coords = slots[:, tile : tile + 128]
            if shifted:
                shift = jnp.zeros((8, 128), F32)
                for step in range(3):
                    if d["vec"][step]:
                        shift = jnp.where(line == 4 + step, float(d["vec"][step]), shift)
                coords = coords - shift
            ref[d["tile"] : d["tile"] + 4, :] = jnp.where(inside, coords, 0.0)[4:8]

    def remote(source, target, start, size, pair, vec, sign):
        rows = pl.ds(start, size)
        return pltpu.make_async_remote_copy(
            src_ref=source.at[rows],
            dst_ref=target.at[rows],
            send_sem=sems.at[pair],
            recv_sem=sems.at[pair + 1],
            device_id=place(vec, sign),
            device_id_type=MESH,
        )

    def send_lines(table, source, target, pair, sign):
        for d in table:
            remote(source, target, d["slot"], d["cap"], pair, d["vec"], sign).start()

    def send_coords(source, target, pair, sign):
        for d in TABLE[::-1]:
            remote(source, target, d["tile"], 4, pair, d["vec"], sign).start()

    def lines_of(source, target, pair):
        return remote(source, target, 0, FEAT_SENT, pair, TABLE[0]["vec"], 1)

    def coords_of(source, target, pair):
        return remote(source, target, 0, COORDS_SENT, pair, TABLE[0]["vec"], 1)

    for d in TABLE:
        n, rows = d["number"], d["rows"]
        count = prefix[0, n + 1] - prefix[0, n]
        lines = list_v[pl.ds(prefix[0, n], rows), :]
        pick_v[d["slot"] : d["slot"] + rows, :] = jnp.where(iota((rows, ATOMS), 0) < count, lines, 0.0)
    pick = pick_v[...].astype(BF16)
    store_coords(coords_out1, sum_pieces(nt(own_pieces, pick), 3), True)
    out1[...] = mm(pick, feat16)
    groups = [[d for d in TABLE[::-1] if d["kind"] > 1], [d for d in TABLE if d["kind"] == 1]]
    split_at = groups[1][-1]["slot"] + groups[1][-1]["rows"]
    spans = [(split_at, SLOTS), (0, split_at)]
    pl.semaphore_wait(barrier, len(TABLE))
    send_coords(coords_out1, coords_in1, 0, 1)
    for table in groups:
        send_lines(table, out1, in1, 2, 1)

    for copy in loads[4:]:
        copy.wait()
    src_row, dst_row = src_v[...], dst_v[...]
    centre = onehot(iota((ATOMS, EDGES), 0) == src_row)
    near = onehot(iota((ATOMS, EDGES), 0) == dst_row)
    ghost = slot_ids(dst_row)
    same = (tn(centre, centre) * (1.0 / NEIGHBOURS)).astype(BF16)
    in_fill = jnp.where(iota((1, EDGES), 1) < fill[...], 1.0, 0.0)
    eye = iota((CH, CH), 0) == iota((CH, CH), 1)
    mix = mixing(wenv_v[...], wlat_v[...])
    w = dict(
        dst_t=wdst_v[...].T,
        rad_t=wrad_v[...].T,
        mix=jnp.concatenate(mix, axis=0),
        mix_t=jnp.concatenate([part.T for part in mix], axis=0),
        hid_t=whid_v[...].T,
        rad=wrad_v[...],
        hid=whid_v[...],
        ro=jnp.sum(jnp.where(eye, wro_v[...], 0.0), axis=1, keepdims=True),
    )
    feat_t = feat16.T
    own_lhs = jnp.concatenate([feat_t, own_pieces], axis=0)
    at_i = mm(own_lhs, centre)
    at_j = mm(own_lhs, near)
    pre_own = mm(wsrc_v[...].T, at_i[:CH].astype(BF16)) + mm(w["dst_t"], at_j[:CH].astype(BF16))
    pos_i = sum_pieces(at_i[CH:], 3)
    pos_j_own = sum_pieces(at_j[CH:], 3)
    pick_t_v[...] = pick.T
    pick_out = pltpu.make_async_copy(pick_t_v, pick_hbm, out_sem.at[0])
    pick_out.start()

    coords_of(coords_out1, coords_in1, 0).wait_recv()
    pos_g = mm(split_rows(unpack_coords(coords_in1), 3), ghost)
    geo = geometry(pos_i, pos_j_own + sum_pieces(pos_g, 3), in_fill, same)

    pre_known = pre_own + mm(w["rad_t"], geo["radial"].astype(BF16))

    lines_of(out1, in1, 2).wait_recv()
    far = nt(w["dst_t"], unpack_lines(in1)).astype(BF16)
    dpre, kept = edge_pass(pre_known + mm(far, ghost), geo, w)

    for table, (first, last) in zip(groups, spans):
        out2[first:last, :] = nt(ghost[first:last], dpre)
        send_lines(table, out2, in2, 4, -1)
    dq_pieces = split_rows(edge_coords(dpre, kept, geo, same, w), 2)
    store_coords(coords_out2, sum_pieces(nt(dq_pieces, ghost), 2), False)
    send_coords(coords_out2, coords_in2, 6, -1)

    own = nt(jnp.concatenate([centre, near], axis=0), dpre).astype(BF16)
    own_v[0:ATOMS, :] = nt(own[:ATOMS], wsrc_v[...]) + nt(own[ATOMS:], wdst_v[...])
    own_v[ATOMS:, :] = sum_pieces(nt(dq_pieces, near - centre), 2)
    own_out = pltpu.make_async_copy(own_v, own_hbm, out_sem.at[1])
    own_out.start()

    pick_out.wait()
    own_out.wait()
    coords_of(coords_out1, coords_in1, 0).wait_send()
    lines_of(out1, in1, 2).wait_send()
    lines_of(out2, in2, 4).wait()
    coords_of(coords_out2, coords_in2, 6).wait()


def finish(back_ref, coords_ref, own_ref, pick_ref, wdst_ref, force_ref, grad_ref):
    pick_t = pick_ref[...]
    returned = mm(pick_t, unpack_lines(back_ref)).astype(BF16)
    grad_ref[...] = own_ref[0:ATOMS, :] + nt(returned, wdst_ref[...])
    total8 = own_ref[ATOMS:, :] + sum_pieces(nt(split_rows(unpack_coords(coords_ref), 2), pick_t), 2)
    force_ref[...] = -total8[4:7]


def body(
    features,
    positions,
    send_ids,
    ghost_prefix,
    edge_fill,
    edge_src,
    edge_dst,
    weight_src,
    weight_dst,
    weight_radial,
    weight_env,
    weight_latent,
    weight_hidden,
    weight_readout,
):
    arrays = [
        features,
        positions,
        send_ids,
        edge_src,
        edge_dst,
        weight_src,
        weight_dst,
        weight_radial,
        weight_env,
        weight_latent,
        weight_hidden,
        weight_readout.reshape(1, CH),
    ]
    hbm = pl.BlockSpec(memory_space=pltpu.HBM)
    vmem = pl.BlockSpec(memory_space=pltpu.VMEM)
    back, coords, own, pick_t = pl.pallas_call(
        kernel,
        out_shape=(
            jax.ShapeDtypeStruct((SLOTS, CH), F32),
            jax.ShapeDtypeStruct((COORDS, CH), F32),
            jax.ShapeDtypeStruct((ATOMS + 8, CH), F32),
            jax.ShapeDtypeStruct((ATOMS, SLOTS), BF16),
        ),
        in_specs=[hbm] * (2 + len(arrays)),
        out_specs=(hbm, hbm, hbm, hbm),
        scratch_shapes=[pltpu.SMEM(ghost_prefix.shape, jnp.int32), pltpu.VMEM((1, 1), jnp.int32)]
        + [pltpu.VMEM(a.shape, a.dtype) for a in arrays]
        + [
            pltpu.VMEM((SLOTS, ATOMS), F32),
            pltpu.VMEM((SLOTS, ATOMS), F32),
            pltpu.VMEM((SLOTS, CH), F32),
            pltpu.VMEM((SLOTS, CH), F32),
            pltpu.VMEM((COORDS, CH), F32),
            pltpu.VMEM((COORDS, CH), F32),
            pltpu.VMEM((SLOTS, CH), F32),
            pltpu.VMEM((COORDS, CH), F32),
            pltpu.VMEM((ATOMS + 8, CH), F32),
            pltpu.VMEM((ATOMS, SLOTS), BF16),
            pltpu.SemaphoreType.DMA((2 + len(arrays),)),
            pltpu.SemaphoreType.DMA((8,)),
            pltpu.SemaphoreType.DMA((2,)),
        ],
        compiler_params=pltpu.CompilerParams(collective_id=0, has_side_effects=True, vmem_limit_bytes=VMEM),
        name="allegro",
    )(ghost_prefix, edge_fill.reshape(1, 1), *arrays)
    return pl.pallas_call(
        finish,
        out_shape=(
            jax.ShapeDtypeStruct((3, ATOMS), F32),
            jax.ShapeDtypeStruct((ATOMS, CH), F32),
        ),
        in_specs=[vmem] * 5,
        out_specs=(vmem, vmem),
        compiler_params=pltpu.CompilerParams(vmem_limit_bytes=VMEM),
        name="finish",
    )(back, coords, own, pick_t, weight_dst)


def solution(mesh):
    return jax.shard_map(
        body,
        mesh=mesh,
        in_specs=(
            P(("dom", "gz"), None),
            P(None, ("dom", "gz")),
            P(("dom", "gz"), None),
            P(("dom", "gz"), None),
            P(("dom", "gz")),
            P(("dom", "gz"), None),
            P(("dom", "gz"), None),
            P(),
            P(),
            P(),
            P(),
            P(),
            P(),
            P(),
        ),
        out_specs=(P(None, ("dom", "gz")), P(("dom", "gz"), None)),
        check_vma=False,
    )
```

```python
import math

import jax
import jax.numpy as jnp
import numpy as np
from jax import lax
from jax.experimental import pallas as pl
from jax.experimental.pallas import tpu as pltpu
from jax.sharding import PartitionSpec as P

NEIGHBOURS = 4
CAPS = (0, 64, 16, 4)
ROW_Y = 8

ATOMS = 128
EDGES = 512
CH = 128
SLOTS = 640
SHARPNESS = 8.0
VMEM = 56 * 1024 * 1024

BF16 = jnp.bfloat16
F32 = jnp.float32
MESH = pl.DeviceIdType.MESH


def directions():
    table = []
    offset = 0
    number = 0
    for a in (-1, 0, 1):
        for b in (-1, 0, 1):
            for c in (-1, 0, 1):
                kind = abs(a) + abs(b) + abs(c)
                if kind == 0:
                    continue
                cap = CAPS[kind]
                table.append(dict(vec=(a, b, c), kind=kind, cap=cap, number=number, offset=offset))
                offset += cap
                number += 1
    table.sort(key=lambda d: (d["kind"], d["number"]))
    slot = 0
    for step, d in enumerate(table):
        d["rows"] = {1: 64, 2: 16, 3: 8}[d["kind"]]
        d["slot"] = slot
        d["tile"] = 8 * step
        slot += d["rows"]
    assert slot == SLOTS
    return table


TABLE = directions()
FACES = [d for d in TABLE if d["kind"] == 1]
LINES = [d for d in TABLE if d["kind"] == 2]
CORNERS = [d for d in TABLE if d["kind"] == 3]
LINES_AT, CORNERS_AT = LINES[0]["slot"], CORNERS[0]["slot"]
COORDS = 8 * len(TABLE)
COORDS_SENT = 4 * len(TABLE) + 4 * len(CORNERS)


def mm(a, b):
    return lax.dot_general(a, b, (((1,), (0,)), ((), ())), preferred_element_type=F32)


def nt(a, b):
    return lax.dot_general(a, b, (((1,), (1,)), ((), ())), preferred_element_type=F32)


def tn(a, b):
    return lax.dot_general(a, b, (((0,), (0,)), ((), ())), preferred_element_type=F32)


def iota(shape, dim):
    return lax.broadcasted_iota(jnp.int32, shape, dim)


def onehot(cond):
    return jnp.where(cond, 1.0, 0.0).astype(BF16)


def split(x, pieces):
    out = []
    for step in range(pieces):
        part = x.astype(BF16)
        out.append(part)
        if step + 1 < pieces:
            x = x - part.astype(F32)
    return out


def split_rows(x, pieces):
    parts = []
    for step in range(pieces):
        part = x.astype(BF16).astype(F32)
        parts.append(part)
        x = x - part
    if pieces % 2:
        parts.append(jnp.zeros_like(x))
    return jnp.concatenate(parts, axis=0).astype(BF16)


def sum_pieces(x, pieces):
    total = x[0:8]
    for step in range(1, pieces):
        total = total + x[8 * step : 8 * step + 8]
    return total


def sigmoid(v):
    return 0.5 * jnp.tanh(0.5 * v) + 0.5


def silu_pair(v):
    sig = sigmoid(v)
    value = v * sig
    return value, sig + value * (1.0 - sig)


def rows_to_eight(rows, first):
    place = iota((8, rows[0].shape[1]), 0)
    out = jnp.zeros((8, rows[0].shape[1]), F32)
    for step, row in enumerate(rows):
        out = jnp.where(place == first + step, row, out)
    return out


def slot_ids(dst_row):
    blocks = []
    for d in TABLE:
        if d["kind"] <= 2:
            place = iota((d["rows"], EDGES), 0) + (ATOMS + d["offset"])
            blocks.append(onehot(place == dst_row))
    place = iota((8 * len(CORNERS), EDGES), 0)
    inner = place % 8
    base = jnp.zeros_like(place)
    for step, d in enumerate(CORNERS):
        base = jnp.where(place // 8 == step, ATOMS - 4 + d["offset"], base)
    blocks.append(onehot((inner >= 4) & (base + inner == dst_row)))
    return jnp.concatenate(blocks, axis=0)


def side_by_side(x):
    rows = x.shape[0] // 3
    return jnp.concatenate([x[rows * step : rows * (step + 1)] for step in range(3)], axis=1)


def mixing(wenv, wlat):
    parts = [wlat[:CH]]
    for step in range(1, 4):
        parts.append(mm(wenv, wlat[CH * step : CH * (step + 1)]).astype(BF16))
    return parts


def geometry(pos_i, pos_j, in_fill, same):
    diff = pos_j - pos_i
    qx, qy, qz = diff[4:5], diff[5:6], diff[6:7]
    live = pos_j[7:8]
    rsq = qx * qx + qy * qy + qz * qz
    in_use = in_fill * live
    inside = jnp.where(rsq < 1.0, 1.0 - rsq, 0.0)
    env = inside * inside * in_use
    centers = iota((8, EDGES), 0).astype(F32) / 7.0
    offset = rsq - centers
    radial = jnp.exp(-SHARPNESS * offset * offset)

    r3, r15, r5 = math.sqrt(3.0), math.sqrt(15.0), math.sqrt(5.0)
    y1 = rows_to_eight([r3 * qx, r3 * qy, r3 * qz], 0)
    y2 = rows_to_eight(
        [
            r15 * qx * qy,
            r15 * qy * qz,
            r15 * qz * qx,
            0.5 * r15 * (qx * qx - qy * qy),
            0.5 * r5 * (2.0 * qz * qz - qx * qx - qy * qy),
        ],
        0,
    )
    h1, l1 = (part.astype(F32) for part in split(y1, 2))
    h2, l2 = (part.astype(F32) for part in split(y2, 2))
    zero8 = jnp.zeros((8, EDGES), F32)
    left1 = jnp.concatenate([h1, h1, l1, zero8], axis=0).astype(BF16)
    right1 = jnp.concatenate([h1, l1, h1, zero8], axis=0).astype(BF16)
    left2 = jnp.concatenate([h2, h2, l2, zero8], axis=0).astype(BF16)
    right2 = jnp.concatenate([h2, l2, h2, zero8], axis=0).astype(BF16)
    k1 = tn(left1, right1).astype(BF16) * same
    k2 = tn(left2, right2).astype(BF16) * same

    return dict(
        q=(qx, qy, qz),
        in_use=in_use,
        inside=inside,
        env=env,
        offset=offset,
        radial=radial,
        left1=left1,
        left2=left2,
        kernels=jnp.concatenate([same, k1, k2], axis=0),
    )


def edge_pass(pre, geo, w):
    env, kernels = geo["env"], geo["kernels"]
    act, dact = silu_pair(pre)
    latent = (act * env).astype(BF16)
    mixed = mm(w["mix_t"], latent)
    near_far = mixed[CH:].astype(BF16)
    upd = mixed[:CH] + mm(side_by_side(near_far), kernels)
    upd_act, upd_d = silu_pair(upd)
    updated = (latent.astype(F32) + upd_act).astype(BF16)
    hid = mm(w["hid_t"], updated)
    hid_act, hid_d = silu_pair(hid)
    ro = w["ro"]
    dhid = (hid_d * ro * env).astype(BF16)
    dupdated = mm(w["hid"], dhid).astype(BF16).astype(F32)
    dupd = (dupdated * upd_d).astype(BF16)
    dmixed = mm(w["mix"], dupd)
    dlatent = dupdated + dmixed[:CH] + mm(side_by_side(dmixed[CH:].astype(BF16)), kernels)
    dpre = (dlatent * env * dact).astype(BF16)
    b1, b2 = near_far[CH : 2 * CH], near_far[2 * CH :]
    dupd_t = dupd.T
    pairs = [
        (jnp.concatenate([dupd_t, b.T], axis=1), jnp.concatenate([b, dupd], axis=0)) for b in (b1, b2)
    ]
    return dpre, (dlatent, act, hid_act, pairs)


def edge_coords(dpre, kept, geo, same, w):
    dlatent, act, hid_act, pairs = kept
    r3, r15, r5 = math.sqrt(3.0), math.sqrt(15.0), math.sqrt(5.0)
    qx, qy, qz = geo["q"]
    denv = jnp.sum(hid_act * w["ro"] + dlatent * act, axis=0, keepdims=True)
    t1, t2 = (mm(*pair).astype(BF16) * same for pair in pairs)
    dy1 = mm(geo["left1"], t1)
    dy1 = dy1[0:8] + dy1[16:24]
    dy2 = mm(geo["left2"], t2)
    dy2 = dy2[0:8] + dy2[16:24]

    drad = mm(w["rad"], dpre)
    drsq = jnp.sum(drad * geo["radial"] * geo["offset"], axis=0, keepdims=True) * (-2.0 * SHARPNESS)
    drsq = drsq - 2.0 * denv * geo["in_use"] * geo["inside"]
    a0, a1, a2, a3, a4 = (dy2[step : step + 1] for step in range(5))
    two = 2.0 * drsq
    gx = two * qx + r3 * dy1[0:1] + r15 * (a0 * qy + a2 * qz + a3 * qx) - r5 * a4 * qx
    gy = two * qy + r3 * dy1[1:2] + r15 * (a0 * qx + a1 * qz - a3 * qy) - r5 * a4 * qy
    gz = two * qz + r3 * dy1[2:3] + r15 * (a1 * qy + a2 * qx) + 2.0 * r5 * a4 * qz
    return rows_to_eight([gx, gy, gz], 4)


def corner_lines(ref):
    tiles = ref[CORNERS[0]["tile"] :, :]
    return jnp.where(iota(tiles.shape, 0) % 8 >= 4, tiles, 0.0).astype(BF16)


def unpack_coords(ref):
    tiles = [None] * (SLOTS // 128)
    for d in TABLE:
        tile = d["slot"] // 128
        piece = ref[d["tile"] : d["tile"] + 4, :]
        tiles[tile] = piece if tiles[tile] is None else tiles[tile] + piece
    coords = jnp.concatenate(tiles, axis=1)
    return jnp.concatenate([jnp.zeros_like(coords), coords], axis=0)


def kernel(
    prefix_hbm,
    fill_hbm,
    feat_hbm,
    pos_hbm,
    send_hbm,
    src_hbm,
    dst_hbm,
    wsrc_hbm,
    wdst_hbm,
    wrad_hbm,
    wenv_hbm,
    wlat_hbm,
    whid_hbm,
    wro_hbm,
    in2,
    coords_in2,
    own_hbm,
    pick_hbm,
    prefix,
    fill,
    feat_v,
    pos_v,
    send_v,
    src_v,
    dst_v,
    wsrc_v,
    wdst_v,
    wrad_v,
    wenv_v,
    wlat_v,
    whid_v,
    wro_v,
    list_v,
    pick_v,
    out1,
    in1,
    coords_out1,
    coords_in1,
    out2,
    coords_out2,
    own_v,
    pick_t_v,
    in_sem,
    sems,
    out_sem,
):
    planes = lax.axis_size("dom") // ROW_Y
    depth = lax.axis_size("gz")
    dom = lax.axis_index("dom")
    cz = lax.axis_index("gz")
    cx, cy = lax.div(dom, ROW_Y), lax.rem(dom, ROW_Y)
    along_x = {step: lax.rem(cx + (step + planes), planes) * ROW_Y for step in (-1, 0, 1)}
    along_y = {step: lax.rem(cy + (step + ROW_Y), ROW_Y) for step in (-1, 0, 1)}
    along_z = {step: lax.rem(cz + (step + depth), depth) for step in (-1, 0, 1)}

    def place(vec, sign):
        return (along_x[sign * vec[0]] + along_y[sign * vec[1]], along_z[sign * vec[2]])

    loads = []
    for step, (source, target) in enumerate(
        [
            (send_hbm, send_v),
            (prefix_hbm, prefix),
            (feat_hbm, feat_v),
            (pos_hbm, pos_v),
            (src_hbm, src_v),
            (dst_hbm, dst_v),
            (wsrc_hbm, wsrc_v),
            (wdst_hbm, wdst_v),
            (wrad_hbm, wrad_v),
            (wenv_hbm, wenv_v),
            (wlat_hbm, wlat_v),
            (whid_hbm, whid_v),
            (wro_hbm, wro_v),
            (fill_hbm, fill),
        ]
    ):
        copy = pltpu.make_async_copy(source, target, in_sem.at[step])
        copy.start()
        loads.append(copy)

    barrier = pltpu.get_barrier_semaphore()
    for d in TABLE:
        pl.semaphore_signal(barrier, inc=1, device_id=place(d["vec"], 1), device_id_type=MESH)

    loads[0].wait()
    listed = jnp.where(iota((ATOMS, 608), 0) == send_v[...], 1.0, 0.0)
    list_v[0:608, :] = listed.T
    list_v[608:640, :] = jnp.zeros((32, ATOMS), F32)
    loads[1].wait()
    loads[2].wait()
    loads[3].wait()
    feat16 = feat_v[...].astype(BF16)
    pos = pos_v[...]
    own8 = rows_to_eight([pos[0:1], pos[1:2], pos[2:3], jnp.ones((1, ATOMS), F32)], 4)
    own_pieces = split_rows(own8, 3)
    lane = iota((8, 128), 1)
    line = iota((8, 128), 0)

    def store_coords(ref, slots, corners, shifted):
        for d in TABLE:
            tile, low = d["slot"] // 128 * 128, d["slot"] % 128
            inside = (lane >= low) & (lane < low + d["rows"])
            coords = slots[:, tile : tile + 128]
            if shifted:
                shift = jnp.zeros((8, 128), F32)
                for step in range(3):
                    if d["vec"][step]:
                        shift = jnp.where(line == 4 + step, float(d["vec"][step]), shift)
                coords = coords - shift
            coords = jnp.where(inside, coords, 0.0)[4:8]
            if d["kind"] == 3:
                first = d["slot"] - CORNERS_AT
                coords = jnp.concatenate([coords, corners[first + 4 : first + 8]], axis=0)
            ref[d["tile"] : d["tile"] + coords.shape[0], :] = coords

    def remote(source, target, start, size, pair, vec, sign):
        rows = pl.ds(start, size)
        return pltpu.make_async_remote_copy(
            src_ref=source.at[rows],
            dst_ref=target.at[rows],
            send_sem=sems.at[pair],
            recv_sem=sems.at[pair + 1],
            device_id=place(vec, sign),
            device_id_type=MESH,
        )

    def send_lines(table, source, target, pair, sign):
        for d in table:
            remote(source, target, d["slot"], d["rows"], pair, d["vec"], sign).start()

    def send_coords(source, target, pair, sign):
        for d in TABLE[::-1]:
            remote(source, target, d["tile"], 8 if d["kind"] == 3 else 4, pair, d["vec"], sign).start()

    def lines_of(source, target, pair, first, last):
        return remote(source, target, first, last - first, pair, TABLE[0]["vec"], 1)

    def coords_of(source, target, pair):
        return remote(source, target, 0, COORDS_SENT, pair, TABLE[0]["vec"], 1)

    for d in TABLE:
        n, rows = d["number"], d["rows"]
        count = prefix[0, n + 1] - prefix[0, n]
        lines = list_v[pl.ds(prefix[0, n], rows), :]
        lines = jnp.where(iota((rows, ATOMS), 0) < count, lines, 0.0)
        if d["kind"] == 3:
            lines = jnp.concatenate([jnp.zeros((4, ATOMS), F32), lines[:4]], axis=0)
        pick_v[d["slot"] : d["slot"] + rows, :] = lines
    pick = pick_v[...].astype(BF16)
    packed = mm(pick, feat16)
    store_coords(coords_out1, sum_pieces(nt(own_pieces, pick), 3), packed[CORNERS_AT:], True)
    out1[...] = packed[:CORNERS_AT]
    pl.semaphore_wait(barrier, len(TABLE))
    send_coords(coords_out1, coords_in1, 0, 1)
    send_lines(LINES, out1, in1, 2, 1)
    send_lines(FACES, out1, in1, 4, 1)

    for copy in loads[4:]:
        copy.wait()
    src_row, dst_row = src_v[...], dst_v[...]
    centre = onehot(iota((ATOMS, EDGES), 0) == src_row)
    near = onehot(iota((ATOMS, EDGES), 0) == dst_row)
    ghost = slot_ids(dst_row)
    same = (tn(centre, centre) * (1.0 / NEIGHBOURS)).astype(BF16)
    in_fill = jnp.where(iota((1, EDGES), 1) < fill[...], 1.0, 0.0)
    eye = iota((CH, CH), 0) == iota((CH, CH), 1)
    mix = mixing(wenv_v[...], wlat_v[...])
    w = dict(
        dst_t=wdst_v[...].T,
        rad_t=wrad_v[...].T,
        mix=jnp.concatenate(mix, axis=0),
        mix_t=jnp.concatenate([part.T for part in mix], axis=0),
        hid_t=whid_v[...].T,
        rad=wrad_v[...],
        hid=whid_v[...],
        ro=jnp.sum(jnp.where(eye, wro_v[...], 0.0), axis=1, keepdims=True),
    )
    feat_t = feat16.T
    own_lhs = jnp.concatenate([feat_t, own_pieces], axis=0)
    at_i = mm(own_lhs, centre)
    at_j = mm(own_lhs, near)
    pre_own = mm(wsrc_v[...].T, at_i[:CH].astype(BF16)) + mm(w["dst_t"], at_j[:CH].astype(BF16))
    pos_i = sum_pieces(at_i[CH:], 3)
    pos_j_own = sum_pieces(at_j[CH:], 3)
    pick_t_v[...] = pick.T
    pick_out = pltpu.make_async_copy(pick_t_v, pick_hbm, out_sem.at[0])
    pick_out.start()

    coords_of(coords_out1, coords_in1, 0).wait_recv()
    pos_g = mm(split_rows(unpack_coords(coords_in1), 3), ghost)
    geo = geometry(pos_i, pos_j_own + sum_pieces(pos_g, 3), in_fill, same)

    pre_known = pre_own + mm(w["rad_t"], geo["radial"].astype(BF16))

    lines_of(out1, in1, 2, LINES_AT, CORNERS_AT).wait_recv()
    some = jnp.concatenate([in1[LINES_AT:, :].astype(BF16), corner_lines(coords_in1)], axis=0)
    pre_known = pre_known + mm(nt(w["dst_t"], some).astype(BF16), ghost[LINES_AT:])
    lines_of(out1, in1, 4, 0, LINES_AT).wait_recv()
    far = nt(w["dst_t"], in1[0:LINES_AT, :].astype(BF16)).astype(BF16)
    dpre, kept = edge_pass(pre_known + mm(far, ghost[:LINES_AT]), geo, w)

    some = nt(ghost[LINES_AT:], dpre)
    out2[LINES_AT:, :] = some[: CORNERS_AT - LINES_AT]
    send_lines(LINES, out2, in2, 6, -1)
    out2[0:LINES_AT, :] = nt(ghost[:LINES_AT], dpre)
    send_lines(FACES, out2, in2, 8, -1)
    dq_pieces = split_rows(edge_coords(dpre, kept, geo, same, w), 2)
    store_coords(coords_out2, sum_pieces(nt(dq_pieces, ghost), 2), some[CORNERS_AT - LINES_AT :], False)
    send_coords(coords_out2, coords_in2, 10, -1)

    own = nt(jnp.concatenate([centre, near], axis=0), dpre).astype(BF16)
    own_v[0:ATOMS, :] = nt(own[:ATOMS], wsrc_v[...]) + nt(own[ATOMS:], wdst_v[...])
    own_v[ATOMS:, :] = sum_pieces(nt(dq_pieces, near - centre), 2)
    own_out = pltpu.make_async_copy(own_v, own_hbm, out_sem.at[1])
    own_out.start()

    pick_out.wait()
    own_out.wait()
    coords_of(coords_out1, coords_in1, 0).wait_send()
    for pair, first, last in ((2, LINES_AT, CORNERS_AT), (4, 0, LINES_AT)):
        lines_of(out1, in1, pair, first, last).wait_send()
        lines_of(out2, in2, pair + 4, first, last).wait()
    coords_of(coords_out2, coords_in2, 10).wait()


def finish(back_ref, coords_ref, own_ref, pick_ref, wdst_ref, force_ref, grad_ref):
    pick_t = pick_ref[...]
    lines = jnp.concatenate([back_ref[...].astype(BF16), corner_lines(coords_ref)], axis=0)
    returned = mm(pick_t, lines).astype(BF16)
    grad_ref[...] = own_ref[0:ATOMS, :] + nt(returned, wdst_ref[...])
    total8 = own_ref[ATOMS:, :] + sum_pieces(nt(split_rows(unpack_coords(coords_ref), 2), pick_t), 2)
    force_ref[...] = -total8[4:7]


def body(
    features,
    positions,
    send_ids,
    ghost_prefix,
    edge_fill,
    edge_src,
    edge_dst,
    weight_src,
    weight_dst,
    weight_radial,
    weight_env,
    weight_latent,
    weight_hidden,
    weight_readout,
):
    arrays = [
        features,
        positions,
        send_ids,
        edge_src,
        edge_dst,
        weight_src,
        weight_dst,
        weight_radial,
        weight_env,
        weight_latent,
        weight_hidden,
        weight_readout.reshape(1, CH),
    ]
    hbm = pl.BlockSpec(memory_space=pltpu.HBM)
    vmem = pl.BlockSpec(memory_space=pltpu.VMEM)
    back, coords, own, pick_t = pl.pallas_call(
        kernel,
        out_shape=(
            jax.ShapeDtypeStruct((CORNERS_AT, CH), F32),
            jax.ShapeDtypeStruct((COORDS, CH), F32),
            jax.ShapeDtypeStruct((ATOMS + 8, CH), F32),
            jax.ShapeDtypeStruct((ATOMS, SLOTS), BF16),
        ),
        in_specs=[hbm] * (2 + len(arrays)),
        out_specs=(hbm, hbm, hbm, hbm),
        scratch_shapes=[pltpu.SMEM(ghost_prefix.shape, jnp.int32), pltpu.VMEM((1, 1), jnp.int32)]
        + [pltpu.VMEM(a.shape, a.dtype) for a in arrays]
        + [
            pltpu.VMEM((SLOTS, ATOMS), F32),
            pltpu.VMEM((SLOTS, ATOMS), F32),
            pltpu.VMEM((CORNERS_AT, CH), F32),
            pltpu.VMEM((CORNERS_AT, CH), F32),
            pltpu.VMEM((COORDS, CH), F32),
            pltpu.VMEM((COORDS, CH), F32),
            pltpu.VMEM((CORNERS_AT, CH), F32),
            pltpu.VMEM((COORDS, CH), F32),
            pltpu.VMEM((ATOMS + 8, CH), F32),
            pltpu.VMEM((ATOMS, SLOTS), BF16),
            pltpu.SemaphoreType.DMA((2 + len(arrays),)),
            pltpu.SemaphoreType.DMA((12,)),
            pltpu.SemaphoreType.DMA((2,)),
        ],
        compiler_params=pltpu.CompilerParams(collective_id=0, has_side_effects=True, vmem_limit_bytes=VMEM),
        name="allegro",
    )(ghost_prefix, edge_fill.reshape(1, 1), *arrays)
    return pl.pallas_call(
        finish,
        out_shape=(
            jax.ShapeDtypeStruct((3, ATOMS), F32),
            jax.ShapeDtypeStruct((ATOMS, CH), F32),
        ),
        in_specs=[vmem] * 5,
        out_specs=(vmem, vmem),
        compiler_params=pltpu.CompilerParams(vmem_limit_bytes=VMEM),
        name="finish",
    )(back, coords, own, pick_t, weight_dst)


def solution(mesh):
    return jax.shard_map(
        body,
        mesh=mesh,
        in_specs=(
            P(("dom", "gz"), None),
            P(None, ("dom", "gz")),
            P(("dom", "gz"), None),
            P(("dom", "gz"), None),
            P(("dom", "gz")),
            P(("dom", "gz"), None),
            P(("dom", "gz"), None),
            P(),
            P(),
            P(),
            P(),
            P(),
            P(),
            P(),
        ),
        out_specs=(P(None, ("dom", "gz")), P(("dom", "gz"), None)),
        check_vma=False,
    )
```

```python
import math

import jax
import jax.numpy as jnp
import numpy as np
from jax import lax
from jax.experimental import pallas as pl
from jax.experimental.pallas import tpu as pltpu
from jax.sharding import PartitionSpec as P

NEIGHBOURS = 4
CAPS = (0, 64, 16, 4)
ROW_Y = 8

ATOMS = 128
EDGES = 512
CH = 128
SLOTS = 640
SHARPNESS = 8.0
VMEM = 56 * 1024 * 1024

BF16 = jnp.bfloat16
F32 = jnp.float32
MESH = pl.DeviceIdType.MESH


def directions():
    table = []
    offset = 0
    number = 0
    for a in (-1, 0, 1):
        for b in (-1, 0, 1):
            for c in (-1, 0, 1):
                kind = abs(a) + abs(b) + abs(c)
                if kind == 0:
                    continue
                cap = CAPS[kind]
                table.append(dict(vec=(a, b, c), kind=kind, cap=cap, number=number, offset=offset))
                offset += cap
                number += 1
    table.sort(key=lambda d: (d["kind"], d["number"]))
    slot = 0
    for step, d in enumerate(table):
        d["rows"] = {1: 64, 2: 16, 3: 8}[d["kind"]]
        d["slot"] = slot
        d["tile"] = 8 * step
        slot += d["rows"]
    assert slot == SLOTS
    return table


TABLE = directions()
FACES = [d for d in TABLE if d["kind"] == 1]
LINES = [d for d in TABLE if d["kind"] == 2]
CORNERS = [d for d in TABLE if d["kind"] == 3]
LINES_AT, CORNERS_AT = LINES[0]["slot"], CORNERS[0]["slot"]
COORDS = 8 * len(TABLE)
COORDS_SENT = 4 * len(TABLE) + 4 * len(CORNERS)


def mm(a, b):
    return lax.dot_general(a, b, (((1,), (0,)), ((), ())), preferred_element_type=F32)


def nt(a, b):
    return lax.dot_general(a, b, (((1,), (1,)), ((), ())), preferred_element_type=F32)


def tn(a, b):
    return lax.dot_general(a, b, (((0,), (0,)), ((), ())), preferred_element_type=F32)


def iota(shape, dim):
    return lax.broadcasted_iota(jnp.int32, shape, dim)


def onehot(cond):
    return jnp.where(cond, 1.0, 0.0).astype(BF16)


def split(x, pieces):
    out = []
    for step in range(pieces):
        part = x.astype(BF16)
        out.append(part)
        if step + 1 < pieces:
            x = x - part.astype(F32)
    return out


def split_rows(x, pieces):
    parts = []
    for step in range(pieces):
        part = x.astype(BF16).astype(F32)
        parts.append(part)
        x = x - part
    if pieces % 2:
        parts.append(jnp.zeros_like(x))
    return jnp.concatenate(parts, axis=0).astype(BF16)


def sum_pieces(x, pieces):
    total = x[0:8]
    for step in range(1, pieces):
        total = total + x[8 * step : 8 * step + 8]
    return total


def sigmoid(v):
    return 0.5 * jnp.tanh(0.5 * v) + 0.5


def silu_pair(v):
    v = v.astype(BF16)
    sig = sigmoid(v)
    value = v * sig
    return value, sig + value * (1 - sig)


def rows_to_eight(rows, first):
    place = iota((8, rows[0].shape[1]), 0)
    out = jnp.zeros((8, rows[0].shape[1]), F32)
    for step, row in enumerate(rows):
        out = jnp.where(place == first + step, row, out)
    return out


def slot_ids(dst_row):
    blocks = []
    for d in TABLE:
        if d["kind"] <= 2:
            place = iota((d["rows"], EDGES), 0) + (ATOMS + d["offset"])
            blocks.append(onehot(place == dst_row))
    place = iota((8 * len(CORNERS), EDGES), 0)
    inner = place % 8
    base = jnp.zeros_like(place)
    for step, d in enumerate(CORNERS):
        base = jnp.where(place // 8 == step, ATOMS - 4 + d["offset"], base)
    blocks.append(onehot((inner >= 4) & (base + inner == dst_row)))
    return jnp.concatenate(blocks, axis=0)


def side_by_side(x):
    rows = x.shape[0] // 3
    return jnp.concatenate([x[rows * step : rows * (step + 1)] for step in range(3)], axis=1)


def mixing(wenv, wlat):
    parts = [wlat[:CH]]
    for step in range(1, 4):
        parts.append(mm(wenv, wlat[CH * step : CH * (step + 1)]).astype(BF16))
    return parts


def geometry(pos_i, pos_j, in_fill, same):
    diff = pos_j - pos_i
    qx, qy, qz = diff[4:5], diff[5:6], diff[6:7]
    live = pos_j[7:8]
    rsq = qx * qx + qy * qy + qz * qz
    in_use = in_fill * live
    inside = jnp.where(rsq < 1.0, 1.0 - rsq, 0.0)
    env = inside * inside * in_use
    centers = iota((8, EDGES), 0).astype(F32) / 7.0
    offset = rsq - centers
    radial = jnp.exp(-SHARPNESS * offset * offset)

    r3, r15, r5 = math.sqrt(3.0), math.sqrt(15.0), math.sqrt(5.0)
    y1 = rows_to_eight([r3 * qx, r3 * qy, r3 * qz], 0)
    y2 = rows_to_eight(
        [
            r15 * qx * qy,
            r15 * qy * qz,
            r15 * qz * qx,
            0.5 * r15 * (qx * qx - qy * qy),
            0.5 * r5 * (2.0 * qz * qz - qx * qx - qy * qy),
        ],
        0,
    )
    h1, l1 = (part.astype(F32) for part in split(y1, 2))
    h2, l2 = (part.astype(F32) for part in split(y2, 2))
    zero8 = jnp.zeros((8, EDGES), F32)
    left1 = jnp.concatenate([h1, h1, l1, zero8], axis=0).astype(BF16)
    right1 = jnp.concatenate([h1, l1, h1, zero8], axis=0).astype(BF16)
    left2 = jnp.concatenate([h2, h2, l2, zero8], axis=0).astype(BF16)
    right2 = jnp.concatenate([h2, l2, h2, zero8], axis=0).astype(BF16)
    k1 = tn(left1, right1).astype(BF16) * same
    k2 = tn(left2, right2).astype(BF16) * same

    return dict(
        q=(qx, qy, qz),
        in_use=in_use,
        inside=inside,
        env=env,
        offset=offset,
        radial=radial,
        left1=left1,
        left2=left2,
        kernels=jnp.concatenate([same, k1, k2], axis=0),
    )


def edge_pass(pre, geo, w):
    env, kernels = geo["env"], geo["kernels"]
    env16 = env.astype(BF16)
    act, dact = silu_pair(pre)
    latent = act * env16
    mixed = mm(w["mix_t"], latent)
    near_far = mixed[CH:].astype(BF16)
    upd_act, upd_d = silu_pair(mixed[:CH] + mm(side_by_side(near_far), kernels))
    hid_act, hid_d = silu_pair(mm(w["hid_t"], latent + upd_act))
    dhid = hid_d * (w["ro"] * env).astype(BF16)
    dupdated = mm(w["hid"], dhid)
    dupd = dupdated.astype(BF16) * upd_d
    dmixed = mm(w["mix"], dupd)
    dlatent = dupdated + dmixed[:CH] + mm(side_by_side(dmixed[CH:].astype(BF16)), kernels)
    dpre = (dlatent * env).astype(BF16) * dact
    b1, b2 = near_far[CH : 2 * CH], near_far[2 * CH :]
    dupd_t = dupd.T
    pairs = [
        (jnp.concatenate([dupd_t, b.T], axis=1), jnp.concatenate([b, dupd], axis=0)) for b in (b1, b2)
    ]
    return dpre, (dlatent, act, hid_act, pairs)


def edge_coords(dpre, kept, geo, same, w):
    dlatent, act, hid_act, pairs = kept
    r3, r15, r5 = math.sqrt(3.0), math.sqrt(15.0), math.sqrt(5.0)
    qx, qy, qz = geo["q"]
    denv = jnp.sum(hid_act * w["ro"] + dlatent * act, axis=0, keepdims=True)
    t1, t2 = (mm(*pair).astype(BF16) * same for pair in pairs)
    dy1 = mm(geo["left1"], t1)
    dy1 = dy1[0:8] + dy1[16:24]
    dy2 = mm(geo["left2"], t2)
    dy2 = dy2[0:8] + dy2[16:24]

    drad = mm(w["rad"], dpre)
    drsq = jnp.sum(drad * geo["radial"] * geo["offset"], axis=0, keepdims=True) * (-2.0 * SHARPNESS)
    drsq = drsq - 2.0 * denv * geo["in_use"] * geo["inside"]
    a0, a1, a2, a3, a4 = (dy2[step : step + 1] for step in range(5))
    two = 2.0 * drsq
    gx = two * qx + r3 * dy1[0:1] + r15 * (a0 * qy + a2 * qz + a3 * qx) - r5 * a4 * qx
    gy = two * qy + r3 * dy1[1:2] + r15 * (a0 * qx + a1 * qz - a3 * qy) - r5 * a4 * qy
    gz = two * qz + r3 * dy1[2:3] + r15 * (a1 * qy + a2 * qx) + 2.0 * r5 * a4 * qz
    return rows_to_eight([gx, gy, gz], 4)


def corner_lines(ref):
    tiles = ref[CORNERS[0]["tile"] :, :]
    return jnp.where(iota(tiles.shape, 0) % 8 >= 4, tiles, 0.0).astype(BF16)


def unpack_coords(ref):
    tiles = [None] * (SLOTS // 128)
    for d in TABLE:
        tile = d["slot"] // 128
        piece = ref[d["tile"] : d["tile"] + 4, :]
        tiles[tile] = piece if tiles[tile] is None else tiles[tile] + piece
    coords = jnp.concatenate(tiles, axis=1)
    return jnp.concatenate([jnp.zeros_like(coords), coords], axis=0)


def kernel(
    prefix_hbm,
    fill_hbm,
    feat_hbm,
    pos_hbm,
    send_hbm,
    src_hbm,
    dst_hbm,
    wsrc_hbm,
    wdst_hbm,
    wrad_hbm,
    wenv_hbm,
    wlat_hbm,
    whid_hbm,
    wro_hbm,
    in2,
    coords_in2,
    own_hbm,
    pick_hbm,
    prefix,
    fill,
    feat_v,
    pos_v,
    send_v,
    src_v,
    dst_v,
    wsrc_v,
    wdst_v,
    wrad_v,
    wenv_v,
    wlat_v,
    whid_v,
    wro_v,
    list_v,
    pick_v,
    out1,
    in1,
    coords_out1,
    coords_in1,
    out2,
    coords_out2,
    own_v,
    pick_t_v,
    in_sem,
    sems,
    out_sem,
):
    planes = lax.axis_size("dom") // ROW_Y
    depth = lax.axis_size("gz")
    dom = lax.axis_index("dom")
    cz = lax.axis_index("gz")
    cx, cy = lax.div(dom, ROW_Y), lax.rem(dom, ROW_Y)
    along_x = {step: lax.rem(cx + (step + planes), planes) * ROW_Y for step in (-1, 0, 1)}
    along_y = {step: lax.rem(cy + (step + ROW_Y), ROW_Y) for step in (-1, 0, 1)}
    along_z = {step: lax.rem(cz + (step + depth), depth) for step in (-1, 0, 1)}

    def place(vec, sign):
        return (along_x[sign * vec[0]] + along_y[sign * vec[1]], along_z[sign * vec[2]])

    loads = []
    for step, (source, target) in enumerate(
        [
            (send_hbm, send_v),
            (prefix_hbm, prefix),
            (feat_hbm, feat_v),
            (pos_hbm, pos_v),
            (src_hbm, src_v),
            (dst_hbm, dst_v),
            (wsrc_hbm, wsrc_v),
            (wdst_hbm, wdst_v),
            (wrad_hbm, wrad_v),
            (wenv_hbm, wenv_v),
            (wlat_hbm, wlat_v),
            (whid_hbm, whid_v),
            (wro_hbm, wro_v),
            (fill_hbm, fill),
        ]
    ):
        copy = pltpu.make_async_copy(source, target, in_sem.at[step])
        copy.start()
        loads.append(copy)

    barrier = pltpu.get_barrier_semaphore()
    for d in TABLE:
        pl.semaphore_signal(barrier, inc=1, device_id=place(d["vec"], 1), device_id_type=MESH)

    loads[0].wait()
    listed = jnp.where(iota((ATOMS, 608), 0) == send_v[...], 1.0, 0.0)
    list_v[0:608, :] = listed.T
    list_v[608:640, :] = jnp.zeros((32, ATOMS), F32)
    loads[1].wait()
    loads[2].wait()
    loads[3].wait()
    feat16 = feat_v[...].astype(BF16)
    pos = pos_v[...]
    own8 = rows_to_eight([pos[0:1], pos[1:2], pos[2:3], jnp.ones((1, ATOMS), F32)], 4)
    own_pieces = split_rows(own8, 3)
    lane = iota((8, 128), 1)
    line = iota((8, 128), 0)

    def store_coords(ref, slots, corners, shifted):
        for d in TABLE:
            tile, low = d["slot"] // 128 * 128, d["slot"] % 128
            inside = (lane >= low) & (lane < low + d["rows"])
            coords = slots[:, tile : tile + 128]
            if shifted:
                shift = jnp.zeros((8, 128), F32)
                for step in range(3):
                    if d["vec"][step]:
                        shift = jnp.where(line == 4 + step, float(d["vec"][step]), shift)
                coords = coords - shift
            coords = jnp.where(inside, coords, 0.0)[4:8]
            if d["kind"] == 3:
                first = d["slot"] - CORNERS_AT
                coords = jnp.concatenate([coords, corners[first + 4 : first + 8]], axis=0)
            ref[d["tile"] : d["tile"] + coords.shape[0], :] = coords

    def remote(source, target, start, size, pair, vec, sign):
        rows = pl.ds(start, size)
        return pltpu.make_async_remote_copy(
            src_ref=source.at[rows],
            dst_ref=target.at[rows],
            send_sem=sems.at[pair],
            recv_sem=sems.at[pair + 1],
            device_id=place(vec, sign),
            device_id_type=MESH,
        )

    def send_lines(table, source, target, pair, sign):
        for d in table:
            remote(source, target, d["slot"], d["rows"], pair, d["vec"], sign).start()

    def send_coords(source, target, pair, sign):
        for d in TABLE[::-1]:
            remote(source, target, d["tile"], 8 if d["kind"] == 3 else 4, pair, d["vec"], sign).start()

    def lines_of(source, target, pair, first, last):
        return remote(source, target, first, last - first, pair, TABLE[0]["vec"], 1)

    def coords_of(source, target, pair):
        return remote(source, target, 0, COORDS_SENT, pair, TABLE[0]["vec"], 1)

    for d in TABLE:
        n, rows = d["number"], d["rows"]
        count = prefix[0, n + 1] - prefix[0, n]
        lines = list_v[pl.ds(prefix[0, n], rows), :]
        lines = jnp.where(iota((rows, ATOMS), 0) < count, lines, 0.0)
        if d["kind"] == 3:
            lines = jnp.concatenate([jnp.zeros((4, ATOMS), F32), lines[:4]], axis=0)
        pick_v[d["slot"] : d["slot"] + rows, :] = lines
    pick = pick_v[...].astype(BF16)
    packed = mm(pick, feat16)
    store_coords(coords_out1, sum_pieces(nt(own_pieces, pick), 3), packed[CORNERS_AT:], True)
    out1[...] = packed[:CORNERS_AT]
    pl.semaphore_wait(barrier, len(TABLE))
    send_coords(coords_out1, coords_in1, 0, 1)
    send_lines(LINES, out1, in1, 2, 1)
    send_lines(FACES, out1, in1, 4, 1)

    for copy in loads[4:]:
        copy.wait()
    src_row, dst_row = src_v[...], dst_v[...]
    centre = onehot(iota((ATOMS, EDGES), 0) == src_row)
    near = onehot(iota((ATOMS, EDGES), 0) == dst_row)
    ghost = slot_ids(dst_row)
    same = (tn(centre, centre) * (1.0 / NEIGHBOURS)).astype(BF16)
    in_fill = jnp.where(iota((1, EDGES), 1) < fill[...], 1.0, 0.0)
    eye = iota((CH, CH), 0) == iota((CH, CH), 1)
    mix = mixing(wenv_v[...], wlat_v[...])
    w = dict(
        dst_t=wdst_v[...].T,
        rad_t=wrad_v[...].T,
        mix=jnp.concatenate(mix, axis=0),
        mix_t=jnp.concatenate([part.T for part in mix], axis=0),
        hid_t=whid_v[...].T,
        rad=wrad_v[...],
        hid=whid_v[...],
        ro=jnp.sum(jnp.where(eye, wro_v[...], 0.0), axis=1, keepdims=True),
    )
    feat_t = feat16.T
    own_lhs = jnp.concatenate([feat_t, own_pieces], axis=0)
    at_i = mm(own_lhs, centre)
    at_j = mm(own_lhs, near)
    pre_own = mm(wsrc_v[...].T, at_i[:CH].astype(BF16)) + mm(w["dst_t"], at_j[:CH].astype(BF16))
    pos_i = sum_pieces(at_i[CH:], 3)
    pos_j_own = sum_pieces(at_j[CH:], 3)
    pick_t_v[...] = pick.T
    pick_out = pltpu.make_async_copy(pick_t_v, pick_hbm, out_sem.at[0])
    pick_out.start()

    coords_of(coords_out1, coords_in1, 0).wait_recv()
    pos_g = mm(split_rows(unpack_coords(coords_in1), 3), ghost)
    geo = geometry(pos_i, pos_j_own + sum_pieces(pos_g, 3), in_fill, same)

    pre_known = pre_own + mm(w["rad_t"], geo["radial"].astype(BF16))

    lines_of(out1, in1, 2, LINES_AT, CORNERS_AT).wait_recv()
    some = jnp.concatenate([in1[LINES_AT:, :].astype(BF16), corner_lines(coords_in1)], axis=0)
    pre_known = pre_known + mm(nt(w["dst_t"], some).astype(BF16), ghost[LINES_AT:])
    lines_of(out1, in1, 4, 0, LINES_AT).wait_recv()
    far = nt(w["dst_t"], in1[0:LINES_AT, :].astype(BF16)).astype(BF16)
    dpre, kept = edge_pass(pre_known + mm(far, ghost[:LINES_AT]), geo, w)

    some = nt(ghost[LINES_AT:], dpre)
    out2[LINES_AT:, :] = some[: CORNERS_AT - LINES_AT]
    send_lines(LINES, out2, in2, 6, -1)
    out2[0:LINES_AT, :] = nt(ghost[:LINES_AT], dpre)
    send_lines(FACES, out2, in2, 8, -1)
    dq_pieces = split_rows(edge_coords(dpre, kept, geo, same, w), 2)
    store_coords(coords_out2, sum_pieces(nt(dq_pieces, ghost), 2), some[CORNERS_AT - LINES_AT :], False)
    send_coords(coords_out2, coords_in2, 10, -1)

    own = nt(jnp.concatenate([centre, near], axis=0), dpre).astype(BF16)
    own_v[0:ATOMS, :] = nt(own[:ATOMS], wsrc_v[...]) + nt(own[ATOMS:], wdst_v[...])
    own_v[ATOMS:, :] = sum_pieces(nt(dq_pieces, near - centre), 2)
    own_out = pltpu.make_async_copy(own_v, own_hbm, out_sem.at[1])
    own_out.start()

    pick_out.wait()
    own_out.wait()
    coords_of(coords_out1, coords_in1, 0).wait_send()
    for pair, first, last in ((2, LINES_AT, CORNERS_AT), (4, 0, LINES_AT)):
        lines_of(out1, in1, pair, first, last).wait_send()
        lines_of(out2, in2, pair + 4, first, last).wait()
    coords_of(coords_out2, coords_in2, 10).wait()


def finish(back_ref, coords_ref, own_ref, pick_ref, wdst_ref, force_ref, grad_ref):
    pick_t = pick_ref[...]
    lines = jnp.concatenate([back_ref[...].astype(BF16), corner_lines(coords_ref)], axis=0)
    returned = mm(pick_t, lines).astype(BF16)
    grad_ref[...] = own_ref[0:ATOMS, :] + nt(returned, wdst_ref[...])
    total8 = own_ref[ATOMS:, :] + sum_pieces(nt(split_rows(unpack_coords(coords_ref), 2), pick_t), 2)
    force_ref[...] = -total8[4:7]


def body(
    features,
    positions,
    send_ids,
    ghost_prefix,
    edge_fill,
    edge_src,
    edge_dst,
    weight_src,
    weight_dst,
    weight_radial,
    weight_env,
    weight_latent,
    weight_hidden,
    weight_readout,
):
    arrays = [
        features,
        positions,
        send_ids,
        edge_src,
        edge_dst,
        weight_src,
        weight_dst,
        weight_radial,
        weight_env,
        weight_latent,
        weight_hidden,
        weight_readout.reshape(1, CH),
    ]
    hbm = pl.BlockSpec(memory_space=pltpu.HBM)
    vmem = pl.BlockSpec(memory_space=pltpu.VMEM)
    back, coords, own, pick_t = pl.pallas_call(
        kernel,
        out_shape=(
            jax.ShapeDtypeStruct((CORNERS_AT, CH), F32),
            jax.ShapeDtypeStruct((COORDS, CH), F32),
            jax.ShapeDtypeStruct((ATOMS + 8, CH), F32),
            jax.ShapeDtypeStruct((ATOMS, SLOTS), BF16),
        ),
        in_specs=[hbm] * (2 + len(arrays)),
        out_specs=(hbm, hbm, hbm, hbm),
        scratch_shapes=[pltpu.SMEM(ghost_prefix.shape, jnp.int32), pltpu.VMEM((1, 1), jnp.int32)]
        + [pltpu.VMEM(a.shape, a.dtype) for a in arrays]
        + [
            pltpu.VMEM((SLOTS, ATOMS), F32),
            pltpu.VMEM((SLOTS, ATOMS), F32),
            pltpu.VMEM((CORNERS_AT, CH), F32),
            pltpu.VMEM((CORNERS_AT, CH), F32),
            pltpu.VMEM((COORDS, CH), F32),
            pltpu.VMEM((COORDS, CH), F32),
            pltpu.VMEM((CORNERS_AT, CH), F32),
            pltpu.VMEM((COORDS, CH), F32),
            pltpu.VMEM((ATOMS + 8, CH), F32),
            pltpu.VMEM((ATOMS, SLOTS), BF16),
            pltpu.SemaphoreType.DMA((2 + len(arrays),)),
            pltpu.SemaphoreType.DMA((12,)),
            pltpu.SemaphoreType.DMA((2,)),
        ],
        compiler_params=pltpu.CompilerParams(collective_id=0, has_side_effects=True, vmem_limit_bytes=VMEM),
        name="allegro",
    )(ghost_prefix, edge_fill.reshape(1, 1), *arrays)
    return pl.pallas_call(
        finish,
        out_shape=(
            jax.ShapeDtypeStruct((3, ATOMS), F32),
            jax.ShapeDtypeStruct((ATOMS, CH), F32),
        ),
        in_specs=[vmem] * 5,
        out_specs=(vmem, vmem),
        compiler_params=pltpu.CompilerParams(vmem_limit_bytes=VMEM),
        name="finish",
    )(back, coords, own, pick_t, weight_dst)


def solution(mesh):
    return jax.shard_map(
        body,
        mesh=mesh,
        in_specs=(
            P(("dom", "gz"), None),
            P(None, ("dom", "gz")),
            P(("dom", "gz"), None),
            P(("dom", "gz"), None),
            P(("dom", "gz")),
            P(("dom", "gz"), None),
            P(("dom", "gz"), None),
            P(),
            P(),
            P(),
            P(),
            P(),
            P(),
            P(),
        ),
        out_specs=(P(None, ("dom", "gz")), P(("dom", "gz"), None)),
        check_vma=False,
    )
```

```python
import math

import jax
import jax.numpy as jnp
import numpy as np
from jax import lax
from jax.experimental import pallas as pl
from jax.experimental.pallas import tpu as pltpu
from jax.sharding import PartitionSpec as P

NEIGHBOURS = 4
CAPS = (0, 64, 16, 4)
ROW_Y = 8

ATOMS = 128
EDGES = 512
CH = 128
SLOTS = 640
SHARPNESS = 8.0
VMEM = 56 * 1024 * 1024

BF16 = jnp.bfloat16
F32 = jnp.float32
MESH = pl.DeviceIdType.MESH


def directions():
    table = []
    offset = 0
    number = 0
    for a in (-1, 0, 1):
        for b in (-1, 0, 1):
            for c in (-1, 0, 1):
                kind = abs(a) + abs(b) + abs(c)
                if kind == 0:
                    continue
                cap = CAPS[kind]
                table.append(dict(vec=(a, b, c), kind=kind, cap=cap, number=number, offset=offset))
                offset += cap
                number += 1
    table.sort(key=lambda d: (d["kind"], d["number"]))
    slot = 0
    for step, d in enumerate(table):
        d["rows"] = {1: 64, 2: 16, 3: 8}[d["kind"]]
        d["slot"] = slot
        d["tile"] = 8 * step
        slot += d["rows"]
    assert slot == SLOTS
    return table


TABLE = directions()
FACES = [d for d in TABLE if d["kind"] == 1]
LINES = [d for d in TABLE if d["kind"] == 2]
CORNERS = [d for d in TABLE if d["kind"] == 3]
LINES_AT, CORNERS_AT = LINES[0]["slot"], CORNERS[0]["slot"]
COORDS = 8 * len(TABLE)
COORDS_SENT = 4 * len(TABLE) + 4 * len(CORNERS)


def mm(a, b):
    return lax.dot_general(a, b, (((1,), (0,)), ((), ())), preferred_element_type=F32)


def nt(a, b):
    return lax.dot_general(a, b, (((1,), (1,)), ((), ())), preferred_element_type=F32)


def tn(a, b):
    return lax.dot_general(a, b, (((0,), (0,)), ((), ())), preferred_element_type=F32)


def iota(shape, dim):
    return lax.broadcasted_iota(jnp.int32, shape, dim)


def onehot(cond):
    return jnp.where(cond, 1.0, 0.0).astype(BF16)


def split(x, pieces):
    out = []
    for step in range(pieces):
        part = x.astype(BF16)
        out.append(part)
        if step + 1 < pieces:
            x = x - part.astype(F32)
    return out


def split_rows(x, pieces):
    parts = []
    for step in range(pieces):
        part = x.astype(BF16).astype(F32)
        parts.append(part)
        x = x - part
    if pieces % 2:
        parts.append(jnp.zeros_like(x))
    return jnp.concatenate(parts, axis=0).astype(BF16)


def sum_pieces(x, pieces):
    total = x[0:8]
    for step in range(1, pieces):
        total = total + x[8 * step : 8 * step + 8]
    return total


def sigmoid(v):
    return 0.5 * jnp.tanh(0.5 * v) + 0.5


def silu_pair(v):
    v = v.astype(BF16)
    sig = sigmoid(v)
    value = v * sig
    return value, sig + value * (1 - sig)


def rows_to_eight(rows, first):
    place = iota((8, rows[0].shape[1]), 0)
    out = jnp.zeros((8, rows[0].shape[1]), F32)
    for step, row in enumerate(rows):
        out = jnp.where(place == first + step, row, out)
    return out


def slot_ids(dst_row):
    blocks = []
    for d in TABLE:
        if d["kind"] <= 2:
            place = iota((d["rows"], EDGES), 0) + (ATOMS + d["offset"])
            blocks.append(onehot(place == dst_row))
    place = iota((8 * len(CORNERS), EDGES), 0)
    inner = place % 8
    base = jnp.zeros_like(place)
    for step, d in enumerate(CORNERS):
        base = jnp.where(place // 8 == step, ATOMS - 4 + d["offset"], base)
    blocks.append(onehot((inner >= 4) & (base + inner == dst_row)))
    return jnp.concatenate(blocks, axis=0)


def side_by_side(x):
    rows = x.shape[0] // 3
    return jnp.concatenate([x[rows * step : rows * (step + 1)] for step in range(3)], axis=1)


def mixing(wenv, wlat):
    parts = [wlat[:CH]]
    for step in range(1, 4):
        parts.append(mm(wenv, wlat[CH * step : CH * (step + 1)]).astype(BF16))
    return parts


def geometry(pos_i, pos_j, in_fill, same):
    diff = pos_j - pos_i
    qx, qy, qz = diff[4:5], diff[5:6], diff[6:7]
    live = pos_j[7:8]
    rsq = qx * qx + qy * qy + qz * qz
    in_use = in_fill * live
    inside = jnp.where(rsq < 1.0, 1.0 - rsq, 0.0)
    env = inside * inside * in_use
    centers = iota((8, EDGES), 0).astype(F32) / 7.0
    offset = rsq - centers
    radial = jnp.exp(-SHARPNESS * offset * offset)

    r3, r15, r5 = math.sqrt(3.0), math.sqrt(15.0), math.sqrt(5.0)
    y1 = rows_to_eight([r3 * qx, r3 * qy, r3 * qz], 0)
    y2 = rows_to_eight(
        [
            r15 * qx * qy,
            r15 * qy * qz,
            r15 * qz * qx,
            0.5 * r15 * (qx * qx - qy * qy),
            0.5 * r5 * (2.0 * qz * qz - qx * qx - qy * qy),
        ],
        0,
    )
    h1, l1 = (part.astype(F32) for part in split(y1, 2))
    h2, l2 = (part.astype(F32) for part in split(y2, 2))
    zero8 = jnp.zeros((8, EDGES), F32)
    left1 = jnp.concatenate([h1, h1, l1, zero8], axis=0).astype(BF16)
    right1 = jnp.concatenate([h1, l1, h1, zero8], axis=0).astype(BF16)
    left2 = jnp.concatenate([h2, h2, l2, zero8], axis=0).astype(BF16)
    right2 = jnp.concatenate([h2, l2, h2, zero8], axis=0).astype(BF16)
    k1 = tn(left1, right1).astype(BF16) * same
    k2 = tn(left2, right2).astype(BF16) * same

    return dict(
        q=(qx, qy, qz),
        in_use=in_use,
        inside=inside,
        env=env,
        offset=offset,
        radial=radial,
        left1=left1,
        left2=left2,
        kernels=jnp.concatenate([same, k1, k2], axis=0),
    )


def edge_pass(pre, geo, w):
    env, kernels = geo["env"], geo["kernels"]
    env16 = env.astype(BF16)
    act, dact = silu_pair(pre)
    latent = act * env16
    mixed = mm(w["mix_t"], latent)
    near_far = mixed[CH:].astype(BF16)
    upd_act, upd_d = silu_pair(mixed[:CH] + mm(side_by_side(near_far), kernels))
    hid_act, hid_d = silu_pair(mm(w["hid_t"], latent + upd_act))
    dhid = hid_d * (w["ro"] * env).astype(BF16)
    dupdated = mm(w["hid"], dhid)
    dupd = dupdated.astype(BF16) * upd_d
    dmixed = mm(w["mix"], dupd)
    dlatent = dupdated + dmixed[:CH] + mm(side_by_side(dmixed[CH:].astype(BF16)), kernels)
    dpre = (dlatent * env).astype(BF16) * dact
    b1, b2 = near_far[CH : 2 * CH], near_far[2 * CH :]
    dupd_t = dupd.T
    pairs = [
        (jnp.concatenate([dupd_t, b.T], axis=1), jnp.concatenate([b, dupd], axis=0)) for b in (b1, b2)
    ]
    return dpre, (dlatent, act, hid_act, pairs)


def slot_ids_across(dst_row):
    dst = jnp.broadcast_to(dst_row.astype(F32), (128, EDGES)).T
    blocks = []
    for tile in range(SLOTS // 128):
        lane = iota((8, 128), 1)
        ids = jnp.full((8, 128), -1, jnp.int32)
        for d in TABLE:
            if d["slot"] // 128 == tile:
                low = d["slot"] % 128 + (4 if d["kind"] == 3 else 0)
                mine = (lane >= low) & (lane < low + d["cap"])
                ids = jnp.where(mine, lane + (ATOMS + d["offset"] - low), ids)
        blocks.append(onehot(dst == ids.astype(F32)[0:1]))
    return jnp.concatenate(blocks, axis=1)


def edge_coords(dpre, kept, geo, same, w):
    dlatent, act, hid_act, pairs = kept
    r3, r15, r5 = math.sqrt(3.0), math.sqrt(15.0), math.sqrt(5.0)
    qx, qy, qz = geo["q"]
    denv = jnp.sum(hid_act * w["ro"] + dlatent * act, axis=0, keepdims=True)
    t1, t2 = (mm(*pair).astype(BF16) * same for pair in pairs)
    dy1 = mm(geo["left1"], t1)
    dy1 = dy1[0:8] + dy1[16:24]
    dy2 = mm(geo["left2"], t2)
    dy2 = dy2[0:8] + dy2[16:24]

    drad = mm(w["rad"], dpre)
    drsq = jnp.sum(drad * geo["radial"] * geo["offset"], axis=0, keepdims=True) * (-2.0 * SHARPNESS)
    drsq = drsq - 2.0 * denv * geo["in_use"] * geo["inside"]
    a0, a1, a2, a3, a4 = (dy2[step : step + 1] for step in range(5))
    two = 2.0 * drsq
    gx = two * qx + r3 * dy1[0:1] + r15 * (a0 * qy + a2 * qz + a3 * qx) - r5 * a4 * qx
    gy = two * qy + r3 * dy1[1:2] + r15 * (a0 * qx + a1 * qz - a3 * qy) - r5 * a4 * qy
    gz = two * qz + r3 * dy1[2:3] + r15 * (a1 * qy + a2 * qx) + 2.0 * r5 * a4 * qz
    return rows_to_eight([gx, gy, gz], 4)


def corner_lines(ref):
    tiles = ref[CORNERS[0]["tile"] :, :]
    return jnp.where(iota(tiles.shape, 0) % 8 >= 4, tiles, 0.0).astype(BF16)


def unpack_coords(ref):
    tiles = [None] * (SLOTS // 128)
    for d in TABLE:
        tile = d["slot"] // 128
        piece = ref[d["tile"] : d["tile"] + 4, :]
        tiles[tile] = piece if tiles[tile] is None else tiles[tile] + piece
    coords = jnp.concatenate(tiles, axis=1)
    return jnp.concatenate([jnp.zeros_like(coords), coords], axis=0)


def kernel(
    prefix_hbm,
    fill_hbm,
    feat_hbm,
    pos_hbm,
    send_hbm,
    src_hbm,
    dst_hbm,
    wsrc_hbm,
    wdst_hbm,
    wrad_hbm,
    wenv_hbm,
    wlat_hbm,
    whid_hbm,
    wro_hbm,
    in2,
    coords_in2,
    own_hbm,
    pick_hbm,
    prefix,
    fill,
    feat_v,
    pos_v,
    send_v,
    src_v,
    dst_v,
    wsrc_v,
    wdst_v,
    wrad_v,
    wenv_v,
    wlat_v,
    whid_v,
    wro_v,
    list_v,
    pick_v,
    out1,
    in1,
    coords_out1,
    coords_in1,
    out2,
    coords_out2,
    own_v,
    pick_t_v,
    in_sem,
    sems,
    out_sem,
):
    planes = lax.axis_size("dom") // ROW_Y
    depth = lax.axis_size("gz")
    dom = lax.axis_index("dom")
    cz = lax.axis_index("gz")
    cx, cy = lax.div(dom, ROW_Y), lax.rem(dom, ROW_Y)
    along_x = {step: lax.rem(cx + (step + planes), planes) * ROW_Y for step in (-1, 0, 1)}
    along_y = {step: lax.rem(cy + (step + ROW_Y), ROW_Y) for step in (-1, 0, 1)}
    along_z = {step: lax.rem(cz + (step + depth), depth) for step in (-1, 0, 1)}

    def place(vec, sign):
        return (along_x[sign * vec[0]] + along_y[sign * vec[1]], along_z[sign * vec[2]])

    loads = []
    for step, (source, target) in enumerate(
        [
            (send_hbm, send_v),
            (prefix_hbm, prefix),
            (feat_hbm, feat_v),
            (pos_hbm, pos_v),
            (src_hbm, src_v),
            (dst_hbm, dst_v),
            (wsrc_hbm, wsrc_v),
            (wdst_hbm, wdst_v),
            (wrad_hbm, wrad_v),
            (wenv_hbm, wenv_v),
            (wlat_hbm, wlat_v),
            (whid_hbm, whid_v),
            (wro_hbm, wro_v),
            (fill_hbm, fill),
        ]
    ):
        copy = pltpu.make_async_copy(source, target, in_sem.at[step])
        copy.start()
        loads.append(copy)

    barrier = pltpu.get_barrier_semaphore()
    for d in TABLE:
        pl.semaphore_signal(barrier, inc=1, device_id=place(d["vec"], 1), device_id_type=MESH)

    loads[0].wait()
    listed = jnp.where(iota((ATOMS, 608), 0) == send_v[...], 1.0, 0.0)
    list_v[0:608, :] = listed.T
    list_v[608:640, :] = jnp.zeros((32, ATOMS), F32)
    loads[1].wait()
    loads[2].wait()
    loads[3].wait()
    feat16 = feat_v[...].astype(BF16)
    pos = pos_v[...]
    own8 = rows_to_eight([pos[0:1], pos[1:2], pos[2:3], jnp.ones((1, ATOMS), F32)], 4)
    own_pieces = split_rows(own8, 3)
    lane = iota((8, 128), 1)
    line = iota((8, 128), 0)

    def store_coords(ref, slots, corners, shifted):
        for d in TABLE:
            tile, low = d["slot"] // 128 * 128, d["slot"] % 128
            inside = (lane >= low) & (lane < low + d["rows"])
            coords = slots[:, tile : tile + 128]
            if shifted:
                shift = jnp.zeros((8, 128), F32)
                for step in range(3):
                    if d["vec"][step]:
                        shift = jnp.where(line == 4 + step, float(d["vec"][step]), shift)
                coords = coords - shift
            coords = jnp.where(inside, coords, 0.0)[4:8]
            if d["kind"] == 3:
                first = d["slot"] - CORNERS_AT
                coords = jnp.concatenate([coords, corners[first + 4 : first + 8]], axis=0)
            ref[d["tile"] : d["tile"] + coords.shape[0], :] = coords

    def remote(source, target, start, size, pair, vec, sign):
        rows = pl.ds(start, size)
        return pltpu.make_async_remote_copy(
            src_ref=source.at[rows],
            dst_ref=target.at[rows],
            send_sem=sems.at[pair],
            recv_sem=sems.at[pair + 1],
            device_id=place(vec, sign),
            device_id_type=MESH,
        )

    def send_lines(table, source, target, pair, sign):
        for d in table:
            remote(source, target, d["slot"], d["rows"], pair, d["vec"], sign).start()

    def send_coords(source, target, pair, sign):
        for d in TABLE[::-1]:
            remote(source, target, d["tile"], 8 if d["kind"] == 3 else 4, pair, d["vec"], sign).start()

    def lines_of(source, target, pair, first, last):
        return remote(source, target, first, last - first, pair, TABLE[0]["vec"], 1)

    def coords_of(source, target, pair):
        return remote(source, target, 0, COORDS_SENT, pair, TABLE[0]["vec"], 1)

    for d in TABLE:
        n, rows = d["number"], d["rows"]
        count = prefix[0, n + 1] - prefix[0, n]
        lines = list_v[pl.ds(prefix[0, n], rows), :]
        lines = jnp.where(iota((rows, ATOMS), 0) < count, lines, 0.0)
        if d["kind"] == 3:
            lines = jnp.concatenate([jnp.zeros((4, ATOMS), F32), lines[:4]], axis=0)
        pick_v[d["slot"] : d["slot"] + rows, :] = lines
    pick = pick_v[...].astype(BF16)
    packed = mm(pick, feat16)
    store_coords(coords_out1, sum_pieces(nt(own_pieces, pick), 3), packed[CORNERS_AT:], True)
    out1[...] = packed[:CORNERS_AT]
    pl.semaphore_wait(barrier, len(TABLE))
    send_coords(coords_out1, coords_in1, 0, 1)
    send_lines(LINES, out1, in1, 2, 1)
    send_lines(FACES, out1, in1, 4, 1)

    for copy in loads[4:]:
        copy.wait()
    src_row, dst_row = src_v[...], dst_v[...]
    centre = onehot(iota((ATOMS, EDGES), 0) == src_row)
    near = onehot(iota((ATOMS, EDGES), 0) == dst_row)
    ghost = slot_ids(dst_row)
    ghost_t = slot_ids_across(dst_row)
    same = (tn(centre, centre) * (1.0 / NEIGHBOURS)).astype(BF16)
    in_fill = jnp.where(iota((1, EDGES), 1) < fill[...], 1.0, 0.0)
    eye = iota((CH, CH), 0) == iota((CH, CH), 1)
    mix = mixing(wenv_v[...], wlat_v[...])
    w = dict(
        dst_t=wdst_v[...].T,
        rad_t=wrad_v[...].T,
        mix=jnp.concatenate(mix, axis=0),
        mix_t=jnp.concatenate([part.T for part in mix], axis=0),
        hid_t=whid_v[...].T,
        rad=wrad_v[...],
        hid=whid_v[...],
        ro=jnp.sum(jnp.where(eye, wro_v[...], 0.0), axis=1, keepdims=True),
    )
    feat_t = feat16.T
    own_lhs = jnp.concatenate([feat_t, own_pieces], axis=0)
    at_i = mm(own_lhs, centre)
    at_j = mm(own_lhs, near)
    pre_own = mm(wsrc_v[...].T, at_i[:CH].astype(BF16)) + mm(w["dst_t"], at_j[:CH].astype(BF16))
    pos_i = sum_pieces(at_i[CH:], 3)
    pos_j_own = sum_pieces(at_j[CH:], 3)
    pick_t_v[...] = pick.T
    pick_out = pltpu.make_async_copy(pick_t_v, pick_hbm, out_sem.at[0])
    pick_out.start()

    coords_of(coords_out1, coords_in1, 0).wait_recv()
    pos_g = mm(split_rows(unpack_coords(coords_in1), 3), ghost)
    geo = geometry(pos_i, pos_j_own + sum_pieces(pos_g, 3), in_fill, same)

    pre_known = pre_own + mm(w["rad_t"], geo["radial"].astype(BF16))

    lines_of(out1, in1, 2, LINES_AT, CORNERS_AT).wait_recv()
    some = jnp.concatenate([in1[LINES_AT:, :].astype(BF16), corner_lines(coords_in1)], axis=0)
    pre_known = pre_known + mm(nt(w["dst_t"], some).astype(BF16), ghost[LINES_AT:])
    lines_of(out1, in1, 4, 0, LINES_AT).wait_recv()
    far = nt(w["dst_t"], in1[0:LINES_AT, :].astype(BF16)).astype(BF16)
    dpre, kept = edge_pass(pre_known + mm(far, ghost[:LINES_AT]), geo, w)

    some = nt(ghost[LINES_AT:], dpre)
    out2[LINES_AT:, :] = some[: CORNERS_AT - LINES_AT]
    send_lines(LINES, out2, in2, 6, -1)
    out2[0:LINES_AT, :] = nt(ghost[:LINES_AT], dpre)
    send_lines(FACES, out2, in2, 8, -1)
    dq_pieces = split_rows(edge_coords(dpre, kept, geo, same, w), 2)
    store_coords(coords_out2, sum_pieces(mm(dq_pieces, ghost_t), 2), some[CORNERS_AT - LINES_AT :], False)
    send_coords(coords_out2, coords_in2, 10, -1)

    own = nt(jnp.concatenate([centre, near], axis=0), dpre).astype(BF16)
    own_v[0:ATOMS, :] = nt(own[:ATOMS], wsrc_v[...]) + nt(own[ATOMS:], wdst_v[...])
    own_v[ATOMS:, :] = sum_pieces(nt(dq_pieces, near - centre), 2)
    own_out = pltpu.make_async_copy(own_v, own_hbm, out_sem.at[1])
    own_out.start()

    pick_out.wait()
    own_out.wait()
    coords_of(coords_out1, coords_in1, 0).wait_send()
    for pair, first, last in ((2, LINES_AT, CORNERS_AT), (4, 0, LINES_AT)):
        lines_of(out1, in1, pair, first, last).wait_send()
        lines_of(out2, in2, pair + 4, first, last).wait()
    coords_of(coords_out2, coords_in2, 10).wait()


def finish(back_ref, coords_ref, own_ref, pick_ref, wdst_ref, force_ref, grad_ref):
    pick_t = pick_ref[...]
    lines = jnp.concatenate([back_ref[...].astype(BF16), corner_lines(coords_ref)], axis=0)
    returned = mm(pick_t, lines).astype(BF16)
    grad_ref[...] = own_ref[0:ATOMS, :] + nt(returned, wdst_ref[...])
    total8 = own_ref[ATOMS:, :] + sum_pieces(nt(split_rows(unpack_coords(coords_ref), 2), pick_t), 2)
    force_ref[...] = -total8[4:7]


def body(
    features,
    positions,
    send_ids,
    ghost_prefix,
    edge_fill,
    edge_src,
    edge_dst,
    weight_src,
    weight_dst,
    weight_radial,
    weight_env,
    weight_latent,
    weight_hidden,
    weight_readout,
):
    arrays = [
        features,
        positions,
        send_ids,
        edge_src,
        edge_dst,
        weight_src,
        weight_dst,
        weight_radial,
        weight_env,
        weight_latent,
        weight_hidden,
        weight_readout.reshape(1, CH),
    ]
    hbm = pl.BlockSpec(memory_space=pltpu.HBM)
    vmem = pl.BlockSpec(memory_space=pltpu.VMEM)
    back, coords, own, pick_t = pl.pallas_call(
        kernel,
        out_shape=(
            jax.ShapeDtypeStruct((CORNERS_AT, CH), F32),
            jax.ShapeDtypeStruct((COORDS, CH), F32),
            jax.ShapeDtypeStruct((ATOMS + 8, CH), F32),
            jax.ShapeDtypeStruct((ATOMS, SLOTS), BF16),
        ),
        in_specs=[hbm] * (2 + len(arrays)),
        out_specs=(hbm, hbm, hbm, hbm),
        scratch_shapes=[pltpu.SMEM(ghost_prefix.shape, jnp.int32), pltpu.VMEM((1, 1), jnp.int32)]
        + [pltpu.VMEM(a.shape, a.dtype) for a in arrays]
        + [
            pltpu.VMEM((SLOTS, ATOMS), F32),
            pltpu.VMEM((SLOTS, ATOMS), F32),
            pltpu.VMEM((CORNERS_AT, CH), F32),
            pltpu.VMEM((CORNERS_AT, CH), F32),
            pltpu.VMEM((COORDS, CH), F32),
            pltpu.VMEM((COORDS, CH), F32),
            pltpu.VMEM((CORNERS_AT, CH), F32),
            pltpu.VMEM((COORDS, CH), F32),
            pltpu.VMEM((ATOMS + 8, CH), F32),
            pltpu.VMEM((ATOMS, SLOTS), BF16),
            pltpu.SemaphoreType.DMA((2 + len(arrays),)),
            pltpu.SemaphoreType.DMA((12,)),
            pltpu.SemaphoreType.DMA((2,)),
        ],
        compiler_params=pltpu.CompilerParams(collective_id=0, has_side_effects=True, vmem_limit_bytes=VMEM),
        name="allegro",
    )(ghost_prefix, edge_fill.reshape(1, 1), *arrays)
    return pl.pallas_call(
        finish,
        out_shape=(
            jax.ShapeDtypeStruct((3, ATOMS), F32),
            jax.ShapeDtypeStruct((ATOMS, CH), F32),
        ),
        in_specs=[vmem] * 5,
        out_specs=(vmem, vmem),
        compiler_params=pltpu.CompilerParams(vmem_limit_bytes=VMEM),
        name="finish",
    )(back, coords, own, pick_t, weight_dst)


def solution(mesh):
    return jax.shard_map(
        body,
        mesh=mesh,
        in_specs=(
            P(("dom", "gz"), None),
            P(None, ("dom", "gz")),
            P(("dom", "gz"), None),
            P(("dom", "gz"), None),
            P(("dom", "gz")),
            P(("dom", "gz"), None),
            P(("dom", "gz"), None),
            P(),
            P(),
            P(),
            P(),
            P(),
            P(),
            P(),
        ),
        out_specs=(P(None, ("dom", "gz")), P(("dom", "gz"), None)),
        check_vma=False,
    )
```

```python
import math

import jax
import jax.numpy as jnp
import numpy as np
from jax import lax
from jax.experimental import pallas as pl
from jax.experimental.pallas import tpu as pltpu
from jax.sharding import PartitionSpec as P

NEIGHBOURS = 4
CAPS = (0, 64, 16, 4)
ROW_Y = 8

ATOMS = 128
EDGES = 512
CH = 128
SLOTS = 640
SHARPNESS = 8.0
VMEM = 56 * 1024 * 1024

BF16 = jnp.bfloat16
F32 = jnp.float32
MESH = pl.DeviceIdType.MESH


def directions():
    table = []
    offset = 0
    number = 0
    for a in (-1, 0, 1):
        for b in (-1, 0, 1):
            for c in (-1, 0, 1):
                kind = abs(a) + abs(b) + abs(c)
                if kind == 0:
                    continue
                cap = CAPS[kind]
                table.append(dict(vec=(a, b, c), kind=kind, cap=cap, number=number, offset=offset))
                offset += cap
                number += 1
    table.sort(key=lambda d: (d["kind"], d["number"]))
    slot = 0
    for step, d in enumerate(table):
        d["rows"] = {1: 64, 2: 16, 3: 8}[d["kind"]]
        d["slot"] = slot
        d["tile"] = 8 * step
        slot += d["rows"]
    assert slot == SLOTS
    return table


TABLE = directions()
FACES = [d for d in TABLE if d["kind"] == 1]
LINES = [d for d in TABLE if d["kind"] == 2]
CORNERS = [d for d in TABLE if d["kind"] == 3]
ORDER = sorted(TABLE, key=lambda d: (-d["kind"], d["vec"][2] == 0))
LINES_AT, CORNERS_AT = LINES[0]["slot"], CORNERS[0]["slot"]
COORDS = 8 * len(TABLE)
COORDS_SENT = 4 * len(TABLE) + 4 * len(CORNERS)


def mm(a, b):
    return lax.dot_general(a, b, (((1,), (0,)), ((), ())), preferred_element_type=F32)


def nt(a, b):
    return lax.dot_general(a, b, (((1,), (1,)), ((), ())), preferred_element_type=F32)


def tn(a, b):
    return lax.dot_general(a, b, (((0,), (0,)), ((), ())), preferred_element_type=F32)


def iota(shape, dim):
    return lax.broadcasted_iota(jnp.int32, shape, dim)


def onehot(cond):
    return jnp.where(cond, 1.0, 0.0).astype(BF16)


def split(x, pieces):
    out = []
    for step in range(pieces):
        part = x.astype(BF16)
        out.append(part)
        if step + 1 < pieces:
            x = x - part.astype(F32)
    return out


def split_rows(x, pieces):
    parts = []
    for step in range(pieces):
        part = x.astype(BF16).astype(F32)
        parts.append(part)
        x = x - part
    if pieces % 2:
        parts.append(jnp.zeros_like(x))
    return jnp.concatenate(parts, axis=0).astype(BF16)


def sum_pieces(x, pieces):
    total = x[0:8]
    for step in range(1, pieces):
        total = total + x[8 * step : 8 * step + 8]
    return total


def sigmoid(v):
    return 0.5 * jnp.tanh(0.5 * v) + 0.5


def silu_pair(v):
    v = v.astype(BF16)
    sig = sigmoid(v)
    value = v * sig
    return value, sig + value * (1 - sig)


def rows_to_eight(rows, first):
    place = iota((8, rows[0].shape[1]), 0)
    out = jnp.zeros((8, rows[0].shape[1]), F32)
    for step, row in enumerate(rows):
        out = jnp.where(place == first + step, row, out)
    return out


def slot_ids(dst_row):
    blocks = []
    for d in TABLE:
        if d["kind"] <= 2:
            place = iota((d["rows"], EDGES), 0) + (ATOMS + d["offset"])
            blocks.append(onehot(place == dst_row))
    place = iota((8 * len(CORNERS), EDGES), 0)
    inner = place % 8
    base = jnp.zeros_like(place)
    for step, d in enumerate(CORNERS):
        base = jnp.where(place // 8 == step, ATOMS - 4 + d["offset"], base)
    blocks.append(onehot((inner >= 4) & (base + inner == dst_row)))
    return jnp.concatenate(blocks, axis=0)


def side_by_side(x):
    rows = x.shape[0] // 3
    return jnp.concatenate([x[rows * step : rows * (step + 1)] for step in range(3)], axis=1)


def mixing(wenv, wlat):
    parts = [wlat[:CH]]
    for step in range(1, 4):
        parts.append(mm(wenv, wlat[CH * step : CH * (step + 1)]).astype(BF16))
    return parts


def geometry(pos_i, pos_j, in_fill, same):
    diff = pos_j - pos_i
    qx, qy, qz = diff[4:5], diff[5:6], diff[6:7]
    live = pos_j[7:8]
    rsq = qx * qx + qy * qy + qz * qz
    in_use = in_fill * live
    inside = jnp.where(rsq < 1.0, 1.0 - rsq, 0.0)
    env = inside * inside * in_use
    centers = iota((8, EDGES), 0).astype(F32) / 7.0
    offset = rsq - centers
    radial = jnp.exp(-SHARPNESS * offset * offset)

    r3, r15, r5 = math.sqrt(3.0), math.sqrt(15.0), math.sqrt(5.0)
    y1 = rows_to_eight([r3 * qx, r3 * qy, r3 * qz], 0)
    y2 = rows_to_eight(
        [
            r15 * qx * qy,
            r15 * qy * qz,
            r15 * qz * qx,
            0.5 * r15 * (qx * qx - qy * qy),
            0.5 * r5 * (2.0 * qz * qz - qx * qx - qy * qy),
        ],
        0,
    )
    h1, l1 = (part.astype(F32) for part in split(y1, 2))
    h2, l2 = (part.astype(F32) for part in split(y2, 2))
    zero8 = jnp.zeros((8, EDGES), F32)
    left1 = jnp.concatenate([h1, h1, l1, zero8], axis=0).astype(BF16)
    right1 = jnp.concatenate([h1, l1, h1, zero8], axis=0).astype(BF16)
    left2 = jnp.concatenate([h2, h2, l2, zero8], axis=0).astype(BF16)
    right2 = jnp.concatenate([h2, l2, h2, zero8], axis=0).astype(BF16)
    k1 = tn(left1, right1).astype(BF16) * same
    k2 = tn(left2, right2).astype(BF16) * same

    return dict(
        q=(qx, qy, qz),
        in_use=in_use,
        inside=inside,
        env=env,
        offset=offset,
        radial=radial,
        left1=left1,
        left2=left2,
        kernels=jnp.concatenate([same, k1, k2], axis=0),
    )


def edge_pass(pre, geo, w):
    env, kernels = geo["env"], geo["kernels"]
    env16 = env.astype(BF16)
    act, dact = silu_pair(pre)
    latent = act * env16
    mixed = mm(w["mix_t"], latent)
    near_far = mixed[CH:].astype(BF16)
    upd_act, upd_d = silu_pair(mixed[:CH] + mm(side_by_side(near_far), kernels))
    hid_act, hid_d = silu_pair(mm(w["hid_t"], latent + upd_act))
    dhid = hid_d * (w["ro"] * env).astype(BF16)
    dupdated = mm(w["hid"], dhid)
    dupd = dupdated.astype(BF16) * upd_d
    dmixed = mm(w["mix"], dupd)
    dlatent = dupdated + dmixed[:CH] + mm(side_by_side(dmixed[CH:].astype(BF16)), kernels)
    dpre = (dlatent * env).astype(BF16) * dact
    b1, b2 = near_far[CH : 2 * CH], near_far[2 * CH :]
    dupd_t = dupd.T
    pairs = [
        (jnp.concatenate([dupd_t, b.T], axis=1), jnp.concatenate([b, dupd], axis=0)) for b in (b1, b2)
    ]
    return dpre, (dlatent, act, hid_act, pairs)


def slot_ids_across(dst_row):
    dst = jnp.broadcast_to(dst_row.astype(F32), (128, EDGES)).T
    blocks = []
    for tile in range(SLOTS // 128):
        lane = iota((8, 128), 1)
        ids = jnp.full((8, 128), -1, jnp.int32)
        for d in TABLE:
            if d["slot"] // 128 == tile:
                low = d["slot"] % 128 + (4 if d["kind"] == 3 else 0)
                mine = (lane >= low) & (lane < low + d["cap"])
                ids = jnp.where(mine, lane + (ATOMS + d["offset"] - low), ids)
        blocks.append(onehot(dst == ids.astype(F32)[0:1]))
    return jnp.concatenate(blocks, axis=1)


def edge_coords(dpre, kept, geo, same, w):
    dlatent, act, hid_act, pairs = kept
    r3, r15, r5 = math.sqrt(3.0), math.sqrt(15.0), math.sqrt(5.0)
    qx, qy, qz = geo["q"]
    denv = jnp.sum(hid_act * w["ro"] + dlatent * act, axis=0, keepdims=True)
    t1, t2 = (mm(*pair).astype(BF16) * same for pair in pairs)
    dy1 = mm(geo["left1"], t1)
    dy1 = dy1[0:8] + dy1[16:24]
    dy2 = mm(geo["left2"], t2)
    dy2 = dy2[0:8] + dy2[16:24]

    drad = mm(w["rad"], dpre)
    drsq = jnp.sum(drad * geo["radial"] * geo["offset"], axis=0, keepdims=True) * (-2.0 * SHARPNESS)
    drsq = drsq - 2.0 * denv * geo["in_use"] * geo["inside"]
    a0, a1, a2, a3, a4 = (dy2[step : step + 1] for step in range(5))
    two = 2.0 * drsq
    gx = two * qx + r3 * dy1[0:1] + r15 * (a0 * qy + a2 * qz + a3 * qx) - r5 * a4 * qx
    gy = two * qy + r3 * dy1[1:2] + r15 * (a0 * qx + a1 * qz - a3 * qy) - r5 * a4 * qy
    gz = two * qz + r3 * dy1[2:3] + r15 * (a1 * qy + a2 * qx) + 2.0 * r5 * a4 * qz
    return rows_to_eight([gx, gy, gz], 4)


def corner_lines(ref):
    tiles = ref[CORNERS[0]["tile"] :, :]
    return jnp.where(iota(tiles.shape, 0) % 8 >= 4, tiles, 0.0).astype(BF16)


def unpack_coords(ref):
    tiles = [None] * (SLOTS // 128)
    for d in TABLE:
        tile = d["slot"] // 128
        piece = ref[d["tile"] : d["tile"] + 4, :]
        tiles[tile] = piece if tiles[tile] is None else tiles[tile] + piece
    coords = jnp.concatenate(tiles, axis=1)
    return jnp.concatenate([jnp.zeros_like(coords), coords], axis=0)


def kernel(
    prefix_hbm,
    fill_hbm,
    feat_hbm,
    pos_hbm,
    send_hbm,
    src_hbm,
    dst_hbm,
    wsrc_hbm,
    wdst_hbm,
    wrad_hbm,
    wenv_hbm,
    wlat_hbm,
    whid_hbm,
    wro_hbm,
    in2,
    coords_in2,
    own_hbm,
    pick_hbm,
    prefix,
    fill,
    feat_v,
    pos_v,
    send_v,
    src_v,
    dst_v,
    wsrc_v,
    wdst_v,
    wrad_v,
    wenv_v,
    wlat_v,
    whid_v,
    wro_v,
    list_v,
    pick_v,
    out1,
    in1,
    coords_out1,
    coords_in1,
    out2,
    coords_out2,
    own_v,
    pick_t_v,
    in_sem,
    sems,
    out_sem,
):
    planes = lax.axis_size("dom") // ROW_Y
    depth = lax.axis_size("gz")
    dom = lax.axis_index("dom")
    cz = lax.axis_index("gz")
    cx, cy = lax.div(dom, ROW_Y), lax.rem(dom, ROW_Y)
    along_x = {step: lax.rem(cx + (step + planes), planes) * ROW_Y for step in (-1, 0, 1)}
    along_y = {step: lax.rem(cy + (step + ROW_Y), ROW_Y) for step in (-1, 0, 1)}
    along_z = {step: lax.rem(cz + (step + depth), depth) for step in (-1, 0, 1)}

    def place(vec, sign):
        return (along_x[sign * vec[0]] + along_y[sign * vec[1]], along_z[sign * vec[2]])

    loads = []
    for step, (source, target) in enumerate(
        [
            (send_hbm, send_v),
            (prefix_hbm, prefix),
            (feat_hbm, feat_v),
            (pos_hbm, pos_v),
            (src_hbm, src_v),
            (dst_hbm, dst_v),
            (wsrc_hbm, wsrc_v),
            (wdst_hbm, wdst_v),
            (wrad_hbm, wrad_v),
            (wenv_hbm, wenv_v),
            (wlat_hbm, wlat_v),
            (whid_hbm, whid_v),
            (wro_hbm, wro_v),
            (fill_hbm, fill),
        ]
    ):
        copy = pltpu.make_async_copy(source, target, in_sem.at[step])
        loads.append(copy)

    barrier = pltpu.get_barrier_semaphore()
    for copy in loads[:4]:
        copy.start()
    for d in ORDER:
        pl.semaphore_signal(barrier, inc=1, device_id=place(d["vec"], 1), device_id_type=MESH)
    for copy in loads[4:]:
        copy.start()

    loads[0].wait()
    listed = jnp.where(iota((ATOMS, 608), 0) == send_v[...], 1.0, 0.0)
    list_v[0:608, :] = listed.T
    list_v[608:640, :] = jnp.zeros((32, ATOMS), F32)
    loads[1].wait()
    loads[2].wait()
    loads[3].wait()
    feat16 = feat_v[...].astype(BF16)
    pos = pos_v[...]
    own8 = rows_to_eight([pos[0:1], pos[1:2], pos[2:3], jnp.ones((1, ATOMS), F32)], 4)
    own_pieces = split_rows(own8, 3)
    lane = iota((8, 128), 1)
    line = iota((8, 128), 0)

    def store_coords(ref, slots, corners, shifted):
        for d in TABLE:
            tile, low = d["slot"] // 128 * 128, d["slot"] % 128
            inside = (lane >= low) & (lane < low + d["rows"])
            coords = slots[:, tile : tile + 128]
            if shifted:
                shift = jnp.zeros((8, 128), F32)
                for step in range(3):
                    if d["vec"][step]:
                        shift = jnp.where(line == 4 + step, float(d["vec"][step]), shift)
                coords = coords - shift
            coords = jnp.where(inside, coords, 0.0)[4:8]
            if d["kind"] == 3:
                first = d["slot"] - CORNERS_AT
                coords = jnp.concatenate([coords, corners[first + 4 : first + 8]], axis=0)
            ref[d["tile"] : d["tile"] + coords.shape[0], :] = coords

    def remote(source, target, start, size, pair, vec, sign):
        rows = pl.ds(start, size)
        return pltpu.make_async_remote_copy(
            src_ref=source.at[rows],
            dst_ref=target.at[rows],
            send_sem=sems.at[pair],
            recv_sem=sems.at[pair + 1],
            device_id=place(vec, sign),
            device_id_type=MESH,
        )

    def send_lines(table, source, target, pair, sign):
        for d in ORDER:
            if d not in table:
                continue
            remote(source, target, d["slot"], d["rows"], pair, d["vec"], sign).start()

    def send_coords(source, target, pair, sign):
        for d in ORDER:
            remote(source, target, d["tile"], 8 if d["kind"] == 3 else 4, pair, d["vec"], sign).start()

    def lines_of(source, target, pair, first, last):
        return remote(source, target, first, last - first, pair, TABLE[0]["vec"], 1)

    def coords_of(source, target, pair):
        return remote(source, target, 0, COORDS_SENT, pair, TABLE[0]["vec"], 1)

    for d in TABLE:
        n, rows = d["number"], d["rows"]
        count = prefix[0, n + 1] - prefix[0, n]
        lines = list_v[pl.ds(prefix[0, n], rows), :]
        lines = jnp.where(iota((rows, ATOMS), 0) < count, lines, 0.0)
        if d["kind"] == 3:
            lines = jnp.concatenate([jnp.zeros((4, ATOMS), F32), lines[:4]], axis=0)
        pick_v[d["slot"] : d["slot"] + rows, :] = lines
    pick = pick_v[...].astype(BF16)
    packed = mm(pick, feat16)
    store_coords(coords_out1, sum_pieces(nt(own_pieces, pick), 3), packed[CORNERS_AT:], True)
    out1[...] = packed[:CORNERS_AT]
    pl.semaphore_wait(barrier, len(TABLE))
    send_coords(coords_out1, coords_in1, 0, 1)
    send_lines(LINES, out1, in1, 2, 1)
    send_lines(FACES, out1, in1, 4, 1)

    for copy in loads[4:]:
        copy.wait()
    src_row, dst_row = src_v[...], dst_v[...]
    centre = onehot(iota((ATOMS, EDGES), 0) == src_row)
    near = onehot(iota((ATOMS, EDGES), 0) == dst_row)
    ghost = slot_ids(dst_row)
    ghost_t = slot_ids_across(dst_row)
    same = (tn(centre, centre) * (1.0 / NEIGHBOURS)).astype(BF16)
    in_fill = jnp.where(iota((1, EDGES), 1) < fill[...], 1.0, 0.0)
    eye = iota((CH, CH), 0) == iota((CH, CH), 1)
    mix = mixing(wenv_v[...], wlat_v[...])
    w = dict(
        dst_t=wdst_v[...].T,
        rad_t=wrad_v[...].T,
        mix=jnp.concatenate(mix, axis=0),
        mix_t=jnp.concatenate([part.T for part in mix], axis=0),
        hid_t=whid_v[...].T,
        rad=wrad_v[...],
        hid=whid_v[...],
        ro=jnp.sum(jnp.where(eye, wro_v[...], 0.0), axis=1, keepdims=True),
    )
    feat_t = feat16.T
    own_lhs = jnp.concatenate([feat_t, own_pieces], axis=0)
    at_i = mm(own_lhs, centre)
    at_j = mm(own_lhs, near)
    pre_own = mm(wsrc_v[...].T, at_i[:CH].astype(BF16)) + mm(w["dst_t"], at_j[:CH].astype(BF16))
    pos_i = sum_pieces(at_i[CH:], 3)
    pos_j_own = sum_pieces(at_j[CH:], 3)
    pick_t_v[...] = pick.T
    pick_out = pltpu.make_async_copy(pick_t_v, pick_hbm, out_sem.at[0])
    pick_out.start()

    coords_of(coords_out1, coords_in1, 0).wait_recv()
    pos_g = mm(split_rows(unpack_coords(coords_in1), 3), ghost)
    geo = geometry(pos_i, pos_j_own + sum_pieces(pos_g, 3), in_fill, same)

    pre_known = pre_own + mm(w["rad_t"], geo["radial"].astype(BF16))

    lines_of(out1, in1, 2, LINES_AT, CORNERS_AT).wait_recv()
    some = jnp.concatenate([in1[LINES_AT:, :].astype(BF16), corner_lines(coords_in1)], axis=0)
    pre_known = pre_known + mm(nt(w["dst_t"], some).astype(BF16), ghost[LINES_AT:])
    lines_of(out1, in1, 4, 0, LINES_AT).wait_recv()
    far = nt(w["dst_t"], in1[0:LINES_AT, :].astype(BF16)).astype(BF16)
    dpre, kept = edge_pass(pre_known + mm(far, ghost[:LINES_AT]), geo, w)

    some = nt(ghost[LINES_AT:], dpre)
    out2[LINES_AT:, :] = some[: CORNERS_AT - LINES_AT]
    send_lines(LINES, out2, in2, 6, -1)
    out2[0:LINES_AT, :] = nt(ghost[:LINES_AT], dpre)
    send_lines(FACES, out2, in2, 8, -1)
    dq_pieces = split_rows(edge_coords(dpre, kept, geo, same, w), 2)
    store_coords(coords_out2, sum_pieces(mm(dq_pieces, ghost_t), 2), some[CORNERS_AT - LINES_AT :], False)
    send_coords(coords_out2, coords_in2, 10, -1)

    own = nt(jnp.concatenate([centre, near], axis=0), dpre).astype(BF16)
    own_v[0:ATOMS, :] = nt(own[:ATOMS], wsrc_v[...]) + nt(own[ATOMS:], wdst_v[...])
    own_v[ATOMS:, :] = sum_pieces(nt(dq_pieces, near - centre), 2)
    own_out = pltpu.make_async_copy(own_v, own_hbm, out_sem.at[1])
    own_out.start()

    pick_out.wait()
    own_out.wait()
    coords_of(coords_out1, coords_in1, 0).wait_send()
    for pair, first, last in ((2, LINES_AT, CORNERS_AT), (4, 0, LINES_AT)):
        lines_of(out1, in1, pair, first, last).wait_send()
        lines_of(out2, in2, pair + 4, first, last).wait()
    coords_of(coords_out2, coords_in2, 10).wait()


def finish(back_ref, coords_ref, own_ref, pick_ref, wdst_ref, force_ref, grad_ref):
    pick_t = pick_ref[...]
    lines = jnp.concatenate([back_ref[...].astype(BF16), corner_lines(coords_ref)], axis=0)
    returned = mm(pick_t, lines).astype(BF16)
    grad_ref[...] = own_ref[0:ATOMS, :] + nt(returned, wdst_ref[...])
    total8 = own_ref[ATOMS:, :] + sum_pieces(nt(split_rows(unpack_coords(coords_ref), 2), pick_t), 2)
    force_ref[...] = -total8[4:7]


def body(
    features,
    positions,
    send_ids,
    ghost_prefix,
    edge_fill,
    edge_src,
    edge_dst,
    weight_src,
    weight_dst,
    weight_radial,
    weight_env,
    weight_latent,
    weight_hidden,
    weight_readout,
):
    arrays = [
        features,
        positions,
        send_ids,
        edge_src,
        edge_dst,
        weight_src,
        weight_dst,
        weight_radial,
        weight_env,
        weight_latent,
        weight_hidden,
        weight_readout.reshape(1, CH),
    ]
    hbm = pl.BlockSpec(memory_space=pltpu.HBM)
    vmem = pl.BlockSpec(memory_space=pltpu.VMEM)
    back, coords, own, pick_t = pl.pallas_call(
        kernel,
        out_shape=(
            jax.ShapeDtypeStruct((CORNERS_AT, CH), F32),
            jax.ShapeDtypeStruct((COORDS, CH), F32),
            jax.ShapeDtypeStruct((ATOMS + 8, CH), F32),
            jax.ShapeDtypeStruct((ATOMS, SLOTS), BF16),
        ),
        in_specs=[hbm] * (2 + len(arrays)),
        out_specs=(hbm, hbm, hbm, hbm),
        scratch_shapes=[pltpu.SMEM(ghost_prefix.shape, jnp.int32), pltpu.VMEM((1, 1), jnp.int32)]
        + [pltpu.VMEM(a.shape, a.dtype) for a in arrays]
        + [
            pltpu.VMEM((SLOTS, ATOMS), F32),
            pltpu.VMEM((SLOTS, ATOMS), F32),
            pltpu.VMEM((CORNERS_AT, CH), F32),
            pltpu.VMEM((CORNERS_AT, CH), F32),
            pltpu.VMEM((COORDS, CH), F32),
            pltpu.VMEM((COORDS, CH), F32),
            pltpu.VMEM((CORNERS_AT, CH), F32),
            pltpu.VMEM((COORDS, CH), F32),
            pltpu.VMEM((ATOMS + 8, CH), F32),
            pltpu.VMEM((ATOMS, SLOTS), BF16),
            pltpu.SemaphoreType.DMA((2 + len(arrays),)),
            pltpu.SemaphoreType.DMA((12,)),
            pltpu.SemaphoreType.DMA((2,)),
        ],
        compiler_params=pltpu.CompilerParams(collective_id=0, has_side_effects=True, vmem_limit_bytes=VMEM),
        name="allegro",
    )(ghost_prefix, edge_fill.reshape(1, 1), *arrays)
    return pl.pallas_call(
        finish,
        out_shape=(
            jax.ShapeDtypeStruct((3, ATOMS), F32),
            jax.ShapeDtypeStruct((ATOMS, CH), F32),
        ),
        in_specs=[vmem] * 5,
        out_specs=(vmem, vmem),
        compiler_params=pltpu.CompilerParams(vmem_limit_bytes=VMEM),
        name="finish",
    )(back, coords, own, pick_t, weight_dst)


def solution(mesh):
    return jax.shard_map(
        body,
        mesh=mesh,
        in_specs=(
            P(("dom", "gz"), None),
            P(None, ("dom", "gz")),
            P(("dom", "gz"), None),
            P(("dom", "gz"), None),
            P(("dom", "gz")),
            P(("dom", "gz"), None),
            P(("dom", "gz"), None),
            P(),
            P(),
            P(),
            P(),
            P(),
            P(),
            P(),
        ),
        out_specs=(P(None, ("dom", "gz")), P(("dom", "gz"), None)),
        check_vma=False,
    )
```

```python
import math

import jax
import jax.numpy as jnp
import numpy as np
from jax import lax
from jax.experimental import pallas as pl
from jax.experimental.pallas import tpu as pltpu
from jax.sharding import PartitionSpec as P

NEIGHBOURS = 4
CAPS = (0, 64, 16, 4)
ROW_Y = 8

ATOMS = 128
EDGES = 512
CH = 128
SLOTS = 640
SHARPNESS = 8.0
VMEM = 56 * 1024 * 1024

BF16 = jnp.bfloat16
F32 = jnp.float32
MESH = pl.DeviceIdType.MESH


def directions():
    table = []
    offset = 0
    number = 0
    for a in (-1, 0, 1):
        for b in (-1, 0, 1):
            for c in (-1, 0, 1):
                kind = abs(a) + abs(b) + abs(c)
                if kind == 0:
                    continue
                cap = CAPS[kind]
                table.append(dict(vec=(a, b, c), kind=kind, cap=cap, number=number, offset=offset))
                offset += cap
                number += 1
    table.sort(key=lambda d: (d["kind"], d["number"]))
    slot = 0
    for step, d in enumerate(table):
        d["rows"] = {1: 64, 2: 16, 3: 8}[d["kind"]]
        d["slot"] = slot
        d["tile"] = 8 * step
        slot += d["rows"]
    assert slot == SLOTS
    return table


TABLE = directions()
FACES = [d for d in TABLE if d["kind"] == 1]
LINES = [d for d in TABLE if d["kind"] == 2]
CORNERS = [d for d in TABLE if d["kind"] == 3]
ORDER = sorted(TABLE, key=lambda d: (-d["kind"], d["vec"][2] == 0))
LINES_AT, CORNERS_AT = LINES[0]["slot"], CORNERS[0]["slot"]
COORDS = 8 * len(TABLE)
COORDS_SENT = 4 * len(TABLE) + 4 * len(CORNERS)


def mm(a, b):
    return lax.dot_general(a, b, (((1,), (0,)), ((), ())), preferred_element_type=F32)


def nt(a, b):
    return lax.dot_general(a, b, (((1,), (1,)), ((), ())), preferred_element_type=F32)


def tn(a, b):
    return lax.dot_general(a, b, (((0,), (0,)), ((), ())), preferred_element_type=F32)


def iota(shape, dim):
    return lax.broadcasted_iota(jnp.int32, shape, dim)


def onehot(cond):
    return jnp.where(cond, 1.0, 0.0).astype(BF16)


def split(x, pieces):
    out = []
    for step in range(pieces):
        part = x.astype(BF16)
        out.append(part)
        if step + 1 < pieces:
            x = x - part.astype(F32)
    return out


def split_rows(x, pieces):
    parts = []
    for step in range(pieces):
        part = x.astype(BF16).astype(F32)
        parts.append(part)
        x = x - part
    if pieces % 2:
        parts.append(jnp.zeros_like(x))
    return jnp.concatenate(parts, axis=0).astype(BF16)


def sum_pieces(x, pieces):
    total = x[0:8]
    for step in range(1, pieces):
        total = total + x[8 * step : 8 * step + 8]
    return total


def sigmoid(v):
    return 0.5 * jnp.tanh(0.5 * v) + 0.5


def silu_pair(v):
    v = v.astype(BF16)
    sig = sigmoid(v)
    value = v * sig
    return value, sig + value * (1 - sig)


def rows_to_eight(rows, first):
    place = iota((8, rows[0].shape[1]), 0)
    out = jnp.zeros((8, rows[0].shape[1]), F32)
    for step, row in enumerate(rows):
        out = jnp.where(place == first + step, row, out)
    return out


def slot_ids(dst_row):
    blocks = []
    for d in TABLE:
        if d["kind"] <= 2:
            place = iota((d["rows"], EDGES), 0) + (ATOMS + d["offset"])
            blocks.append(onehot(place == dst_row))
    place = iota((8 * len(CORNERS), EDGES), 0)
    inner = place % 8
    base = jnp.zeros_like(place)
    for step, d in enumerate(CORNERS):
        base = jnp.where(place // 8 == step, ATOMS - 4 + d["offset"], base)
    blocks.append(onehot((inner >= 4) & (base + inner == dst_row)))
    return jnp.concatenate(blocks, axis=0)


def side_by_side(x):
    rows = x.shape[0] // 3
    return jnp.concatenate([x[rows * step : rows * (step + 1)] for step in range(3)], axis=1)


def mixing(wenv, wlat):
    parts = [wlat[:CH]]
    for step in range(1, 4):
        parts.append(mm(wenv, wlat[CH * step : CH * (step + 1)]).astype(BF16))
    return parts


def geometry(pos_i, pos_j, in_fill, same):
    diff = pos_j - pos_i
    qx, qy, qz = diff[4:5], diff[5:6], diff[6:7]
    live = pos_j[7:8]
    rsq = qx * qx + qy * qy + qz * qz
    in_use = in_fill * live
    inside = jnp.where(rsq < 1.0, 1.0 - rsq, 0.0)
    env = inside * inside * in_use
    centers = iota((8, EDGES), 0).astype(F32) / 7.0
    offset = rsq - centers
    radial = jnp.exp(-SHARPNESS * offset * offset)

    r3, r15, r5 = math.sqrt(3.0), math.sqrt(15.0), math.sqrt(5.0)
    y1 = rows_to_eight([r3 * qx, r3 * qy, r3 * qz], 0)
    y2 = rows_to_eight(
        [
            r15 * qx * qy,
            r15 * qy * qz,
            r15 * qz * qx,
            0.5 * r15 * (qx * qx - qy * qy),
            0.5 * r5 * (2.0 * qz * qz - qx * qx - qy * qy),
        ],
        0,
    )
    h1, l1 = (part.astype(F32) for part in split(y1, 2))
    h2, l2 = (part.astype(F32) for part in split(y2, 2))
    zero8 = jnp.zeros((8, EDGES), F32)
    left1 = jnp.concatenate([h1, h1, l1, zero8], axis=0).astype(BF16)
    right1 = jnp.concatenate([h1, l1, h1, zero8], axis=0).astype(BF16)
    left2 = jnp.concatenate([h2, h2, l2, zero8], axis=0).astype(BF16)
    right2 = jnp.concatenate([h2, l2, h2, zero8], axis=0).astype(BF16)
    k1 = tn(left1, right1).astype(BF16) * same
    k2 = tn(left2, right2).astype(BF16) * same

    return dict(
        q=(qx, qy, qz),
        in_use=in_use,
        inside=inside,
        env=env,
        offset=offset,
        radial=radial,
        left1=left1,
        left2=left2,
        kernels=jnp.concatenate([same, k1, k2], axis=0),
    )


def edge_pass(pre, geo, same, w):
    env, kernels = geo["env"], geo["kernels"]
    env16 = env.astype(BF16)
    act, dact = silu_pair(pre)
    latent = act * env16
    mixed = mm(w["mix_t"], latent)
    near_far = mixed[CH:].astype(BF16)
    upd_act, upd_d = silu_pair(mixed[:CH] + mm(side_by_side(near_far), kernels))
    hid_act, hid_d = silu_pair(mm(w["hid_t"], latent + upd_act))
    dhid = hid_d * (w["ro"] * env).astype(BF16)
    dupdated = mm(w["hid"], dhid)
    dupd = dupdated.astype(BF16) * upd_d
    dupd_t = dupd.T
    pairs = [
        mm(jnp.concatenate([dupd_t, b.T], axis=1), jnp.concatenate([b, dupd], axis=0)).astype(BF16) * same
        for b in (near_far[CH : 2 * CH], near_far[2 * CH :])
    ]
    dmixed = mm(w["mix"], dupd)
    dlatent = dupdated + dmixed[:CH] + mm(side_by_side(dmixed[CH:].astype(BF16)), kernels)
    dpre = (dlatent * env).astype(BF16) * dact
    return dpre, (dlatent, act, hid_act, pairs)


def slot_ids_across(dst_row):
    dst = jnp.broadcast_to(dst_row.astype(F32), (128, EDGES)).T
    blocks = []
    for tile in range(SLOTS // 128):
        lane = iota((8, 128), 1)
        ids = jnp.full((8, 128), -1, jnp.int32)
        for d in TABLE:
            if d["slot"] // 128 == tile:
                low = d["slot"] % 128 + (4 if d["kind"] == 3 else 0)
                mine = (lane >= low) & (lane < low + d["cap"])
                ids = jnp.where(mine, lane + (ATOMS + d["offset"] - low), ids)
        blocks.append(onehot(dst == ids.astype(F32)[0:1]))
    return jnp.concatenate(blocks, axis=1)


def edge_coords(dpre, kept, geo, w):
    dlatent, act, hid_act, pairs = kept
    r3, r15, r5 = math.sqrt(3.0), math.sqrt(15.0), math.sqrt(5.0)
    qx, qy, qz = geo["q"]
    denv = jnp.sum(hid_act * w["ro"] + dlatent * act, axis=0, keepdims=True)
    t1, t2 = pairs
    dy1 = mm(geo["left1"], t1)
    dy1 = dy1[0:8] + dy1[16:24]
    dy2 = mm(geo["left2"], t2)
    dy2 = dy2[0:8] + dy2[16:24]

    drad = mm(w["rad"], dpre)
    drsq = jnp.sum(drad * geo["radial"] * geo["offset"], axis=0, keepdims=True) * (-2.0 * SHARPNESS)
    drsq = drsq - 2.0 * denv * geo["in_use"] * geo["inside"]
    a0, a1, a2, a3, a4 = (dy2[step : step + 1] for step in range(5))
    two = 2.0 * drsq
    gx = two * qx + r3 * dy1[0:1] + r15 * (a0 * qy + a2 * qz + a3 * qx) - r5 * a4 * qx
    gy = two * qy + r3 * dy1[1:2] + r15 * (a0 * qx + a1 * qz - a3 * qy) - r5 * a4 * qy
    gz = two * qz + r3 * dy1[2:3] + r15 * (a1 * qy + a2 * qx) + 2.0 * r5 * a4 * qz
    return rows_to_eight([gx, gy, gz], 4)


def corner_lines(ref):
    tiles = ref[CORNERS[0]["tile"] :, :]
    return jnp.where(iota(tiles.shape, 0) % 8 >= 4, tiles, 0.0).astype(BF16)


def unpack_coords(ref):
    tiles = [None] * (SLOTS // 128)
    for d in TABLE:
        tile = d["slot"] // 128
        piece = ref[d["tile"] : d["tile"] + 4, :]
        tiles[tile] = piece if tiles[tile] is None else tiles[tile] + piece
    coords = jnp.concatenate(tiles, axis=1)
    return jnp.concatenate([jnp.zeros_like(coords), coords], axis=0)


def kernel(
    prefix_hbm,
    fill_hbm,
    feat_hbm,
    pos_hbm,
    send_hbm,
    src_hbm,
    dst_hbm,
    wsrc_hbm,
    wdst_hbm,
    wrad_hbm,
    wenv_hbm,
    wlat_hbm,
    whid_hbm,
    wro_hbm,
    in2,
    coords_in2,
    own_hbm,
    pick_hbm,
    prefix,
    fill,
    feat_v,
    pos_v,
    send_v,
    src_v,
    dst_v,
    wsrc_v,
    wdst_v,
    wrad_v,
    wenv_v,
    wlat_v,
    whid_v,
    wro_v,
    list_v,
    pick_v,
    out1,
    in1,
    coords_out1,
    coords_in1,
    out2,
    coords_out2,
    own_v,
    pick_t_v,
    in_sem,
    sems,
    out_sem,
):
    planes = lax.axis_size("dom") // ROW_Y
    depth = lax.axis_size("gz")
    dom = lax.axis_index("dom")
    cz = lax.axis_index("gz")
    cx, cy = lax.div(dom, ROW_Y), lax.rem(dom, ROW_Y)
    along_x = {step: lax.rem(cx + (step + planes), planes) * ROW_Y for step in (-1, 0, 1)}
    along_y = {step: lax.rem(cy + (step + ROW_Y), ROW_Y) for step in (-1, 0, 1)}
    along_z = {step: lax.rem(cz + (step + depth), depth) for step in (-1, 0, 1)}

    def place(vec, sign):
        return (along_x[sign * vec[0]] + along_y[sign * vec[1]], along_z[sign * vec[2]])

    loads = []
    for step, (source, target) in enumerate(
        [
            (send_hbm, send_v),
            (prefix_hbm, prefix),
            (feat_hbm, feat_v),
            (pos_hbm, pos_v),
            (src_hbm, src_v),
            (dst_hbm, dst_v),
            (wsrc_hbm, wsrc_v),
            (wdst_hbm, wdst_v),
            (wrad_hbm, wrad_v),
            (wenv_hbm, wenv_v),
            (wlat_hbm, wlat_v),
            (whid_hbm, whid_v),
            (wro_hbm, wro_v),
            (fill_hbm, fill),
        ]
    ):
        copy = pltpu.make_async_copy(source, target, in_sem.at[step])
        loads.append(copy)

    barrier = pltpu.get_barrier_semaphore()
    for copy in loads[:4]:
        copy.start()
    for d in ORDER:
        pl.semaphore_signal(barrier, inc=1, device_id=place(d["vec"], 1), device_id_type=MESH)
    for copy in loads[4:]:
        copy.start()

    loads[0].wait()
    listed = jnp.where(iota((ATOMS, 608), 0) == send_v[...], 1.0, 0.0)
    list_v[0:608, :] = listed.T
    list_v[608:640, :] = jnp.zeros((32, ATOMS), F32)
    loads[1].wait()
    loads[2].wait()
    loads[3].wait()
    feat16 = feat_v[...].astype(BF16)
    pos = pos_v[...]
    own8 = rows_to_eight([pos[0:1], pos[1:2], pos[2:3], jnp.ones((1, ATOMS), F32)], 4)
    own_pieces = split_rows(own8, 3)
    lane = iota((8, 128), 1)
    line = iota((8, 128), 0)

    def store_coords(ref, slots, corners, shifted):
        for d in TABLE:
            tile, low = d["slot"] // 128 * 128, d["slot"] % 128
            inside = (lane >= low) & (lane < low + d["rows"])
            coords = slots[:, tile : tile + 128]
            if shifted:
                shift = jnp.zeros((8, 128), F32)
                for step in range(3):
                    if d["vec"][step]:
                        shift = jnp.where(line == 4 + step, float(d["vec"][step]), shift)
                coords = coords - shift
            coords = jnp.where(inside, coords, 0.0)[4:8]
            if d["kind"] == 3:
                first = d["slot"] - CORNERS_AT
                coords = jnp.concatenate([coords, corners[first + 4 : first + 8]], axis=0)
            ref[d["tile"] : d["tile"] + coords.shape[0], :] = coords

    def remote(source, target, start, size, pair, vec, sign):
        rows = pl.ds(start, size)
        return pltpu.make_async_remote_copy(
            src_ref=source.at[rows],
            dst_ref=target.at[rows],
            send_sem=sems.at[pair],
            recv_sem=sems.at[pair + 1],
            device_id=place(vec, sign),
            device_id_type=MESH,
        )

    def send_lines(table, source, target, pair, sign):
        for d in ORDER:
            if d not in table:
                continue
            remote(source, target, d["slot"], d["rows"], pair, d["vec"], sign).start()

    def send_coords(source, target, pair, sign):
        for d in ORDER:
            remote(source, target, d["tile"], 8 if d["kind"] == 3 else 4, pair, d["vec"], sign).start()

    def lines_of(source, target, pair, first, last):
        return remote(source, target, first, last - first, pair, TABLE[0]["vec"], 1)

    def coords_of(source, target, pair):
        return remote(source, target, 0, COORDS_SENT, pair, TABLE[0]["vec"], 1)

    for d in TABLE:
        n, rows = d["number"], d["rows"]
        count = prefix[0, n + 1] - prefix[0, n]
        lines = list_v[pl.ds(prefix[0, n], rows), :]
        lines = jnp.where(iota((rows, ATOMS), 0) < count, lines, 0.0)
        if d["kind"] == 3:
            lines = jnp.concatenate([jnp.zeros((4, ATOMS), F32), lines[:4]], axis=0)
        pick_v[d["slot"] : d["slot"] + rows, :] = lines
    pick = pick_v[...].astype(BF16)
    packed = mm(pick, feat16)
    store_coords(coords_out1, sum_pieces(nt(own_pieces, pick), 3), packed[CORNERS_AT:], True)
    out1[...] = packed[:CORNERS_AT]
    pl.semaphore_wait(barrier, len(TABLE))
    send_coords(coords_out1, coords_in1, 0, 1)
    send_lines(LINES, out1, in1, 2, 1)
    send_lines(FACES, out1, in1, 4, 1)

    for copy in loads[4:]:
        copy.wait()
    src_row, dst_row = src_v[...], dst_v[...]
    centre = onehot(iota((ATOMS, EDGES), 0) == src_row)
    near = onehot(iota((ATOMS, EDGES), 0) == dst_row)
    ghost = slot_ids(dst_row)
    ghost_t = slot_ids_across(dst_row)
    same = (tn(centre, centre) * (1.0 / NEIGHBOURS)).astype(BF16)
    in_fill = jnp.where(iota((1, EDGES), 1) < fill[...], 1.0, 0.0)
    eye = iota((CH, CH), 0) == iota((CH, CH), 1)
    mix = mixing(wenv_v[...], wlat_v[...])
    w = dict(
        dst_t=wdst_v[...].T,
        rad_t=wrad_v[...].T,
        mix=jnp.concatenate(mix, axis=0),
        mix_t=jnp.concatenate([part.T for part in mix], axis=0),
        hid_t=whid_v[...].T,
        rad=wrad_v[...],
        hid=whid_v[...],
        ro=jnp.sum(jnp.where(eye, wro_v[...], 0.0), axis=1, keepdims=True),
    )
    feat_t = feat16.T
    own_lhs = jnp.concatenate([feat_t, own_pieces], axis=0)
    at_i = mm(own_lhs, centre)
    at_j = mm(own_lhs, near)
    pre_own = mm(wsrc_v[...].T, at_i[:CH].astype(BF16)) + mm(w["dst_t"], at_j[:CH].astype(BF16))
    pos_i = sum_pieces(at_i[CH:], 3)
    pos_j_own = sum_pieces(at_j[CH:], 3)
    pick_t_v[...] = pick.T
    pick_out = pltpu.make_async_copy(pick_t_v, pick_hbm, out_sem.at[0])
    pick_out.start()

    coords_of(coords_out1, coords_in1, 0).wait_recv()
    pos_g = mm(split_rows(unpack_coords(coords_in1), 3), ghost)
    geo = geometry(pos_i, pos_j_own + sum_pieces(pos_g, 3), in_fill, same)

    pre_known = pre_own + mm(w["rad_t"], geo["radial"].astype(BF16))

    lines_of(out1, in1, 2, LINES_AT, CORNERS_AT).wait_recv()
    some = jnp.concatenate([in1[LINES_AT:, :].astype(BF16), corner_lines(coords_in1)], axis=0)
    pre_known = pre_known + mm(nt(w["dst_t"], some).astype(BF16), ghost[LINES_AT:])
    lines_of(out1, in1, 4, 0, LINES_AT).wait_recv()
    far = nt(w["dst_t"], in1[0:LINES_AT, :].astype(BF16)).astype(BF16)
    dpre, kept = edge_pass(pre_known + mm(far, ghost[:LINES_AT]), geo, same, w)

    some = nt(ghost[LINES_AT:], dpre)
    out2[LINES_AT:, :] = some[: CORNERS_AT - LINES_AT]
    send_lines(LINES, out2, in2, 6, -1)
    out2[0:LINES_AT, :] = nt(ghost[:LINES_AT], dpre)
    send_lines(FACES, out2, in2, 8, -1)
    dq_pieces = split_rows(edge_coords(dpre, kept, geo, w), 2)
    store_coords(coords_out2, sum_pieces(mm(dq_pieces, ghost_t), 2), some[CORNERS_AT - LINES_AT :], False)
    send_coords(coords_out2, coords_in2, 10, -1)

    own = nt(jnp.concatenate([centre, near], axis=0), dpre).astype(BF16)
    own_v[0:ATOMS, :] = nt(own[:ATOMS], wsrc_v[...]) + nt(own[ATOMS:], wdst_v[...])
    own_v[ATOMS:, :] = sum_pieces(nt(dq_pieces, near - centre), 2)
    own_out = pltpu.make_async_copy(own_v, own_hbm, out_sem.at[1])
    own_out.start()

    pick_out.wait()
    own_out.wait()
    coords_of(coords_out1, coords_in1, 0).wait_send()
    for pair, first, last in ((2, LINES_AT, CORNERS_AT), (4, 0, LINES_AT)):
        lines_of(out1, in1, pair, first, last).wait_send()
        lines_of(out2, in2, pair + 4, first, last).wait()
    coords_of(coords_out2, coords_in2, 10).wait()


def finish(
    back_hbm,
    coords_hbm,
    pick_hbm,
    own_hbm,
    wdst_hbm,
    force_hbm,
    grad_hbm,
    back_v,
    coords_v,
    pick_v,
    own_v,
    wdst_v,
    force_v,
    grad_v,
    sems,
):
    sources = (back_hbm, coords_hbm, pick_hbm, own_hbm, wdst_hbm)
    targets = (back_v, coords_v, pick_v, own_v, wdst_v)
    loads = [pltpu.make_async_copy(a, b, sems.at[step]) for step, (a, b) in enumerate(zip(sources, targets))]
    for copy in loads:
        copy.start()
    for copy in loads:
        copy.wait()
    pick_t = pick_v[...]
    lines = jnp.concatenate([back_v[...].astype(BF16), corner_lines(coords_v)], axis=0)
    returned = mm(pick_t, lines).astype(BF16)
    total8 = own_v[ATOMS:, :] + sum_pieces(nt(split_rows(unpack_coords(coords_v), 2), pick_t), 2)
    force_v[...] = -total8[4:7]
    force_out = pltpu.make_async_copy(force_v, force_hbm, sems.at[5])
    force_out.start()
    grad_v[...] = own_v[0:ATOMS, :] + nt(returned, wdst_v[...])
    grad_out = pltpu.make_async_copy(grad_v, grad_hbm, sems.at[6])
    grad_out.start()
    force_out.wait()
    grad_out.wait()


def body(
    features,
    positions,
    send_ids,
    ghost_prefix,
    edge_fill,
    edge_src,
    edge_dst,
    weight_src,
    weight_dst,
    weight_radial,
    weight_env,
    weight_latent,
    weight_hidden,
    weight_readout,
):
    arrays = [
        features,
        positions,
        send_ids,
        edge_src,
        edge_dst,
        weight_src,
        weight_dst,
        weight_radial,
        weight_env,
        weight_latent,
        weight_hidden,
        weight_readout.reshape(1, CH),
    ]
    hbm = pl.BlockSpec(memory_space=pltpu.HBM)
    back, coords, own, pick_t = pl.pallas_call(
        kernel,
        out_shape=(
            jax.ShapeDtypeStruct((CORNERS_AT, CH), F32),
            jax.ShapeDtypeStruct((COORDS, CH), F32),
            jax.ShapeDtypeStruct((ATOMS + 8, CH), F32),
            jax.ShapeDtypeStruct((ATOMS, SLOTS), BF16),
        ),
        in_specs=[hbm] * (2 + len(arrays)),
        out_specs=(hbm, hbm, hbm, hbm),
        scratch_shapes=[pltpu.SMEM(ghost_prefix.shape, jnp.int32), pltpu.VMEM((1, 1), jnp.int32)]
        + [pltpu.VMEM(a.shape, a.dtype) for a in arrays]
        + [
            pltpu.VMEM((SLOTS, ATOMS), F32),
            pltpu.VMEM((SLOTS, ATOMS), F32),
            pltpu.VMEM((CORNERS_AT, CH), F32),
            pltpu.VMEM((CORNERS_AT, CH), F32),
            pltpu.VMEM((COORDS, CH), F32),
            pltpu.VMEM((COORDS, CH), F32),
            pltpu.VMEM((CORNERS_AT, CH), F32),
            pltpu.VMEM((COORDS, CH), F32),
            pltpu.VMEM((ATOMS + 8, CH), F32),
            pltpu.VMEM((ATOMS, SLOTS), BF16),
            pltpu.SemaphoreType.DMA((2 + len(arrays),)),
            pltpu.SemaphoreType.DMA((12,)),
            pltpu.SemaphoreType.DMA((2,)),
        ],
        compiler_params=pltpu.CompilerParams(collective_id=0, has_side_effects=True, vmem_limit_bytes=VMEM),
        name="allegro",
    )(ghost_prefix, edge_fill.reshape(1, 1), *arrays)
    return pl.pallas_call(
        finish,
        out_shape=(
            jax.ShapeDtypeStruct((3, ATOMS), F32),
            jax.ShapeDtypeStruct((ATOMS, CH), F32),
        ),
        in_specs=[hbm] * 5,
        out_specs=(hbm, hbm),
        scratch_shapes=[
            pltpu.VMEM((CORNERS_AT, CH), F32),
            pltpu.VMEM((COORDS, CH), F32),
            pltpu.VMEM((ATOMS, SLOTS), BF16),
            pltpu.VMEM((ATOMS + 8, CH), F32),
            pltpu.VMEM((CH, CH), BF16),
            pltpu.VMEM((3, ATOMS), F32),
            pltpu.VMEM((ATOMS, CH), F32),
            pltpu.SemaphoreType.DMA((7,)),
        ],
        compiler_params=pltpu.CompilerParams(vmem_limit_bytes=VMEM),
        name="finish",
    )(back, coords, pick_t, own, weight_dst)


def solution(mesh):
    return jax.shard_map(
        body,
        mesh=mesh,
        in_specs=(
            P(("dom", "gz"), None),
            P(None, ("dom", "gz")),
            P(("dom", "gz"), None),
            P(("dom", "gz"), None),
            P(("dom", "gz")),
            P(("dom", "gz"), None),
            P(("dom", "gz"), None),
            P(),
            P(),
            P(),
            P(),
            P(),
            P(),
            P(),
        ),
        out_specs=(P(None, ("dom", "gz")), P(("dom", "gz"), None)),
        check_vma=False,
    )
```

```python
import math

import jax
import jax.numpy as jnp
import numpy as np
from jax import lax
from jax.experimental import pallas as pl
from jax.experimental.pallas import tpu as pltpu
from jax.sharding import PartitionSpec as P

NEIGHBOURS = 4
CAPS = (0, 64, 16, 4)
ROW_Y = 8

ATOMS = 128
EDGES = 512
CH = 128
SLOTS = 640
SHARPNESS = 8.0
VMEM = 56 * 1024 * 1024

BF16 = jnp.bfloat16
F32 = jnp.float32
MESH = pl.DeviceIdType.MESH


def directions():
    table = []
    offset = 0
    number = 0
    for a in (-1, 0, 1):
        for b in (-1, 0, 1):
            for c in (-1, 0, 1):
                kind = abs(a) + abs(b) + abs(c)
                if kind == 0:
                    continue
                cap = CAPS[kind]
                table.append(dict(vec=(a, b, c), kind=kind, cap=cap, number=number, offset=offset))
                offset += cap
                number += 1
    table.sort(key=lambda d: (d["kind"], d["number"]))
    slot = 0
    for step, d in enumerate(table):
        d["rows"] = {1: 64, 2: 16, 3: 8}[d["kind"]]
        d["slot"] = slot
        d["tile"] = 8 * step
        slot += d["rows"]
    assert slot == SLOTS
    return table


TABLE = directions()
FACES = [d for d in TABLE if d["kind"] == 1]
LINES = [d for d in TABLE if d["kind"] == 2]
CORNERS = [d for d in TABLE if d["kind"] == 3]
ORDER = sorted(TABLE, key=lambda d: (-d["kind"], d["vec"][2] == 0))
LINES_AT, CORNERS_AT = LINES[0]["slot"], CORNERS[0]["slot"]
COORDS = 8 * len(TABLE)
COORDS_SENT = 4 * len(TABLE) + 4 * len(CORNERS)


def mm(a, b):
    return lax.dot_general(a, b, (((1,), (0,)), ((), ())), preferred_element_type=F32)


def nt(a, b):
    return lax.dot_general(a, b, (((1,), (1,)), ((), ())), preferred_element_type=F32)


def tn(a, b):
    return lax.dot_general(a, b, (((0,), (0,)), ((), ())), preferred_element_type=F32)


def iota(shape, dim):
    return lax.broadcasted_iota(jnp.int32, shape, dim)


def onehot(cond):
    return jnp.where(cond, 1.0, 0.0).astype(BF16)


def split(x, pieces):
    out = []
    for step in range(pieces):
        part = x.astype(BF16)
        out.append(part)
        if step + 1 < pieces:
            x = x - part.astype(F32)
    return out


def split_rows(x, pieces):
    parts = []
    for step in range(pieces):
        part = x.astype(BF16).astype(F32)
        parts.append(part)
        x = x - part
    if pieces % 2:
        parts.append(jnp.zeros_like(x))
    return jnp.concatenate(parts, axis=0).astype(BF16)


def sum_pieces(x, pieces):
    total = x[0:8]
    for step in range(1, pieces):
        total = total + x[8 * step : 8 * step + 8]
    return total


def sigmoid(v):
    return 0.5 * jnp.tanh(0.5 * v) + 0.5


def silu_pair(v):
    v = v.astype(BF16)
    sig = sigmoid(v)
    value = v * sig
    return value, sig + value * (1 - sig)


def rows_to_eight(rows, first):
    place = iota((8, rows[0].shape[1]), 0)
    out = jnp.zeros((8, rows[0].shape[1]), F32)
    for step, row in enumerate(rows):
        out = jnp.where(place == first + step, row, out)
    return out


def slot_ids(dst_row):
    blocks = []
    for d in TABLE:
        if d["kind"] <= 2:
            place = iota((d["rows"], EDGES), 0) + (ATOMS + d["offset"])
            blocks.append(onehot(place == dst_row))
    place = iota((8 * len(CORNERS), EDGES), 0)
    inner = place % 8
    base = jnp.zeros_like(place)
    for step, d in enumerate(CORNERS):
        base = jnp.where(place // 8 == step, ATOMS - 4 + d["offset"], base)
    blocks.append(onehot((inner >= 4) & (base + inner == dst_row)))
    return jnp.concatenate(blocks, axis=0)


def side_by_side(x):
    rows = x.shape[0] // 3
    return jnp.concatenate([x[rows * step : rows * (step + 1)] for step in range(3)], axis=1)


def mixing(wenv, wlat):
    parts = [wlat[:CH]]
    for step in range(1, 4):
        parts.append(mm(wenv, wlat[CH * step : CH * (step + 1)]).astype(BF16))
    return parts


def geometry(pos_i, pos_j, in_fill, same):
    diff = pos_j - pos_i
    qx, qy, qz = diff[4:5], diff[5:6], diff[6:7]
    live = pos_j[7:8]
    rsq = qx * qx + qy * qy + qz * qz
    in_use = in_fill * live
    inside = jnp.where(rsq < 1.0, 1.0 - rsq, 0.0)
    env = inside * inside * in_use
    centers = iota((8, EDGES), 0).astype(F32) / 7.0
    offset = rsq - centers
    radial = jnp.exp(-SHARPNESS * offset * offset)

    r3, r15, r5 = math.sqrt(3.0), math.sqrt(15.0), math.sqrt(5.0)
    y1 = rows_to_eight([r3 * qx, r3 * qy, r3 * qz], 0)
    y2 = rows_to_eight(
        [
            r15 * qx * qy,
            r15 * qy * qz,
            r15 * qz * qx,
            0.5 * r15 * (qx * qx - qy * qy),
            0.5 * r5 * (2.0 * qz * qz - qx * qx - qy * qy),
        ],
        0,
    )
    h1, l1 = (part.astype(F32) for part in split(y1, 2))
    h2, l2 = (part.astype(F32) for part in split(y2, 2))
    zero8 = jnp.zeros((8, EDGES), F32)
    left1 = jnp.concatenate([h1, h1, l1, zero8], axis=0).astype(BF16)
    right1 = jnp.concatenate([h1, l1, h1, zero8], axis=0).astype(BF16)
    left2 = jnp.concatenate([h2, h2, l2, zero8], axis=0).astype(BF16)
    right2 = jnp.concatenate([h2, l2, h2, zero8], axis=0).astype(BF16)
    k1 = tn(left1, right1).astype(BF16) * same
    k2 = tn(left2, right2).astype(BF16) * same

    return dict(
        q=(qx, qy, qz),
        in_use=in_use,
        inside=inside,
        env=env,
        offset=offset,
        radial=radial,
        left1=left1,
        left2=left2,
        kernels=jnp.concatenate([same, k1, k2], axis=0),
    )


def edge_pass(pre, geo, w):
    env, kernels = geo["env"], geo["kernels"]
    env16 = env.astype(BF16)
    act, dact = silu_pair(pre)
    latent = act * env16
    mixed = mm(w["mix_t"], latent)
    near_far = mixed[CH:].astype(BF16)
    upd_act, upd_d = silu_pair(mixed[:CH] + mm(side_by_side(near_far), kernels))
    hid_act, hid_d = silu_pair(mm(w["hid_t"], latent + upd_act))
    dhid = hid_d * (w["ro"] * env).astype(BF16)
    dupdated = mm(w["hid"], dhid)
    dupd = dupdated.astype(BF16) * upd_d
    dmixed = mm(w["mix"], dupd)
    dlatent = dupdated + dmixed[:CH] + mm(side_by_side(dmixed[CH:].astype(BF16)), kernels)
    dpre = (dlatent * env).astype(BF16) * dact
    return dpre, (dlatent, act, hid_act, near_far, dupd)


def slot_ids_across(dst_row):
    dst = jnp.broadcast_to(dst_row.astype(F32), (128, EDGES)).T
    blocks = []
    for tile in range(SLOTS // 128):
        lane = iota((8, 128), 1)
        ids = jnp.full((8, 128), -1, jnp.int32)
        for d in TABLE:
            if d["slot"] // 128 == tile:
                low = d["slot"] % 128 + (4 if d["kind"] == 3 else 0)
                mine = (lane >= low) & (lane < low + d["cap"])
                ids = jnp.where(mine, lane + (ATOMS + d["offset"] - low), ids)
        blocks.append(onehot(dst == ids.astype(F32)[0:1]))
    return jnp.concatenate(blocks, axis=1)


def edge_coords(dpre, kept, geo, same, w):
    dlatent, act, hid_act, near_far, dupd = kept
    r3, r15, r5 = math.sqrt(3.0), math.sqrt(15.0), math.sqrt(5.0)
    qx, qy, qz = geo["q"]
    denv = jnp.sum(hid_act * w["ro"] + dlatent * act, axis=0, keepdims=True)
    dupd_t = dupd.T
    t1, t2 = (
        mm(jnp.concatenate([dupd_t, b.T], axis=1), jnp.concatenate([b, dupd], axis=0)).astype(BF16) * same
        for b in (near_far[CH : 2 * CH], near_far[2 * CH :])
    )
    dy1 = mm(geo["left1"], t1)
    dy1 = dy1[0:8] + dy1[16:24]
    dy2 = mm(geo["left2"], t2)
    dy2 = dy2[0:8] + dy2[16:24]

    drad = mm(w["rad"], dpre)
    drsq = jnp.sum(drad * geo["radial"] * geo["offset"], axis=0, keepdims=True) * (-2.0 * SHARPNESS)
    drsq = drsq - 2.0 * denv * geo["in_use"] * geo["inside"]
    a0, a1, a2, a3, a4 = (dy2[step : step + 1] for step in range(5))
    two = 2.0 * drsq
    gx = two * qx + r3 * dy1[0:1] + r15 * (a0 * qy + a2 * qz + a3 * qx) - r5 * a4 * qx
    gy = two * qy + r3 * dy1[1:2] + r15 * (a0 * qx + a1 * qz - a3 * qy) - r5 * a4 * qy
    gz = two * qz + r3 * dy1[2:3] + r15 * (a1 * qy + a2 * qx) + 2.0 * r5 * a4 * qz
    return rows_to_eight([gx, gy, gz], 4)


def corner_lines(ref):
    tiles = ref[CORNERS[0]["tile"] :, :]
    return jnp.where(iota(tiles.shape, 0) % 8 >= 4, tiles, 0.0).astype(BF16)


def unpack_coords(ref):
    tiles = [None] * (SLOTS // 128)
    for d in TABLE:
        tile = d["slot"] // 128
        piece = ref[d["tile"] : d["tile"] + 4, :]
        tiles[tile] = piece if tiles[tile] is None else tiles[tile] + piece
    coords = jnp.concatenate(tiles, axis=1)
    return jnp.concatenate([jnp.zeros_like(coords), coords], axis=0)


def kernel(
    prefix_hbm,
    fill_hbm,
    feat_hbm,
    pos_hbm,
    send_hbm,
    src_hbm,
    dst_hbm,
    wsrc_hbm,
    wdst_hbm,
    wrad_hbm,
    wenv_hbm,
    wlat_hbm,
    whid_hbm,
    wro_hbm,
    in2,
    coords_in2,
    own_hbm,
    pick_hbm,
    prefix,
    fill,
    feat_v,
    pos_v,
    send_v,
    src_v,
    dst_v,
    wsrc_v,
    wdst_v,
    wrad_v,
    wenv_v,
    wlat_v,
    whid_v,
    wro_v,
    list_v,
    pick_v,
    out1,
    in1,
    coords_out1,
    coords_in1,
    out2,
    coords_out2,
    own_v,
    pick_t_v,
    in_sem,
    sems,
    out_sem,
):
    planes = lax.axis_size("dom") // ROW_Y
    depth = lax.axis_size("gz")
    dom = lax.axis_index("dom")
    cz = lax.axis_index("gz")
    cx, cy = lax.div(dom, ROW_Y), lax.rem(dom, ROW_Y)
    along_x = {step: lax.rem(cx + (step + planes), planes) * ROW_Y for step in (-1, 0, 1)}
    along_y = {step: lax.rem(cy + (step + ROW_Y), ROW_Y) for step in (-1, 0, 1)}
    along_z = {step: lax.rem(cz + (step + depth), depth) for step in (-1, 0, 1)}

    def place(vec, sign):
        return (along_x[sign * vec[0]] + along_y[sign * vec[1]], along_z[sign * vec[2]])

    loads = []
    for step, (source, target) in enumerate(
        [
            (send_hbm, send_v),
            (prefix_hbm, prefix),
            (feat_hbm, feat_v),
            (pos_hbm, pos_v),
            (src_hbm, src_v),
            (dst_hbm, dst_v),
            (wsrc_hbm, wsrc_v),
            (wdst_hbm, wdst_v),
            (wrad_hbm, wrad_v),
            (wenv_hbm, wenv_v),
            (wlat_hbm, wlat_v),
            (whid_hbm, whid_v),
            (wro_hbm, wro_v),
            (fill_hbm, fill),
        ]
    ):
        copy = pltpu.make_async_copy(source, target, in_sem.at[step])
        loads.append(copy)

    barrier = pltpu.get_barrier_semaphore()
    for copy in loads[:4]:
        copy.start()
    for d in ORDER:
        pl.semaphore_signal(barrier, inc=1, device_id=place(d["vec"], 1), device_id_type=MESH)
    for copy in loads[4:]:
        copy.start()

    loads[0].wait()
    listed = jnp.where(iota((ATOMS, 608), 0) == send_v[...], 1.0, 0.0)
    list_v[0:608, :] = listed.T
    list_v[608:640, :] = jnp.zeros((32, ATOMS), F32)
    loads[1].wait()
    loads[2].wait()
    loads[3].wait()
    feat16 = feat_v[...].astype(BF16)
    pos = pos_v[...]
    own8 = rows_to_eight([pos[0:1], pos[1:2], pos[2:3], jnp.ones((1, ATOMS), F32)], 4)
    own_pieces = split_rows(own8, 3)
    lane = iota((8, 128), 1)
    line = iota((8, 128), 0)

    def store_coords(ref, slots, corners, shifted):
        for d in TABLE:
            tile, low = d["slot"] // 128 * 128, d["slot"] % 128
            inside = (lane >= low) & (lane < low + d["rows"])
            coords = slots[:, tile : tile + 128]
            if shifted:
                shift = jnp.zeros((8, 128), F32)
                for step in range(3):
                    if d["vec"][step]:
                        shift = jnp.where(line == 4 + step, float(d["vec"][step]), shift)
                coords = coords - shift
            coords = jnp.where(inside, coords, 0.0)[4:8]
            if d["kind"] == 3:
                first = d["slot"] - CORNERS_AT
                coords = jnp.concatenate([coords, corners[first + 4 : first + 8]], axis=0)
            ref[d["tile"] : d["tile"] + coords.shape[0], :] = coords

    def remote(source, target, start, size, pair, vec, sign):
        rows = pl.ds(start, size)
        return pltpu.make_async_remote_copy(
            src_ref=source.at[rows],
            dst_ref=target.at[rows],
            send_sem=sems.at[pair],
            recv_sem=sems.at[pair + 1],
            device_id=place(vec, sign),
            device_id_type=MESH,
        )

    def send_lines(table, source, target, pair, sign):
        for d in ORDER:
            if d not in table:
                continue
            remote(source, target, d["slot"], d["rows"], pair, d["vec"], sign).start()

    def send_coords(source, target, pair, sign):
        for d in ORDER:
            remote(source, target, d["tile"], 8 if d["kind"] == 3 else 4, pair, d["vec"], sign).start()

    def lines_of(source, target, pair, first, last):
        return remote(source, target, first, last - first, pair, TABLE[0]["vec"], 1)

    def coords_of(source, target, pair):
        return remote(source, target, 0, COORDS_SENT, pair, TABLE[0]["vec"], 1)

    for d in TABLE:
        n, rows = d["number"], d["rows"]
        count = prefix[0, n + 1] - prefix[0, n]
        lines = list_v[pl.ds(prefix[0, n], rows), :]
        lines = jnp.where(iota((rows, ATOMS), 0) < count, lines, 0.0)
        if d["kind"] == 3:
            lines = jnp.concatenate([jnp.zeros((4, ATOMS), F32), lines[:4]], axis=0)
        pick_v[d["slot"] : d["slot"] + rows, :] = lines
    pick = pick_v[...].astype(BF16)
    packed = mm(pick, feat16)
    store_coords(coords_out1, sum_pieces(nt(own_pieces, pick), 3), packed[CORNERS_AT:], True)
    out1[...] = packed[:CORNERS_AT]
    pl.semaphore_wait(barrier, len(TABLE))
    send_coords(coords_out1, coords_in1, 0, 1)
    send_lines(LINES, out1, in1, 2, 1)
    send_lines(FACES, out1, in1, 4, 1)

    for copy in loads[4:]:
        copy.wait()
    src_row, dst_row = src_v[...], dst_v[...]
    centre = onehot(iota((ATOMS, EDGES), 0) == src_row)
    near = onehot(iota((ATOMS, EDGES), 0) == dst_row)
    ghost = slot_ids(dst_row)
    ghost_t = slot_ids_across(dst_row)
    same = (tn(centre, centre) * (1.0 / NEIGHBOURS)).astype(BF16)
    in_fill = jnp.where(iota((1, EDGES), 1) < fill[...], 1.0, 0.0)
    eye = iota((CH, CH), 0) == iota((CH, CH), 1)
    mix = mixing(wenv_v[...], wlat_v[...])
    w = dict(
        dst_t=wdst_v[...].T,
        rad_t=wrad_v[...].T,
        mix=jnp.concatenate(mix, axis=0),
        mix_t=jnp.concatenate([part.T for part in mix], axis=0),
        hid_t=whid_v[...].T,
        rad=wrad_v[...],
        hid=whid_v[...],
        ro=jnp.sum(jnp.where(eye, wro_v[...], 0.0), axis=1, keepdims=True),
    )
    feat_t = feat16.T
    own_lhs = jnp.concatenate([feat_t, own_pieces], axis=0)
    at_i = mm(own_lhs, centre)
    at_j = mm(own_lhs, near)
    pre_own = mm(wsrc_v[...].T, at_i[:CH].astype(BF16)) + mm(w["dst_t"], at_j[:CH].astype(BF16))
    pos_i = sum_pieces(at_i[CH:], 3)
    pos_j_own = sum_pieces(at_j[CH:], 3)
    pick_t_v[...] = pick.T
    pick_out = pltpu.make_async_copy(pick_t_v, pick_hbm, out_sem.at[0])
    pick_out.start()

    coords_of(coords_out1, coords_in1, 0).wait_recv()
    pos_g = mm(split_rows(unpack_coords(coords_in1), 3), ghost)
    geo = geometry(pos_i, pos_j_own + sum_pieces(pos_g, 3), in_fill, same)

    pre_known = pre_own + mm(w["rad_t"], geo["radial"].astype(BF16))

    lines_of(out1, in1, 2, LINES_AT, CORNERS_AT).wait_recv()
    some = jnp.concatenate([in1[LINES_AT:, :].astype(BF16), corner_lines(coords_in1)], axis=0)
    pre_known = pre_known + mm(nt(w["dst_t"], some).astype(BF16), ghost[LINES_AT:])
    lines_of(out1, in1, 4, 0, LINES_AT).wait_recv()
    far = nt(w["dst_t"], in1[0:LINES_AT, :].astype(BF16)).astype(BF16)
    dpre, kept = edge_pass(pre_known + mm(far, ghost[:LINES_AT]), geo, w)

    some = nt(ghost[LINES_AT:], dpre)
    out2[LINES_AT:, :] = some[: CORNERS_AT - LINES_AT]
    send_lines(LINES, out2, in2, 6, -1)
    out2[0:LINES_AT, :] = nt(ghost[:LINES_AT], dpre)
    send_lines(FACES, out2, in2, 8, -1)
    dq_pieces = split_rows(edge_coords(dpre, kept, geo, same, w), 2)
    store_coords(coords_out2, sum_pieces(mm(dq_pieces, ghost_t), 2), some[CORNERS_AT - LINES_AT :], False)
    send_coords(coords_out2, coords_in2, 10, -1)

    own = nt(jnp.concatenate([centre, near], axis=0), dpre).astype(BF16)
    own_v[0:ATOMS, :] = nt(own[:ATOMS], wsrc_v[...]) + nt(own[ATOMS:], wdst_v[...])
    own_v[ATOMS:, :] = sum_pieces(nt(dq_pieces, near - centre), 2)
    own_out = pltpu.make_async_copy(own_v, own_hbm, out_sem.at[1])
    own_out.start()

    pick_out.wait()
    own_out.wait()
    coords_of(coords_out1, coords_in1, 0).wait_send()
    for pair, first, last in ((2, LINES_AT, CORNERS_AT), (4, 0, LINES_AT)):
        lines_of(out1, in1, pair, first, last).wait_send()
        lines_of(out2, in2, pair + 4, first, last).wait()
    coords_of(coords_out2, coords_in2, 10).wait()


def finish(back_ref, coords_ref, own_ref, pick_ref, wdst_ref, force_ref, grad_ref):
    pick_t = pick_ref[...]
    lines = jnp.concatenate([back_ref[...].astype(BF16), corner_lines(coords_ref)], axis=0)
    returned = mm(pick_t, lines).astype(BF16)
    grad_ref[...] = own_ref[0:ATOMS, :] + nt(returned, wdst_ref[...])
    total8 = own_ref[ATOMS:, :] + sum_pieces(nt(split_rows(unpack_coords(coords_ref), 2), pick_t), 2)
    force_ref[...] = -total8[4:7]


def body(
    features,
    positions,
    send_ids,
    ghost_prefix,
    edge_fill,
    edge_src,
    edge_dst,
    weight_src,
    weight_dst,
    weight_radial,
    weight_env,
    weight_latent,
    weight_hidden,
    weight_readout,
):
    arrays = [
        features,
        positions,
        send_ids,
        edge_src,
        edge_dst,
        weight_src,
        weight_dst,
        weight_radial,
        weight_env,
        weight_latent,
        weight_hidden,
        weight_readout.reshape(1, CH),
    ]
    hbm = pl.BlockSpec(memory_space=pltpu.HBM)
    vmem = pl.BlockSpec(memory_space=pltpu.VMEM)
    back, coords, own, pick_t = pl.pallas_call(
        kernel,
        out_shape=(
            jax.ShapeDtypeStruct((CORNERS_AT, CH), F32),
            jax.ShapeDtypeStruct((COORDS, CH), F32),
            jax.ShapeDtypeStruct((ATOMS + 8, CH), F32),
            jax.ShapeDtypeStruct((ATOMS, SLOTS), BF16),
        ),
        in_specs=[hbm] * (2 + len(arrays)),
        out_specs=(hbm, hbm, hbm, hbm),
        scratch_shapes=[pltpu.SMEM(ghost_prefix.shape, jnp.int32), pltpu.VMEM((1, 1), jnp.int32)]
        + [pltpu.VMEM(a.shape, a.dtype) for a in arrays]
        + [
            pltpu.VMEM((SLOTS, ATOMS), F32),
            pltpu.VMEM((SLOTS, ATOMS), F32),
            pltpu.VMEM((CORNERS_AT, CH), F32),
            pltpu.VMEM((CORNERS_AT, CH), F32),
            pltpu.VMEM((COORDS, CH), F32),
            pltpu.VMEM((COORDS, CH), F32),
            pltpu.VMEM((CORNERS_AT, CH), F32),
            pltpu.VMEM((COORDS, CH), F32),
            pltpu.VMEM((ATOMS + 8, CH), F32),
            pltpu.VMEM((ATOMS, SLOTS), BF16),
            pltpu.SemaphoreType.DMA((2 + len(arrays),)),
            pltpu.SemaphoreType.DMA((12,)),
            pltpu.SemaphoreType.DMA((2,)),
        ],
        compiler_params=pltpu.CompilerParams(collective_id=0, has_side_effects=True, vmem_limit_bytes=VMEM),
        name="allegro",
    )(ghost_prefix, edge_fill.reshape(1, 1), *arrays)
    return pl.pallas_call(
        finish,
        out_shape=(
            jax.ShapeDtypeStruct((3, ATOMS), F32),
            jax.ShapeDtypeStruct((ATOMS, CH), F32),
        ),
        in_specs=[vmem] * 5,
        out_specs=(vmem, vmem),
        compiler_params=pltpu.CompilerParams(vmem_limit_bytes=VMEM),
        name="finish",
    )(back, coords, own, pick_t, weight_dst)


def solution(mesh):
    return jax.shard_map(
        body,
        mesh=mesh,
        in_specs=(
            P(("dom", "gz"), None),
            P(None, ("dom", "gz")),
            P(("dom", "gz"), None),
            P(("dom", "gz"), None),
            P(("dom", "gz")),
            P(("dom", "gz"), None),
            P(("dom", "gz"), None),
            P(),
            P(),
            P(),
            P(),
            P(),
            P(),
            P(),
        ),
        out_specs=(P(None, ("dom", "gz")), P(("dom", "gz"), None)),
        check_vma=False,
    )
```

```python
import math

import jax
import jax.numpy as jnp
import numpy as np
from jax import lax
from jax.experimental import pallas as pl
from jax.experimental.pallas import tpu as pltpu
from jax.sharding import PartitionSpec as P

NEIGHBOURS = 4
CAPS = (0, 64, 16, 4)
ROW_Y = 8

ATOMS = 128
EDGES = 512
CH = 128
SLOTS = 640
SHARPNESS = 8.0
VMEM = 56 * 1024 * 1024

BF16 = jnp.bfloat16
F32 = jnp.float32
MESH = pl.DeviceIdType.MESH


def directions():
    table = []
    offset = 0
    number = 0
    for a in (-1, 0, 1):
        for b in (-1, 0, 1):
            for c in (-1, 0, 1):
                kind = abs(a) + abs(b) + abs(c)
                if kind == 0:
                    continue
                cap = CAPS[kind]
                table.append(dict(vec=(a, b, c), kind=kind, cap=cap, number=number, offset=offset))
                offset += cap
                number += 1
    table.sort(key=lambda d: (d["kind"], d["number"]))
    slot = 0
    for step, d in enumerate(table):
        d["rows"] = {1: 64, 2: 16, 3: 8}[d["kind"]]
        d["slot"] = slot
        d["tile"] = 8 * step
        slot += d["rows"]
    assert slot == SLOTS
    return table


TABLE = directions()
FACES = [d for d in TABLE if d["kind"] == 1]
LINES = [d for d in TABLE if d["kind"] == 2]
CORNERS = [d for d in TABLE if d["kind"] == 3]
ORDER = sorted(TABLE, key=lambda d: (-d["kind"], d["vec"][2] == 0))
LINES_AT, CORNERS_AT = LINES[0]["slot"], CORNERS[0]["slot"]
COORDS = 8 * len(TABLE)
COORDS_SENT = 4 * len(TABLE) + 4 * len(CORNERS)


def mm(a, b):
    return lax.dot_general(a, b, (((1,), (0,)), ((), ())), preferred_element_type=F32)


def nt(a, b):
    return lax.dot_general(a, b, (((1,), (1,)), ((), ())), preferred_element_type=F32)


def tn(a, b):
    return lax.dot_general(a, b, (((0,), (0,)), ((), ())), preferred_element_type=F32)


def iota(shape, dim):
    return lax.broadcasted_iota(jnp.int32, shape, dim)


def onehot(cond):
    return jnp.where(cond, 1.0, 0.0).astype(BF16)


def split(x, pieces):
    out = []
    for step in range(pieces):
        part = x.astype(BF16)
        out.append(part)
        if step + 1 < pieces:
            x = x - part.astype(F32)
    return out


def split_rows(x, pieces):
    parts = []
    for step in range(pieces):
        part = x.astype(BF16).astype(F32)
        parts.append(part)
        x = x - part
    if pieces % 2:
        parts.append(jnp.zeros_like(x))
    return jnp.concatenate(parts, axis=0).astype(BF16)


def sum_pieces(x, pieces):
    total = x[0:8]
    for step in range(1, pieces):
        total = total + x[8 * step : 8 * step + 8]
    return total


def sigmoid(v):
    return 0.5 * jnp.tanh(0.5 * v) + 0.5


def silu_pair(v):
    v = v.astype(BF16)
    sig = sigmoid(v)
    value = v * sig
    return value, sig + value * (1 - sig)


def rows_to_eight(rows, first):
    place = iota((8, rows[0].shape[1]), 0)
    out = jnp.zeros((8, rows[0].shape[1]), F32)
    for step, row in enumerate(rows):
        out = jnp.where(place == first + step, row, out)
    return out


def slot_ids(dst_row):
    blocks = []
    for d in TABLE:
        if d["kind"] <= 2:
            place = iota((d["rows"], EDGES), 0) + (ATOMS + d["offset"])
            blocks.append(onehot(place == dst_row))
    place = iota((8 * len(CORNERS), EDGES), 0)
    inner = place % 8
    base = jnp.zeros_like(place)
    for step, d in enumerate(CORNERS):
        base = jnp.where(place // 8 == step, ATOMS - 4 + d["offset"], base)
    blocks.append(onehot((inner >= 4) & (base + inner == dst_row)))
    return jnp.concatenate(blocks, axis=0)


def side_by_side(x):
    rows = x.shape[0] // 3
    return jnp.concatenate([x[rows * step : rows * (step + 1)] for step in range(3)], axis=1)


def mixing(wenv, wlat):
    parts = [wlat[:CH]]
    for step in range(1, 4):
        parts.append(mm(wenv, wlat[CH * step : CH * (step + 1)]).astype(BF16))
    return parts


def geometry(pos_i, pos_j, in_fill, same):
    diff = pos_j - pos_i
    qx, qy, qz = diff[4:5], diff[5:6], diff[6:7]
    live = pos_j[7:8]
    rsq = qx * qx + qy * qy + qz * qz
    in_use = in_fill * live
    inside = jnp.where(rsq < 1.0, 1.0 - rsq, 0.0)
    env = inside * inside * in_use
    centers = iota((8, EDGES), 0).astype(F32) / 7.0
    offset = rsq - centers
    radial = jnp.exp(-SHARPNESS * offset * offset)

    r3, r15, r5 = math.sqrt(3.0), math.sqrt(15.0), math.sqrt(5.0)
    y1 = rows_to_eight([r3 * qx, r3 * qy, r3 * qz], 0)
    y2 = rows_to_eight(
        [
            r15 * qx * qy,
            r15 * qy * qz,
            r15 * qz * qx,
            0.5 * r15 * (qx * qx - qy * qy),
            0.5 * r5 * (2.0 * qz * qz - qx * qx - qy * qy),
        ],
        0,
    )
    h1, l1 = (part.astype(F32) for part in split(y1, 2))
    h2, l2 = (part.astype(F32) for part in split(y2, 2))
    zero8 = jnp.zeros((8, EDGES), F32)
    left1 = jnp.concatenate([h1, h1, l1, zero8], axis=0).astype(BF16)
    right1 = jnp.concatenate([h1, l1, h1, zero8], axis=0).astype(BF16)
    left2 = jnp.concatenate([h2, h2, l2, zero8], axis=0).astype(BF16)
    right2 = jnp.concatenate([h2, l2, h2, zero8], axis=0).astype(BF16)
    k1 = tn(left1, right1).astype(BF16) * same
    k2 = tn(left2, right2).astype(BF16) * same

    return dict(
        q=(qx, qy, qz),
        in_use=in_use,
        inside=inside,
        env=env,
        offset=offset,
        radial=radial,
        left1=left1,
        left2=left2,
        kernels=jnp.concatenate([same, k1, k2], axis=0),
    )


def edge_pass(pre, geo, w):
    env, kernels = geo["env"], geo["kernels"]
    env16 = env.astype(BF16)
    act, dact = silu_pair(pre)
    latent = act * env16
    mixed = mm(w["mix_t"], latent)
    near_far = mixed[CH:].astype(BF16)
    upd_act, upd_d = silu_pair(mixed[:CH] + mm(side_by_side(near_far), kernels))
    hid_act, hid_d = silu_pair(mm(w["hid_t"], latent + upd_act))
    dhid = hid_d * (w["ro"] * env).astype(BF16)
    dupdated = mm(w["hid"], dhid)
    dupd = dupdated.astype(BF16) * upd_d
    dmixed = mm(w["mix"], dupd)
    dlatent = dupdated + dmixed[:CH] + mm(side_by_side(dmixed[CH:].astype(BF16)), kernels)
    dpre = (dlatent * env).astype(BF16) * dact
    b1, b2 = near_far[CH : 2 * CH], near_far[2 * CH :]
    dupd_t = dupd.T
    pairs = [
        (jnp.concatenate([dupd_t, b.T], axis=1), jnp.concatenate([b, dupd], axis=0)) for b in (b1, b2)
    ]
    return dpre, (dlatent, act, hid_act, pairs)


def slot_ids_across(dst_row):
    dst = jnp.broadcast_to(dst_row.astype(F32), (128, EDGES)).T
    blocks = []
    for tile in range(SLOTS // 128):
        lane = iota((8, 128), 1)
        ids = jnp.full((8, 128), -1, jnp.int32)
        for d in TABLE:
            if d["slot"] // 128 == tile:
                low = d["slot"] % 128 + (4 if d["kind"] == 3 else 0)
                mine = (lane >= low) & (lane < low + d["cap"])
                ids = jnp.where(mine, lane + (ATOMS + d["offset"] - low), ids)
        blocks.append(onehot(dst == ids.astype(F32)[0:1]))
    return jnp.concatenate(blocks, axis=1)


def edge_coords(dpre, kept, geo, same, w):
    dlatent, act, hid_act, pairs = kept
    r3, r15, r5 = math.sqrt(3.0), math.sqrt(15.0), math.sqrt(5.0)
    qx, qy, qz = geo["q"]
    denv = jnp.sum(hid_act * w["ro"] + dlatent * act, axis=0, keepdims=True)
    t1, t2 = (mm(*pair).astype(BF16) * same for pair in pairs)
    dy1 = mm(geo["left1"], t1)
    dy1 = dy1[0:8] + dy1[16:24]
    dy2 = mm(geo["left2"], t2)
    dy2 = dy2[0:8] + dy2[16:24]

    drad = mm(w["rad"], dpre)
    drsq = jnp.sum(drad * geo["radial"] * geo["offset"], axis=0, keepdims=True) * (-2.0 * SHARPNESS)
    drsq = drsq - 2.0 * denv * geo["in_use"] * geo["inside"]
    a0, a1, a2, a3, a4 = (dy2[step : step + 1] for step in range(5))
    two = 2.0 * drsq
    gx = two * qx + r3 * dy1[0:1] + r15 * (a0 * qy + a2 * qz + a3 * qx) - r5 * a4 * qx
    gy = two * qy + r3 * dy1[1:2] + r15 * (a0 * qx + a1 * qz - a3 * qy) - r5 * a4 * qy
    gz = two * qz + r3 * dy1[2:3] + r15 * (a1 * qy + a2 * qx) + 2.0 * r5 * a4 * qz
    return rows_to_eight([gx, gy, gz], 4)


def corner_lines(ref):
    tiles = ref[CORNERS[0]["tile"] :, :]
    return jnp.where(iota(tiles.shape, 0) % 8 >= 4, tiles, 0.0).astype(BF16)


def unpack_coords(ref):
    tiles = [None] * (SLOTS // 128)
    for d in TABLE:
        tile = d["slot"] // 128
        piece = ref[d["tile"] : d["tile"] + 4, :]
        tiles[tile] = piece if tiles[tile] is None else tiles[tile] + piece
    coords = jnp.concatenate(tiles, axis=1)
    return jnp.concatenate([jnp.zeros_like(coords), coords], axis=0)


def kernel(
    prefix_hbm,
    fill_hbm,
    feat_hbm,
    pos_hbm,
    send_hbm,
    src_hbm,
    dst_hbm,
    wsrc_hbm,
    wdst_hbm,
    wrad_hbm,
    wenv_hbm,
    wlat_hbm,
    whid_hbm,
    wro_hbm,
    in2,
    coords_in2,
    own_hbm,
    pick_hbm,
    prefix,
    fill,
    feat_v,
    pos_v,
    send_v,
    src_v,
    dst_v,
    wsrc_v,
    wdst_v,
    wrad_v,
    wenv_v,
    wlat_v,
    whid_v,
    wro_v,
    list_v,
    pick_v,
    out1,
    in1,
    coords_out1,
    coords_in1,
    out2,
    coords_out2,
    own_v,
    pick_t_v,
    in_sem,
    sems,
    out_sem,
):
    planes = lax.axis_size("dom") // ROW_Y
    depth = lax.axis_size("gz")
    dom = lax.axis_index("dom")
    cz = lax.axis_index("gz")
    cx, cy = lax.div(dom, ROW_Y), lax.rem(dom, ROW_Y)
    along_x = {step: lax.rem(cx + (step + planes), planes) * ROW_Y for step in (-1, 0, 1)}
    along_y = {step: lax.rem(cy + (step + ROW_Y), ROW_Y) for step in (-1, 0, 1)}
    along_z = {step: lax.rem(cz + (step + depth), depth) for step in (-1, 0, 1)}

    def place(vec, sign):
        return (along_x[sign * vec[0]] + along_y[sign * vec[1]], along_z[sign * vec[2]])

    loads = []
    for step, (source, target) in enumerate(
        [
            (send_hbm, send_v),
            (prefix_hbm, prefix),
            (feat_hbm, feat_v),
            (pos_hbm, pos_v),
            (src_hbm, src_v),
            (dst_hbm, dst_v),
            (wsrc_hbm, wsrc_v),
            (wdst_hbm, wdst_v),
            (wrad_hbm, wrad_v),
            (wenv_hbm, wenv_v),
            (wlat_hbm, wlat_v),
            (whid_hbm, whid_v),
            (wro_hbm, wro_v),
            (fill_hbm, fill),
        ]
    ):
        copy = pltpu.make_async_copy(source, target, in_sem.at[step])
        loads.append(copy)

    barrier = pltpu.get_barrier_semaphore()
    for copy in loads[:4]:
        copy.start()
    for d in ORDER:
        pl.semaphore_signal(barrier, inc=1, device_id=place(d["vec"], 1), device_id_type=MESH)
    for copy in loads[4:]:
        copy.start()

    loads[0].wait()
    listed = jnp.where(iota((ATOMS, 608), 0) == send_v[...], 1.0, 0.0)
    list_v[0:608, :] = listed.T
    list_v[608:640, :] = jnp.zeros((32, ATOMS), F32)
    loads[1].wait()
    loads[2].wait()
    loads[3].wait()
    feat16 = feat_v[...].astype(BF16)
    pos = pos_v[...]
    own8 = rows_to_eight([pos[0:1], pos[1:2], pos[2:3], jnp.ones((1, ATOMS), F32)], 4)
    own_pieces = split_rows(own8, 3)
    lane = iota((8, 128), 1)
    line = iota((8, 128), 0)

    def store_coords(ref, slots, corners, shifted):
        for d in TABLE:
            tile, low = d["slot"] // 128 * 128, d["slot"] % 128
            inside = (lane >= low) & (lane < low + d["rows"])
            coords = slots[:, tile : tile + 128]
            if shifted:
                shift = jnp.zeros((8, 128), F32)
                for step in range(3):
                    if d["vec"][step]:
                        shift = jnp.where(line == 4 + step, float(d["vec"][step]), shift)
                coords = coords - shift
            coords = jnp.where(inside, coords, 0.0)[4:8]
            if d["kind"] == 3:
                first = d["slot"] - CORNERS_AT
                coords = jnp.concatenate([coords, corners[first + 4 : first + 8]], axis=0)
            ref[d["tile"] : d["tile"] + coords.shape[0], :] = coords

    def remote(source, target, start, size, pair, vec, sign):
        rows = pl.ds(start, size)
        return pltpu.make_async_remote_copy(
            src_ref=source.at[rows],
            dst_ref=target.at[rows],
            send_sem=sems.at[pair],
            recv_sem=sems.at[pair + 1],
            device_id=place(vec, sign),
            device_id_type=MESH,
        )

    def send_lines(table, source, target, pair, sign):
        for d in ORDER:
            if d not in table:
                continue
            remote(source, target, d["slot"], d["rows"], pair, d["vec"], sign).start()

    def send_coords(source, target, pair, sign):
        for d in ORDER:
            remote(source, target, d["tile"], 8 if d["kind"] == 3 else 4, pair, d["vec"], sign).start()

    def lines_of(source, target, pair, first, last):
        return remote(source, target, first, last - first, pair, TABLE[0]["vec"], 1)

    def coords_of(source, target, pair):
        return remote(source, target, 0, COORDS_SENT, pair, TABLE[0]["vec"], 1)

    for d in TABLE:
        n, rows = d["number"], d["rows"]
        count = prefix[0, n + 1] - prefix[0, n]
        lines = list_v[pl.ds(prefix[0, n], rows), :]
        lines = jnp.where(iota((rows, ATOMS), 0) < count, lines, 0.0)
        if d["kind"] == 3:
            lines = jnp.concatenate([jnp.zeros((4, ATOMS), F32), lines[:4]], axis=0)
        pick_v[d["slot"] : d["slot"] + rows, :] = lines
    pick = pick_v[...].astype(BF16)
    packed = mm(pick, feat16)
    store_coords(coords_out1, sum_pieces(nt(own_pieces, pick), 3), packed[CORNERS_AT:], True)
    out1[...] = packed[:CORNERS_AT]
    pl.semaphore_wait(barrier, len(TABLE))
    send_coords(coords_out1, coords_in1, 0, 1)
    send_lines(LINES, out1, in1, 2, 1)
    send_lines(FACES, out1, in1, 4, 1)

    for copy in loads[4:]:
        copy.wait()
    src_row, dst_row = src_v[...], dst_v[...]
    centre = onehot(iota((ATOMS, EDGES), 0) == src_row)
    near = onehot(iota((ATOMS, EDGES), 0) == dst_row)
    ghost = slot_ids(dst_row)
    ghost_t = slot_ids_across(dst_row)
    same = (tn(centre, centre) * (1.0 / NEIGHBOURS)).astype(BF16)
    in_fill = jnp.where(iota((1, EDGES), 1) < fill[...], 1.0, 0.0)
    eye = iota((CH, CH), 0) == iota((CH, CH), 1)
    mix = mixing(wenv_v[...], wlat_v[...])
    w = dict(
        dst_t=wdst_v[...].T,
        rad_t=wrad_v[...].T,
        mix=jnp.concatenate(mix, axis=0),
        mix_t=jnp.concatenate([part.T for part in mix], axis=0),
        hid_t=whid_v[...].T,
        rad=wrad_v[...],
        hid=whid_v[...],
        ro=jnp.sum(jnp.where(eye, wro_v[...], 0.0), axis=1, keepdims=True),
    )
    feat_t = feat16.T
    own_lhs = jnp.concatenate([feat_t, own_pieces], axis=0)
    at_i = mm(own_lhs, centre)
    at_j = mm(own_lhs, near)
    pre_own = mm(wsrc_v[...].T, at_i[:CH].astype(BF16)) + mm(w["dst_t"], at_j[:CH].astype(BF16))
    pos_i = sum_pieces(at_i[CH:], 3)
    pos_j_own = sum_pieces(at_j[CH:], 3)
    pick_t_v[...] = pick.T
    pick_out = pltpu.make_async_copy(pick_t_v, pick_hbm, out_sem.at[0])
    pick_out.start()

    coords_of(coords_out1, coords_in1, 0).wait_recv()
    pos_g = mm(split_rows(unpack_coords(coords_in1), 3), ghost)
    geo = geometry(pos_i, pos_j_own + sum_pieces(pos_g, 3), in_fill, same)

    pre_known = pre_own + mm(w["rad_t"], geo["radial"].astype(BF16))

    lines_of(out1, in1, 2, LINES_AT, CORNERS_AT).wait_recv()
    some = jnp.concatenate([in1[LINES_AT:, :].astype(BF16), corner_lines(coords_in1)], axis=0)
    pre_known = pre_known + mm(nt(w["dst_t"], some).astype(BF16), ghost[LINES_AT:])
    lines_of(out1, in1, 4, 0, LINES_AT).wait_recv()
    far = nt(w["dst_t"], in1[0:LINES_AT, :].astype(BF16)).astype(BF16)
    dpre, kept = edge_pass(pre_known + mm(far, ghost[:LINES_AT]), geo, w)

    back = nt(ghost, dpre)
    some = back[LINES_AT:]
    out2[LINES_AT:, :] = some[: CORNERS_AT - LINES_AT]
    send_lines(LINES, out2, in2, 6, -1)
    out2[0:LINES_AT, :] = back[:LINES_AT]
    send_lines(FACES, out2, in2, 8, -1)
    dq_pieces = split_rows(edge_coords(dpre, kept, geo, same, w), 2)
    store_coords(coords_out2, sum_pieces(mm(dq_pieces, ghost_t), 2), some[CORNERS_AT - LINES_AT :], False)
    send_coords(coords_out2, coords_in2, 10, -1)

    own = nt(jnp.concatenate([centre, near], axis=0), dpre).astype(BF16)
    own_v[0:ATOMS, :] = nt(own[:ATOMS], wsrc_v[...]) + nt(own[ATOMS:], wdst_v[...])
    own_v[ATOMS:, :] = sum_pieces(nt(dq_pieces, near - centre), 2)
    own_out = pltpu.make_async_copy(own_v, own_hbm, out_sem.at[1])
    own_out.start()

    pick_out.wait()
    own_out.wait()
    coords_of(coords_out1, coords_in1, 0).wait_send()
    for pair, first, last in ((2, LINES_AT, CORNERS_AT), (4, 0, LINES_AT)):
        lines_of(out1, in1, pair, first, last).wait_send()
        lines_of(out2, in2, pair + 4, first, last).wait()
    coords_of(coords_out2, coords_in2, 10).wait()


def finish(back_ref, coords_ref, own_ref, pick_ref, wdst_ref, force_ref, grad_ref):
    pick_t = pick_ref[...]
    lines = jnp.concatenate([back_ref[...].astype(BF16), corner_lines(coords_ref)], axis=0)
    returned = mm(pick_t, lines).astype(BF16)
    grad_ref[...] = own_ref[0:ATOMS, :] + nt(returned, wdst_ref[...])
    total8 = own_ref[ATOMS:, :] + sum_pieces(nt(split_rows(unpack_coords(coords_ref), 2), pick_t), 2)
    force_ref[...] = -total8[4:7]


def body(
    features,
    positions,
    send_ids,
    ghost_prefix,
    edge_fill,
    edge_src,
    edge_dst,
    weight_src,
    weight_dst,
    weight_radial,
    weight_env,
    weight_latent,
    weight_hidden,
    weight_readout,
):
    arrays = [
        features,
        positions,
        send_ids,
        edge_src,
        edge_dst,
        weight_src,
        weight_dst,
        weight_radial,
        weight_env,
        weight_latent,
        weight_hidden,
        weight_readout.reshape(1, CH),
    ]
    hbm = pl.BlockSpec(memory_space=pltpu.HBM)
    vmem = pl.BlockSpec(memory_space=pltpu.VMEM)
    back, coords, own, pick_t = pl.pallas_call(
        kernel,
        out_shape=(
            jax.ShapeDtypeStruct((CORNERS_AT, CH), F32),
            jax.ShapeDtypeStruct((COORDS, CH), F32),
            jax.ShapeDtypeStruct((ATOMS + 8, CH), F32),
            jax.ShapeDtypeStruct((ATOMS, SLOTS), BF16),
        ),
        in_specs=[hbm] * (2 + len(arrays)),
        out_specs=(hbm, hbm, hbm, hbm),
        scratch_shapes=[pltpu.SMEM(ghost_prefix.shape, jnp.int32), pltpu.VMEM((1, 1), jnp.int32)]
        + [pltpu.VMEM(a.shape, a.dtype) for a in arrays]
        + [
            pltpu.VMEM((SLOTS, ATOMS), F32),
            pltpu.VMEM((SLOTS, ATOMS), F32),
            pltpu.VMEM((CORNERS_AT, CH), F32),
            pltpu.VMEM((CORNERS_AT, CH), F32),
            pltpu.VMEM((COORDS, CH), F32),
            pltpu.VMEM((COORDS, CH), F32),
            pltpu.VMEM((CORNERS_AT, CH), F32),
            pltpu.VMEM((COORDS, CH), F32),
            pltpu.VMEM((ATOMS + 8, CH), F32),
            pltpu.VMEM((ATOMS, SLOTS), BF16),
            pltpu.SemaphoreType.DMA((2 + len(arrays),)),
            pltpu.SemaphoreType.DMA((12,)),
            pltpu.SemaphoreType.DMA((2,)),
        ],
        compiler_params=pltpu.CompilerParams(collective_id=0, has_side_effects=True, vmem_limit_bytes=VMEM),
        name="allegro",
    )(ghost_prefix, edge_fill.reshape(1, 1), *arrays)
    return pl.pallas_call(
        finish,
        out_shape=(
            jax.ShapeDtypeStruct((3, ATOMS), F32),
            jax.ShapeDtypeStruct((ATOMS, CH), F32),
        ),
        in_specs=[vmem] * 5,
        out_specs=(vmem, vmem),
        compiler_params=pltpu.CompilerParams(vmem_limit_bytes=VMEM),
        name="finish",
    )(back, coords, own, pick_t, weight_dst)


def solution(mesh):
    return jax.shard_map(
        body,
        mesh=mesh,
        in_specs=(
            P(("dom", "gz"), None),
            P(None, ("dom", "gz")),
            P(("dom", "gz"), None),
            P(("dom", "gz"), None),
            P(("dom", "gz")),
            P(("dom", "gz"), None),
            P(("dom", "gz"), None),
            P(),
            P(),
            P(),
            P(),
            P(),
            P(),
            P(),
        ),
        out_specs=(P(None, ("dom", "gz")), P(("dom", "gz"), None)),
        check_vma=False,
    )
```
